256 devices in a mesh: lon: 16 (over y_hi, z), lat: 4 (over x), mem: 4 (over y_lo, core).
Axes of the slice: x: 4, y: 4 (y_hi: 2, y_lo: 2; y = y_hi * 2 + y_lo), z: 8, core: 2. Of those that a mesh axis runs over, the one named last changes fastest.
Arguments:
- tracer: float32 [128, 8, 32, 2048], P('mem', None, 'lat', 'lon'), parts along dimension 0, may hold values from -3 to 3
- courant: float32 [2, 8, 32, 2048], P(None, None, 'lat', 'lon'), may hold values from -0.45 to 0.45
- mixing: float32 [7, 32, 2048], P(None, 'lat', 'lon'), may hold values from 0.1 to 10
- forcing: float32 [5, 196608], P(None, ('lon', 'lat')), may hold values from 0 to 1
- plant_type: int32 [196608], P(('lon', 'lat')), may hold values from 0 to 15
- land_params: float32 [3, 128, 16], P(None, 'mem'), parts along dimension 1, may hold values from 0 to 1
- send_slot: int32 [196608], P(('lon', 'lat')), may hold values from -1 to 4095, as said below
- recv_cell: int32 [4096, 64], P(('lon', 'lat')), may hold values from 0 to 1024, as said below
Outputs:
- tracer_next: float32 [128, 8, 32, 2048], P('mem', None, 'lat', 'lon'), parts along dimension 0
- surface_flux: float32 [128, 32, 2048], P('mem', 'lat', 'lon'), parts along dimension 0
The draws below stay inside these ranges and needn't reach their ends.
There are 4 independent parts, one for each index of `mem`. The reference program is written for one: setup_inputs(seed, part) draws one part's arguments, and reference() takes and returns one part's arrays. A program takes and returns all parts, laid end to end along the dimension named above; an argument that names none is the same for every part. Nothing has to cross between parts.
Inputs may be any that keep to these rules, and one draw needn't show every extreme that they name: `send_slot`: -1 marks an empty column slot; otherwise the value is tile * 64 + place. Each device holds 1536 or more live columns and some device holds 3072. No two columns of one device share a tile and place, at most 64 columns of one device go to one tile, and that many are reached. A quarter of the tiles receive no columns. `recv_cell`: row t * 64 + d, place k gives the local cell (row * 128 + column) of tile t for the column that device d sends to that place, or 1024 where it sends none; it agrees with send_slot.
All inputs are finite; a program needn't handle non-finite values.
Results may differ from the reference program's by a relative error of at most 0.0003.
Values sent between devices are 32-bit elements; how exact they have to be, the bound alone decides.
No kernel may reach another device: no remote copies, remote signals or barrier semaphores. Data moves between devices by JAX's collectives and lax.ppermute only.
A program may use at most 64 MiB of HBM per device.

```python
import math
import jax
import jax.numpy as jnp
from jax import lax

MEMB = 32
LEV = 8
PFT = 16
TX = 128
TY = 8
CAP = 3072
TILES = 64
LAND_TILES = 48
SLOT = 64
NX = 2048
NY = 32
COLS = 196608
N_LAT = 4


def coupling_tables(key):
    base_key = jax.random.fold_in(key, 4099)
    key_live, key_land, key_order, key_place, key_cell, key_full = jax.random.split(base_key, 6)
    device_ids = jnp.arange(TILES, dtype=jnp.int32)
    live_count = jax.random.randint(key_live, (TILES,), CAP // 2, CAP + 1)
    full_device = jax.random.randint(key_full, (), 0, TILES)
    live_count = jnp.where(device_ids == full_device, CAP, live_count)
    land_list = jax.random.permutation(key_land, TILES)[:LAND_TILES]
    orders = jax.vmap(lambda entry_key: jax.random.permutation(entry_key, LAND_TILES))(jax.random.split(key_order, TILES))
    destination = land_list[orders]
    places = jax.vmap(lambda entry_key: jax.random.permutation(entry_key, CAP))(jax.random.split(key_place, TILES))
    column_ids = jnp.arange(CAP, dtype=jnp.int32)
    target_tile = destination[:, column_ids % LAND_TILES]
    slot_value = target_tile * SLOT + column_ids[None, :] // LAND_TILES
    slot_value = jnp.where(column_ids[None, :] < live_count[:, None], slot_value, -1).astype(jnp.int32)
    send_table = jnp.zeros((TILES, CAP), jnp.int32).at[device_ids[:, None], places].set(slot_value)
    rank_values = jnp.broadcast_to(jnp.arange(LAND_TILES, dtype=jnp.int32)[None, :], (TILES, LAND_TILES))
    rank_table = jnp.full((TILES, TILES), CAP + 1, jnp.int32).at[device_ids[:, None], destination].set(rank_values)
    slot_ids = jnp.arange(SLOT, dtype=jnp.int32)
    slot_used = slot_ids[None, None, :] * LAND_TILES + rank_table.T[:, :, None] < live_count[None, :, None]
    cell_draw = jax.random.randint(key_cell, (TILES, TILES, SLOT), 0, TY * TX)
    recv_table = jnp.where(slot_used, cell_draw, TY * TX).astype(jnp.int32).reshape(TILES * TILES, SLOT)
    return (send_table.reshape(TILES * CAP), recv_table)


def draw_send_slot(key, part):
    return coupling_tables(key)[0]


def draw_recv_cell(key, part):
    return coupling_tables(key)[1]


def set_ends(values, own_key, smallest, largest):
    dims = values.shape
    spot = [jax.random.randint(jax.random.fold_in(own_key, axis), (), 0, dims[axis]) for axis in range(len(dims))]
    values = values.at[tuple(spot)].set(smallest)
    longest = dims.index(max(dims))
    spot[longest] = (spot[longest] + 1) % dims[longest]
    return values.at[tuple(spot)].set(largest)


def level_of(own_key, shape, cuts, smallest, top_value):
    gain = 1.0
    for dim, parts in cuts:
        draws = jax.random.uniform(jax.random.fold_in(jax.random.fold_in(own_key, 6), dim), (parts,), jnp.float32, smallest / len(cuts), top_value / len(cuts))
        gain = gain * jnp.repeat(jnp.exp(draws), shape[dim] // parts).reshape((-1,) + (1,) * (len(shape) - 1 - dim))
    return gain


def centred(rng, shape, deviation, most, cuts=(), kind=jnp.bfloat16):
    entries = jax.random.normal(rng, shape, jnp.float32) * deviation
    if len(cuts) > 0:
        entries = level_of(rng, shape, cuts, -0.22, 0.18) * entries
    return jnp.clip(entries, min=-most, max=most).astype(kind)


def setup_inputs(seed: int = 0, part: int = 0) -> dict:
    keys = jax.random.split(jax.random.key(seed), 9)
    part_keys = jax.random.split(jax.random.fold_in(keys[8], part), 9)
    return {
        "tracer": centred(part_keys[0], (MEMB, LEV, NY, NX), 1.0, 3.0, ((2, 4), (3, 16)), jnp.float32),
        "courant": jnp.clip(jax.random.uniform(keys[1], (2, LEV, NY, NX), jnp.float32, -0.45, 0.45) * level_of(keys[1], (2, LEV, NY, NX), ((2, 4), (3, 16)), -0.4, 0.0), -0.45, 0.45),
        "mixing": jnp.clip(jnp.exp(math.log(10.0) - 4.6051702 * jax.random.uniform(keys[2], (LEV - 1, NY, NX), jnp.float32) ** level_of(keys[2], (LEV - 1, NY, NX), ((1, 4), (2, 16)), -0.2, 0.2)), 0.1, 10.0),
        "forcing": jnp.clip(1.0 * jax.random.uniform(keys[3], (5, COLS), jnp.float32) ** level_of(keys[3], (5, COLS), ((1, 64),), -0.2, 0.2), 0.0, 1.0),
        "plant_type": set_ends(jax.random.randint(keys[4], (COLS,), 0, PFT), jax.random.fold_in(keys[4], 1), 0, PFT - 1).astype(jnp.int32),
        "land_params": jnp.clip(jax.random.uniform(part_keys[5], (3, MEMB, PFT), jnp.float32, 0.0, 1.0), 0.0, 1.0),
        "send_slot": draw_send_slot(jax.random.fold_in(keys[8], 71), part),
        "recv_cell": draw_recv_cell(jax.random.fold_in(keys[8], 71), part),
    }


FLUX_SCALE = 0.02
GAS_CONSTANT = 8.314

def arrhenius(energy, leaf_temp):
    return jnp.exp(energy * (leaf_temp - 25.0) / (298.15 * GAS_CONSTANT * (leaf_temp + 273.15)))

def column_exchange(drivers, param_rows, bottom_tracer):
    light = 2000.0 * drivers[0]
    leaf_temp = 35.0 * drivers[1]
    water_factor = 0.2 + 0.8 * drivers[2]
    leaf_area = 0.5 + 5.5 * drivers[3]
    area_share = 0.05 + 0.55 * drivers[4]
    carbox_ref = 30.0 + 70.0 * param_rows[0]
    transport_ratio = 1.4 + 0.8 * param_rows[1]
    respiration_share = 0.005 + 0.025 * param_rows[2]
    carbon_leaf = 0.7 * (400.0 + 100.0 * bottom_tracer)
    carboxylation = carbox_ref * arrhenius(65330.0, leaf_temp) * water_factor
    transport_max = transport_ratio * carbox_ref * arrhenius(43540.0, leaf_temp)
    michaelis_carbon = 404.9 * arrhenius(79430.0, leaf_temp)
    michaelis_oxygen = 278.4 * arrhenius(36380.0, leaf_temp)
    compensation = 42.75 * arrhenius(37830.0, leaf_temp)
    absorbed = 0.425 * light
    total_rate = absorbed + transport_max
    electron_rate = (total_rate - jnp.sqrt(total_rate * total_rate - 2.8 * absorbed * transport_max)) / 1.4
    rubisco_rate = carboxylation * (carbon_leaf - compensation) / (carbon_leaf + michaelis_carbon * (1.0 + 210.0 / michaelis_oxygen))
    light_rate = electron_rate * (carbon_leaf - compensation) / (4.0 * carbon_leaf + 8.0 * compensation)
    gross_rate = jnp.minimum(rubisco_rate, light_rate)
    canopy_scale = (1.0 - jnp.exp(-0.5 * leaf_area)) / 0.5
    return -FLUX_SCALE * area_share * canopy_scale * (gross_rate - respiration_share * carboxylation)

def window(array_in, start_at, count, dimension):
    return lax.slice_in_dim(array_in, start_at, start_at + count, axis=dimension)

def flux_divergence(padded, courant_pad, dimension):
    extent = padded.shape[dimension] - 6
    edge_values = 7.0 / 12.0 * (window(padded, 1, extent + 3, dimension) + window(padded, 2, extent + 3, dimension)) - 1.0 / 12.0 * (window(padded, 0, extent + 3, dimension) + window(padded, 3, extent + 3, dimension))
    left_low = window(edge_values, 0, extent + 1, dimension)
    left_high = window(edge_values, 1, extent + 1, dimension)
    right_high = window(edge_values, 2, extent + 1, dimension)
    left_mean = window(padded, 2, extent + 1, dimension)
    right_mean = window(padded, 3, extent + 1, dimension)
    face_courant = window(courant_pad, 2, extent + 1, dimension)
    slope_left = left_high - left_low
    curve_left = 6.0 * (left_mean - 0.5 * (left_low + left_high))
    slope_right = right_high - left_high
    curve_right = 6.0 * (right_mean - 0.5 * (left_high + right_high))
    from_left = left_high - 0.5 * face_courant * (slope_left - (1.0 - 2.0 / 3.0 * face_courant) * curve_left)
    from_right = left_high - 0.5 * face_courant * (slope_right + (1.0 + 2.0 / 3.0 * face_courant) * curve_right)
    fluxes = face_courant * jnp.where(face_courant > 0, from_left, from_right)
    return window(fluxes, 1, extent, dimension) - window(fluxes, 0, extent, dimension)

def implicit_mixing(rhs_field, coefficient):
    layers = rhs_field.shape[-3]
    ratios = []
    sweep_values = []
    for layer_index in range(layers):
        weight_below = coefficient[layer_index - 1] if layer_index > 0 else jnp.zeros_like(coefficient[0])
        weight_above = coefficient[layer_index] if layer_index < layers - 1 else jnp.zeros_like(coefficient[0])
        pivot_value = 1.0 + weight_below + weight_above
        carried = rhs_field[..., layer_index, :, :]
        if layer_index > 0:
            pivot_value = pivot_value - weight_below * ratios[-1]
            carried = carried + weight_below * sweep_values[-1]
        ratios.append(weight_above / pivot_value)
        sweep_values.append(carried / pivot_value)
    solved = [sweep_values[-1]]
    for layer_index in range(layers - 2, -1, -1):
        solved.insert(0, sweep_values[layer_index] + ratios[layer_index] * solved[0])
    return jnp.stack(solved, axis=-3)

def reference(tracer, courant, mixing, forcing, plant_type, land_params, send_slot, recv_cell):
    live_column = send_slot >= 0
    target_tile = jnp.where(live_column, send_slot // SLOT, 0).astype(jnp.int32)
    target_place = jnp.where(live_column, send_slot % SLOT, 0).astype(jnp.int32)
    source_device = (jnp.arange(COLS, dtype=jnp.int32) // CAP).astype(jnp.int32)
    local_cell = recv_cell[target_tile * TILES + source_device, target_place]
    grid_row = target_tile % N_LAT * TY + local_cell // TX
    grid_column = target_tile // N_LAT * TX + local_cell % TX
    flat_cell = jnp.where(live_column, grid_row * NX + grid_column, NY * NX).astype(jnp.int32)
    bottom = tracer[:, 0].reshape(MEMB, NY * NX)
    bottom_tracer = jnp.take(bottom, jnp.minimum(flat_cell, NY * NX - 1), axis=1)
    param_rows = land_params[:, :, plant_type]
    column_flux = column_exchange(forcing, param_rows, bottom_tracer)
    surface = jnp.zeros((MEMB, NY * NX), jnp.float32).at[:, flat_cell].add(column_flux, mode='drop')
    surface = surface.reshape(MEMB, NY, NX)
    wind_east = courant[0]
    row_ids = lax.broadcasted_iota(jnp.int32, (1, NY, 1), 1)
    wind_north = jnp.where(row_ids == NY - 1, 0.0, courant[1])
    wind_east_pad = jnp.pad(wind_east, ((0, 0), (0, 0), (3, 3)), mode='wrap')
    wind_north_pad = jnp.pad(wind_north, ((0, 0), (3, 3), (0, 0)))

    def member_step(operands):
        member_tracer, member_surface = operands
        east_pad = jnp.pad(member_tracer, ((0, 0), (0, 0), (3, 3)), mode='wrap')
        north_pad = jnp.pad(member_tracer, ((0, 0), (3, 3), (0, 0)))
        advected = member_tracer - flux_divergence(east_pad, wind_east_pad, 2) - flux_divergence(north_pad, wind_north_pad, 1)
        forced = advected.at[0].add(member_surface)
        return implicit_mixing(forced, mixing)
    tracer_next = lax.map(member_step, (tracer, surface))
    return (tracer_next, surface)
```

```python
import functools

import jax
import jax.numpy as jnp
from jax import lax
from jax.experimental import pallas as pl
from jax.experimental.pallas import tpu as pltpu
from jax.sharding import PartitionSpec as P

FLUX_SCALE = 0.02
GAS_CONSTANT = 8.314
LANES = 128
ROWS = 8
VMEM_BYTES = 40 * 2**20


def nt_dot(left, right):
    return lax.dot_general(
        left, right, (((1,), (1,)), ((), ())), preferred_element_type=jnp.float32
    )


def bf16_parts(values, count):
    parts = []
    rest = values
    for _ in range(count):
        part = rest.astype(jnp.bfloat16)
        rest = rest - part.astype(jnp.float32)
        parts.append(part)
    return parts


def column_kernel(forcing_ref, type_ref, slot_ref, out_ref):
    columns = slot_ref.shape[1]
    tiles = out_ref.shape[0]
    places = 64
    slot = slot_ref[...]
    tile = jnp.right_shift(slot, 6)
    place = jnp.bitwise_and(slot, places - 1)
    light = forcing_ref[0:1, :]
    leaf_temp = forcing_ref[1:2, :]
    water = forcing_ref[2:3, :]
    leaf_area = 0.5 + 5.5 * forcing_ref[3:4, :]
    area_share = 0.05 + 0.55 * forcing_ref[4:5, :]
    canopy_scale = (1.0 - jnp.exp(-0.5 * leaf_area)) / 0.5
    flux_scale = -FLUX_SCALE * area_share * canopy_scale
    plant = type_ref[...].astype(jnp.float32)

    tile_onehot = (
        lax.broadcasted_iota(jnp.int32, (tiles, columns), 0) == tile
    ).astype(jnp.float32).astype(jnp.bfloat16)
    place_ids = lax.broadcasted_iota(jnp.int32, (LANES, columns), 0)
    first_half = (place_ids == place).astype(jnp.float32).astype(jnp.bfloat16)
    second_half = (place_ids == place + places).astype(jnp.float32).astype(jnp.bfloat16)

    def spread(values, count):
        return [
            tile_onehot * jnp.broadcast_to(part, (tiles, columns))
            for part in bf16_parts(values, count)
        ]

    first = jnp.concatenate(spread(light, 3) + spread(water, 3) + spread(plant, 1), axis=0)
    second = jnp.concatenate(spread(leaf_temp, 3) + spread(flux_scale, 3), axis=0)
    from_first = nt_dot(first, first_half)
    from_second = nt_dot(second, second_half)

    def part_sum(values, start, count):
        total = values[start * tiles : (start + 1) * tiles]
        for step in range(1, count):
            total = total + values[(start + step) * tiles : (start + step + 1) * tiles]
        return total

    out_ref[:, 0, 0:LANES] = part_sum(from_first, 0, 3) + part_sum(from_second, 0, 3)
    out_ref[:, 0, LANES : 2 * LANES] = part_sum(from_first, 3, 3) + part_sum(from_second, 3, 3)
    out_ref[:, 0, 2 * LANES : 3 * LANES] = part_sum(from_first, 6, 1)


def pack_columns(forcing, plant_type, send_slot, tiles):
    columns = send_slot.shape[0]
    return pl.pallas_call(
        column_kernel,
        out_shape=jax.ShapeDtypeStruct((tiles, 1, 3 * LANES), jnp.float32),
        compiler_params=pltpu.CompilerParams(vmem_limit_bytes=VMEM_BYTES),
        cost_estimate=pl.CostEstimate(flops=2 * 448 * columns * 256, bytes_accessed=300000, transcendentals=columns),
        name="pack_columns",
    )(forcing, plant_type.reshape(1, columns), send_slot.reshape(1, columns))


def halo_kernel(tracer_ref, courant_ref, low_ref, high_ref, side_ref):
    blocks = tracer_ref.shape[0] // ROWS
    levels = courant_ref.shape[0] // (2 * ROWS)
    for step in range(3):
        low_ref[step * blocks : (step + 1) * blocks, :] = tracer_ref[
            pl.ds(step, blocks, stride=ROWS), :
        ]
        high_ref[step * blocks : (step + 1) * blocks, :] = tracer_ref[
            pl.ds(ROWS - 3 + step, blocks, stride=ROWS), :
        ]
    high_ref[3 * blocks : 3 * blocks + levels, :] = courant_ref[
        pl.ds(levels * ROWS + ROWS - 1, levels, stride=ROWS), :
    ]
    slot_of_lane = lax.broadcasted_iota(jnp.int32, (ROWS, LANES), 1) // 8

    def merge(read, count):
        total = jnp.zeros((ROWS, LANES), jnp.float32)
        for slot in range(count):
            moved = pltpu.roll(read(slot), 3 + 8 * slot, 1)
            total = jnp.where(slot_of_lane == slot, moved, total)
        return total

    def step(group, carry):
        def read(slot):
            start = pl.multiple_of((group * 16 + slot) * ROWS, ROWS)
            return tracer_ref[pl.ds(start, ROWS), :]

        side_ref[pl.ds(pl.multiple_of(group * ROWS, ROWS), ROWS), :] = merge(read, 16)
        return carry

    lax.fori_loop(0, blocks // 16, step, 0)
    side_ref[blocks // 2 : blocks // 2 + ROWS, :] = merge(
        lambda slot: courant_ref[slot * ROWS : (slot + 1) * ROWS, :], levels
    )


def pack_halos(tracer_rows, courant_rows):
    blocks = tracer_rows.shape[0] // ROWS
    levels = courant_rows.shape[0] // (2 * ROWS)
    return pl.pallas_call(
        halo_kernel,
        out_shape=(
            jax.ShapeDtypeStruct((3 * blocks, LANES), jnp.float32),
            jax.ShapeDtypeStruct((3 * blocks + levels, LANES), jnp.float32),
            jax.ShapeDtypeStruct((blocks // 2 + ROWS, LANES), jnp.float32),
        ),
        compiler_params=pltpu.CompilerParams(vmem_limit_bytes=VMEM_BYTES),
        cost_estimate=pl.CostEstimate(flops=1000000, bytes_accessed=2000000, transcendentals=0),
        name="pack_halos",
    )(tracer_rows, courant_rows)


def face_weights(face_courant):
    half = 0.5 * face_courant
    upwind = face_courant > 0
    shrink_left = 1.0 - 2.0 / 3.0 * face_courant
    shrink_right = 1.0 + 2.0 / 3.0 * face_courant
    curve = half * jnp.where(upwind, shrink_left, shrink_right)
    middle = face_courant * jnp.where(upwind, 1.0 - half - 3.0 * curve, 1.0 + half + 3.0 * curve)
    left_edge = face_courant * jnp.where(upwind, half - 3.0 * curve, 0.0)
    right_edge = face_courant * jnp.where(upwind, 0.0, 3.0 * curve - half)
    left_cell = face_courant * jnp.where(upwind, 6.0 * curve, 0.0)
    right_cell = face_courant * jnp.where(upwind, 0.0, -6.0 * curve)
    near, far = 7.0 / 12.0, 1.0 / 12.0
    return [
        -far * left_edge,
        near * left_edge - far * middle,
        near * (middle + left_edge) - far * right_edge + left_cell,
        near * (middle + right_edge) - far * left_edge + right_cell,
        near * right_edge - far * middle,
        -far * right_edge,
    ]


def divergence_weights(face_after, face_before):
    after = face_weights(face_after)
    before = face_weights(face_before)
    taps = []
    for offset in range(7):
        if offset == 0:
            taps.append(-before[0])
        elif offset == 6:
            taps.append(after[5])
        else:
            taps.append(after[offset - 1] - before[offset])
    return taps


def advect_kernel(
    lat_ref, tracer_ref, courant_ref, mixing_ref, south_ref, north_ref, west_ref, east_ref,
    out_ref, response_ref, rows_ref, side_ref, weight_ref, pivot_ref,
):
    levels = mixing_ref.shape[0] + 1
    members = tracer_ref.shape[0]
    blocks = members * levels
    lat = lat_ref[0]
    first = lat == 0
    last = lat == lat_ref[1] - 1
    zero = jnp.zeros((blocks, LANES), jnp.float32)
    for step in range(3):
        span = slice(step * blocks, (step + 1) * blocks)
        rows_ref[pl.ds(ROWS - 3 + step, blocks, stride=ROWS), :] = jnp.where(
            first, zero, south_ref[span, :]
        )
        rows_ref[pl.ds(step, blocks, stride=ROWS), :] = jnp.where(last, zero, north_ref[span, :])
    lane = lax.broadcasted_iota(jnp.int32, (ROWS, LANES), 1)
    row = lax.broadcasted_iota(jnp.int32, (ROWS, LANES), 0)
    from_west = lane % 8 < 3
    for group in range(blocks // 16):
        span = slice(group * ROWS, (group + 1) * ROWS)
        side_ref[span, :] = jnp.where(from_west, west_ref[span, :], east_ref[span, :])

    side_courant = west_ref[blocks // 2 : blocks // 2 + ROWS, :]
    for level in range(levels):
        east_face = courant_ref[0, level]
        west_cell = pltpu.roll(side_courant, LANES - 3 - 8 * level, 1)
        west_face = pltpu.roll(jnp.where(lane == LANES - 1, west_cell, east_face), 1, 1)
        north_face = courant_ref[1, level]
        below = jnp.where(first, 0.0, south_ref[3 * blocks + level : 3 * blocks + level + 1, :])
        south_face = jnp.where(row == 0, below, pltpu.roll(north_face, 1, 0))
        north_face = jnp.where(jnp.logical_and(last, row == ROWS - 1), 0.0, north_face)
        along_lon = divergence_weights(east_face, west_face)
        along_lat = divergence_weights(north_face, south_face)
        weight_ref[level, 0] = 1.0 - along_lon[3] - along_lat[3]
        for place, offset in enumerate((0, 1, 2, 4, 5, 6)):
            weight_ref[level, 1 + place] = -along_lon[offset]
            weight_ref[level, 7 + place] = -along_lat[offset]

    ratio = None
    response = []
    for level in range(levels):
        pivot = jnp.ones((ROWS, LANES), jnp.float32)
        if level > 0:
            pivot = pivot + mixing_ref[level - 1]
        if level < levels - 1:
            pivot = pivot + mixing_ref[level]
        if level > 0:
            pivot = pivot - mixing_ref[level - 1] * ratio
        inverse = 1.0 / pivot
        carried = inverse
        if level > 0:
            carried = mixing_ref[level - 1] * inverse
            response.append(carried * response[-1])
        else:
            response.append(inverse)
        pivot_ref[level, 0] = inverse
        pivot_ref[level, 1] = carried
        if level < levels - 1:
            ratio = mixing_ref[level] * inverse
            pivot_ref[level, 2] = ratio
    for level in range(levels - 1, -1, -1):
        if level < levels - 1:
            response[level] = response[level] + pivot_ref[level, 2] * response[level + 1]
        response_ref[level] = response[level]

    together = 4

    def member_step(index, carry):
        start = index * together
        swept = [None] * together
        for level in range(levels):
            for step in range(together):
                member = start + step
                inside = (step % 2) * levels + level
                group = index * (together * levels // 16) + step * levels // 16
                cells = tracer_ref[member, level]
                side = side_ref[pl.ds(pl.multiple_of(group * ROWS, ROWS), ROWS), :]
                side = pltpu.roll(side, LANES - 3 - 8 * inside, 1)
                edge = rows_ref[
                    pl.ds(pl.multiple_of((member * levels + level) * ROWS, ROWS), ROWS), :
                ]
                total = weight_ref[level, 0] * cells
                for place, shift in enumerate((3, 2, 1)):
                    padded = jnp.where(lane >= LANES - shift, side, cells)
                    total = total + weight_ref[level, 1 + place] * pltpu.roll(padded, shift, 1)
                for place, shift in enumerate((1, 2, 3)):
                    padded = jnp.where(lane < shift, side, cells)
                    total = total + weight_ref[level, 4 + place] * pltpu.roll(
                        padded, LANES - shift, 1
                    )
                for place, shift in enumerate((3, 2, 1)):
                    padded = jnp.where(row >= ROWS - shift, edge, cells)
                    total = total + weight_ref[level, 7 + place] * pltpu.roll(padded, shift, 0)
                for place, shift in enumerate((1, 2, 3)):
                    padded = jnp.where(row < shift, edge, cells)
                    total = total + weight_ref[level, 10 + place] * pltpu.roll(
                        padded, ROWS - shift, 0
                    )
                total = total * pivot_ref[level, 0]
                if level > 0:
                    total = total + pivot_ref[level, 1] * swept[step]
                swept[step] = total
                out_ref[member, level] = total
        for level in range(levels - 2, -1, -1):
            for step in range(together):
                member = start + step
                swept[step] = out_ref[member, level] + pivot_ref[level, 2] * swept[step]
                out_ref[member, level] = swept[step]
        return carry

    lax.fori_loop(0, members // together, member_step, 0)


def advect_and_mix(lat_place, tracer, courant, mixing, south, north, west, east):
    members, levels, rows, lanes = tracer.shape
    blocks = members * levels
    vmem = pl.BlockSpec(memory_space=pltpu.VMEM)
    return pl.pallas_call(
        advect_kernel,
        out_shape=(
            jax.ShapeDtypeStruct(tracer.shape, jnp.float32),
            jax.ShapeDtypeStruct((levels, rows, lanes), jnp.float32),
        ),
        in_specs=[pl.BlockSpec(memory_space=pltpu.SMEM)] + [vmem] * 7,
        out_specs=(vmem, vmem),
        scratch_shapes=[
            pltpu.VMEM((blocks * ROWS, LANES), jnp.float32),
            pltpu.VMEM((blocks // 2, LANES), jnp.float32),
            pltpu.VMEM((levels, 13, ROWS, LANES), jnp.float32),
            pltpu.VMEM((levels, 3, ROWS, LANES), jnp.float32),
        ],
        compiler_params=pltpu.CompilerParams(vmem_limit_bytes=VMEM_BYTES),
        cost_estimate=pl.CostEstimate(flops=12000000, bytes_accessed=4000000, transcendentals=0),
        name="advect_and_mix",
    )(lat_place, tracer, courant, mixing, south, north, west, east)


def arrhenius(energy, leaf_temp):
    return jnp.exp(energy * (leaf_temp - 25.0) / (298.15 * GAS_CONSTANT * (leaf_temp + 273.15)))


def flux_kernel(
    received_ref, cell_ref, params_ref, bottom_ref, partial_ref, response_ref,
    out_ref, surface_ref, table_ref, bottom_rows_ref, column_ref, index_ref, left_ref, right_ref,
):
    members = params_ref.shape[1]
    types = params_ref.shape[2]
    sources, places = cell_ref.shape
    groups = sources // 2
    levels = response_ref.shape[0]

    carbox = 30.0 + 70.0 * params_ref[0]
    table_ref[0, :, 0:types] = carbox
    table_ref[1, :, 0:types] = (1.4 + 0.8 * params_ref[1]) * carbox
    table_ref[2, :, 0:types] = (0.005 + 0.025 * params_ref[2]) * carbox
    for row in range(ROWS):
        bottom_rows_ref[row] = 0.7 * (400.0 + 100.0 * bottom_ref[:, 0, row, :])

    half = lax.broadcasted_iota(jnp.int32, (groups, LANES), 1) < places

    def pair(values):
        low, high = values[0:groups], values[groups : 2 * groups]
        return (
            jnp.where(half, low, pltpu.roll(high, places, 1)),
            jnp.where(half, pltpu.roll(low, places, 1), high),
        )

    light, leaf_temp = pair(received_ref[:, 0, 0:LANES])
    water, flux_scale = pair(received_ref[:, 0, LANES : 2 * LANES])
    plant, _ = pair(received_ref[:, 0, 2 * LANES : 3 * LANES])
    leaf_temp = 35.0 * leaf_temp
    column_ref[0] = 0.425 * (2000.0 * light)
    column_ref[1] = arrhenius(65330.0, leaf_temp) * (0.2 + 0.8 * water)
    column_ref[2] = arrhenius(43540.0, leaf_temp)
    michaelis_carbon = 404.9 * arrhenius(79430.0, leaf_temp)
    michaelis_oxygen = 278.4 * arrhenius(36380.0, leaf_temp)
    column_ref[3] = michaelis_carbon * (1.0 + 210.0 / michaelis_oxygen)
    column_ref[4] = 42.75 * arrhenius(37830.0, leaf_temp)
    column_ref[5] = flux_scale
    index_ref[0] = plant.astype(jnp.int32)
    cells = cell_ref[...]
    cells = jnp.concatenate([cells[0:groups], cells[groups : 2 * groups]], axis=1)
    index_ref[1] = jnp.right_shift(cells, 7)
    index_ref[2] = jnp.bitwise_and(cells, LANES - 1)

    lane_ids = lax.broadcasted_iota(jnp.int32, (LANES, LANES), 0)

    def group_step(group, carry):
        def spread(ref, quantity):
            return jnp.broadcast_to(ref[quantity, pl.ds(group, 1), :], (members, LANES))

        plant_index = spread(index_ref, 0)
        row_index = spread(index_ref, 1)
        lane_index = spread(index_ref, 2)

        def pick(table, index):
            return jnp.take_along_axis(table, index, axis=1, mode="promise_in_bounds")

        carbon_leaf = pick(bottom_rows_ref[0], lane_index)
        for row in range(1, ROWS):
            carbon_leaf = jnp.where(
                row_index == row, pick(bottom_rows_ref[row], lane_index), carbon_leaf
            )
        absorbed = spread(column_ref, 0)
        warm = spread(column_ref, 1)
        carboxylation = pick(table_ref[0], plant_index) * warm
        transport_max = pick(table_ref[1], plant_index) * spread(column_ref, 2)
        respiration = pick(table_ref[2], plant_index) * warm
        compensation = spread(column_ref, 4)
        total_rate = absorbed + transport_max
        electron_rate = (
            total_rate - jnp.sqrt(total_rate * total_rate - 2.8 * absorbed * transport_max)
        ) / 1.4
        excess = carbon_leaf - compensation
        rubisco_rate = carboxylation * excess / (carbon_leaf + spread(column_ref, 3))
        light_rate = electron_rate * excess / (4.0 * carbon_leaf + 8.0 * compensation)
        flux = spread(column_ref, 5) * (jnp.minimum(rubisco_rate, light_rate) - respiration)
        high, low = bf16_parts(flux, 2)
        span = pl.ds(pl.multiple_of(group * LANES, LANES), LANES)
        zero = jnp.zeros((members, LANES), jnp.bfloat16)
        for row in range(ROWS):
            here = (row_index == row).astype(jnp.float32).astype(jnp.bfloat16)
            left_ref[pl.ds(row * 2 * members, members), span] = high * here
            left_ref[pl.ds(row * 2 * members + members, members), span] = low * here
        lane_row = index_ref[2, pl.ds(group, 1), :]
        right_ref[:, span] = (lane_ids == lane_row).astype(jnp.float32).astype(jnp.bfloat16)
        return carry

    lax.fori_loop(0, groups, group_step, 0)
    summed = nt_dot(left_ref[...], right_ref[...])
    for row in range(ROWS):
        start = row * 2 * members
        surface_ref[:, row, :] = (
            summed[start : start + members] + summed[start + members : start + 2 * members]
        )

    def member_step(member, carry):
        surface = surface_ref[member]
        for level in range(levels):
            out_ref[member, level] = partial_ref[member, level] + response_ref[level] * surface
        return carry

    lax.fori_loop(0, members, member_step, 0, unroll=2)


def fluxes(received, recv_cell, land_params, tracer, partial, response):
    members, levels, rows, lanes = tracer.shape
    tiles = received.shape[0]
    place_count = recv_cell.shape[0] * recv_cell.shape[1]

    def whole(array):
        return pl.BlockSpec(array.shape, lambda step: (0,) * array.ndim)

    return pl.pallas_call(
        flux_kernel,
        out_shape=(
            jax.ShapeDtypeStruct(tracer.shape, jnp.float32),
            jax.ShapeDtypeStruct((members, rows, lanes), jnp.float32),
        ),
        in_specs=[
            whole(received),
            whole(recv_cell),
            whole(land_params),
            pl.BlockSpec((members, 1, rows, lanes), lambda step: (0, 0, 0, 0)),
            whole(partial),
            whole(response),
        ],
        out_specs=(
            pl.BlockSpec(tracer.shape, lambda step: (0, 0, 0, 0)),
            pl.BlockSpec((members, rows, lanes), lambda step: (0, 0, 0)),
        ),
        grid=(1,),
        scratch_shapes=[
            pltpu.VMEM((3, members, LANES), jnp.float32),
            pltpu.VMEM((ROWS, members, LANES), jnp.float32),
            pltpu.VMEM((6, tiles // 2, LANES), jnp.float32),
            pltpu.VMEM((3, tiles // 2, LANES), jnp.int32),
            pltpu.VMEM((2 * ROWS * members, place_count), jnp.bfloat16),
            pltpu.VMEM((LANES, place_count), jnp.bfloat16),
        ],
        compiler_params=pltpu.CompilerParams(vmem_limit_bytes=VMEM_BYTES),
        cost_estimate=pl.CostEstimate(flops=600000000, bytes_accessed=3000000, transcendentals=400000),
        name="fluxes",
    )(received, recv_cell, land_params, tracer, partial, response)


def per_device(tracer, courant, mixing, forcing, plant_type, land_params, send_slot, recv_cell):
    members, levels, row_count, column_count = tracer.shape
    lon_count, lat_count = lax.axis_size("lon"), lax.axis_size("lat")
    low, high, side = pack_halos(
        tracer.reshape(members * levels * row_count, column_count),
        courant.reshape(2 * levels * row_count, column_count),
    )
    north = lax.ppermute(low, "lat", [((i + 1) % lat_count, i) for i in range(lat_count)])
    south = lax.ppermute(high, "lat", [(i, (i + 1) % lat_count) for i in range(lat_count)])
    west = lax.ppermute(side, "lon", [(i, (i + 1) % lon_count) for i in range(lon_count)])
    east = lax.ppermute(side, "lon", [((i + 1) % lon_count, i) for i in range(lon_count)])
    outgoing = pack_columns(forcing, plant_type, send_slot, lon_count * lat_count)
    received = lax.all_to_all(outgoing, ("lon", "lat"), split_axis=0, concat_axis=0, tiled=True)
    lat_place = jnp.stack([lax.axis_index("lat"), jnp.int32(lat_count)]).astype(jnp.int32)
    partial, response = advect_and_mix(
        lat_place, tracer, courant, mixing, south, north, west, east
    )
    return fluxes(received, recv_cell, land_params, tracer, partial, response)


def solution(mesh):
    in_specs = (
        P("mem", None, "lat", "lon"),
        P(None, None, "lat", "lon"),
        P(None, "lat", "lon"),
        P(None, ("lon", "lat")),
        P(("lon", "lat")),
        P(None, "mem", None),
        P(("lon", "lat")),
        P(("lon", "lat"), None),
    )
    out_specs = (P("mem", None, "lat", "lon"), P("mem", "lat", "lon"))
    return jax.shard_map(
        per_device, mesh=mesh, in_specs=in_specs, out_specs=out_specs, check_vma=False
    )
```

```python
import functools

import jax
import jax.numpy as jnp
from jax import lax
from jax.experimental import pallas as pl
from jax.experimental.pallas import tpu as pltpu
from jax.sharding import PartitionSpec as P

FLUX_SCALE = 0.02
GAS_CONSTANT = 8.314
LANES = 128
ROWS = 8
VMEM_BYTES = 40 * 2**20
PACK_VMEM_BYTES = 58 * 2**20
PARTS = 2
ADVECT_BYTES = 4000000


def nt_dot(left, right):
    return lax.dot_general(
        left, right, (((1,), (1,)), ((), ())), preferred_element_type=jnp.float32
    )


def bf16_parts(values, count):
    parts = []
    rest = values
    for _ in range(count):
        part = rest.astype(jnp.bfloat16)
        rest = rest - part.astype(jnp.float32)
        parts.append(part)
    return parts


def pack_kernel(
    tracer_hbm, courant_hbm, forcing_hbm, type_hbm, slot_hbm,
    payload_ref, low_ref, high_ref, westward_ref, eastward_ref,
    cells_ref, faces_ref, forcing_ref, type_ref, slot_ref, copy_sems,
):
    moves = (
        (slot_hbm, slot_ref),
        (forcing_hbm, forcing_ref),
        (type_hbm, type_ref),
        (tracer_hbm, cells_ref),
        (courant_hbm, faces_ref),
    )
    copies = [
        pltpu.make_async_copy(source, target, copy_sems.at[place])
        for place, (source, target) in enumerate(moves)
    ]
    for copy in copies:
        copy.start()
    for copy in copies[0:3]:
        copy.wait()

    columns = slot_ref.shape[1]
    slot = slot_ref[...]
    lon_tile = jnp.right_shift(slot, 8).astype(jnp.float32).astype(jnp.bfloat16)
    place = jnp.bitwise_and(slot, 255).astype(jnp.float32).astype(jnp.bfloat16)
    one, zero = jnp.bfloat16(1.0), jnp.bfloat16(0.0)

    def ids(count):
        return (
            lax.broadcasted_iota(jnp.int32, (count, columns), 0)
            .astype(jnp.float32)
            .astype(jnp.bfloat16)
        )

    tile_mask = ids(16) == lon_tile
    place_onehot = jnp.where(ids(256) == place, one, zero)
    leaf_area = 0.5 + 5.5 * forcing_ref[3:4, :]
    area_share = 0.05 + 0.55 * forcing_ref[4:5, :]
    canopy_scale = (1.0 - jnp.exp(-0.5 * leaf_area)) / 0.5
    values = [
        (forcing_ref[0:1, :], PARTS),
        (forcing_ref[1:2, :], PARTS),
        (forcing_ref[2:3, :], PARTS),
        (-FLUX_SCALE * area_share * canopy_scale, PARTS),
        (type_ref[...].astype(jnp.float32), 1),
    ]
    rows = []
    for value, count in values:
        for part in bf16_parts(value, count):
            rows.append(jnp.where(tile_mask, jnp.broadcast_to(part, (16, columns)), zero))
    moved = nt_dot(jnp.concatenate(rows, axis=0), place_onehot)
    placed = []
    start = 0
    for value, count in values:
        total = moved[start : start + 16]
        for step in range(1, count):
            total = total + moved[start + 16 * step : start + 16 * (step + 1)]
        placed.append(total)
        start += 16 * count
    low_half = lax.broadcasted_iota(jnp.int32, (16, LANES), 1) < 64
    for tile in range(4):
        span = slice((tile // 2) * LANES, (tile // 2 + 1) * LANES)
        for pair in range(3):
            left = placed[2 * pair][:, span]
            right = placed[min(2 * pair + 1, 4)][:, span]
            if tile % 2 == 0:
                joined = jnp.where(low_half, left, pltpu.roll(right, 64, 1))
            else:
                joined = jnp.where(low_half, pltpu.roll(left, 64, 1), right)
            payload_ref[tile * 16 : (tile + 1) * 16, 0, pair * LANES : (pair + 1) * LANES] = joined

    for copy in copies[3:5]:
        copy.wait()
    blocks = cells_ref.shape[0] // ROWS
    levels = faces_ref.shape[0] // (2 * ROWS)
    for step in range(3):
        low_ref[step * blocks : (step + 1) * blocks, :] = cells_ref[
            pl.ds(step, blocks, stride=ROWS), :
        ]
        high_ref[step * blocks : (step + 1) * blocks, :] = cells_ref[
            pl.ds(ROWS - 3 + step, blocks, stride=ROWS), :
        ]
    high_ref[3 * blocks : 3 * blocks + levels, :] = faces_ref[
        pl.ds(levels * ROWS + ROWS - 1, levels, stride=ROWS), :
    ]
    squares = cells_ref.shape[0] // LANES
    for square in range(squares):
        turned = cells_ref[square * LANES : (square + 1) * LANES, :].T
        westward_ref[3 * square : 3 * square + 3, :] = turned[0:3]
        eastward_ref[3 * square : 3 * square + 3, :] = turned[LANES - 3 : LANES]
    turned = faces_ref[...].T
    westward_ref[3 * squares : 3 * squares + ROWS, :] = turned[LANES - ROWS : LANES]
    eastward_ref[3 * squares : 3 * squares + ROWS, :] = turned[LANES - ROWS : LANES]


def pack(tracer_rows, courant_rows, forcing, plant_type, send_slot, tiles):
    columns = send_slot.shape[0]
    blocks = tracer_rows.shape[0] // ROWS
    levels = courant_rows.shape[0] // (2 * ROWS)
    side_rows = 3 * (tracer_rows.shape[0] // LANES) + ROWS
    vmem = pl.BlockSpec(memory_space=pltpu.VMEM)
    hbm = pl.BlockSpec(memory_space=pltpu.HBM)
    return pl.pallas_call(
        pack_kernel,
        out_shape=(
            jax.ShapeDtypeStruct((tiles, 1, 3 * LANES), jnp.float32),
            jax.ShapeDtypeStruct((3 * blocks, LANES), jnp.float32),
            jax.ShapeDtypeStruct((3 * blocks + levels, LANES), jnp.float32),
            jax.ShapeDtypeStruct((side_rows, LANES), jnp.float32),
            jax.ShapeDtypeStruct((side_rows, LANES), jnp.float32),
        ),
        in_specs=[hbm] * 5,
        out_specs=(vmem,) * 5,
        scratch_shapes=[
            pltpu.VMEM(tracer_rows.shape, jnp.float32),
            pltpu.VMEM(courant_rows.shape, jnp.float32),
            pltpu.VMEM(forcing.shape, jnp.float32),
            pltpu.VMEM((1, columns), jnp.int32),
            pltpu.VMEM((1, columns), jnp.int32),
            pltpu.SemaphoreType.DMA((5,)),
        ],
        compiler_params=pltpu.CompilerParams(vmem_limit_bytes=PACK_VMEM_BYTES),
        cost_estimate=pl.CostEstimate(
            flops=300000000, bytes_accessed=2500000, transcendentals=columns
        ),
        name="pack",
    )(
        tracer_rows, courant_rows, forcing,
        plant_type.reshape(1, columns), send_slot.reshape(1, columns),
    )


def face_weights(face_courant):
    half = 0.5 * face_courant
    upwind = face_courant > 0
    shrink_left = 1.0 - 2.0 / 3.0 * face_courant
    shrink_right = 1.0 + 2.0 / 3.0 * face_courant
    curve = half * jnp.where(upwind, shrink_left, shrink_right)
    middle = face_courant * jnp.where(upwind, 1.0 - half - 3.0 * curve, 1.0 + half + 3.0 * curve)
    left_edge = face_courant * jnp.where(upwind, half - 3.0 * curve, 0.0)
    right_edge = face_courant * jnp.where(upwind, 0.0, 3.0 * curve - half)
    left_cell = face_courant * jnp.where(upwind, 6.0 * curve, 0.0)
    right_cell = face_courant * jnp.where(upwind, 0.0, -6.0 * curve)
    near, far = 7.0 / 12.0, 1.0 / 12.0
    return [
        -far * left_edge,
        near * left_edge - far * middle,
        near * (middle + left_edge) - far * right_edge + left_cell,
        near * (middle + right_edge) - far * left_edge + right_cell,
        near * right_edge - far * middle,
        -far * right_edge,
    ]


def divergence_weights(face_after, face_before):
    after = face_weights(face_after)
    before = face_weights(face_before)
    taps = []
    for offset in range(7):
        if offset == 0:
            taps.append(-before[0])
        elif offset == 6:
            taps.append(after[5])
        else:
            taps.append(after[offset - 1] - before[offset])
    return taps


TURNED_ROWS = LANES + 16
PADDED_ROWS = 2 * ROWS


def advect_kernel(
    lat_ref, tracer_ref, courant_ref, mixing_ref, south_ref, north_ref, west_ref, east_ref,
    out_ref, response_ref,
    turned_ref, turned_sum_ref, turned_courant_ref, lon_ref, rows_ref, weight_ref, pivot_ref,
):
    levels = mixing_ref.shape[0] + 1
    members = out_ref.shape[0]
    blocks = members * levels
    squares = blocks * ROWS // LANES
    first = lat_ref[0] == 0
    last = lat_ref[0] == lat_ref[1] - 1

    for square in range(squares):
        base = square * TURNED_ROWS
        turned_ref[base + 5 : base + 8, :] = west_ref[3 * square : 3 * square + 3, :]
        turned_ref[base + 8 + LANES : base + 11 + LANES, :] = east_ref[
            3 * square : 3 * square + 3, :
        ]
        turned_ref[base + 8 : base + 8 + LANES, :] = tracer_ref[
            square * LANES : (square + 1) * LANES, :
        ].T
    half = levels * ROWS
    turned_faces = courant_ref[...].T
    low_half = lax.broadcasted_iota(jnp.int32, (LANES, LANES), 1) < half
    turned_faces = jnp.where(low_half, turned_faces, pltpu.roll(turned_faces, half, 1))
    turned_courant_ref[8 : 8 + LANES, :] = turned_faces
    side_face = west_ref[3 * squares : 3 * squares + ROWS, :]
    side_face = jnp.where(low_half[0:ROWS], side_face, pltpu.roll(side_face, half, 1))
    turned_courant_ref[0:8, :] = side_face

    def lon_step(tile, carry):
        start = pl.multiple_of(tile * ROWS, ROWS)
        taps = divergence_weights(
            turned_courant_ref[pl.ds(start + 8, ROWS), :],
            turned_courant_ref[pl.ds(start + 7, ROWS), :],
        )
        for square in range(squares):
            base = square * TURNED_ROWS + start + 5
            total = taps[0] * turned_ref[pl.ds(base, ROWS), :]
            for offset in range(1, 7):
                total = total + taps[offset] * turned_ref[pl.ds(base + offset, ROWS), :]
            turned_sum_ref[pl.ds(square * LANES + start, ROWS), :] = total
        return carry

    lax.fori_loop(0, LANES // ROWS, lon_step, 0)
    for square in range(squares):
        span = slice(square * LANES, (square + 1) * LANES)
        lon_ref[span, :] = turned_sum_ref[span, :].T

    zero = jnp.zeros((blocks, LANES), jnp.float32)
    for step in range(3):
        span = slice(step * blocks, (step + 1) * blocks)
        rows_ref[pl.ds(5 + step, blocks, stride=PADDED_ROWS), :] = jnp.where(
            first, zero, south_ref[span, :]
        )
        rows_ref[pl.ds(PADDED_ROWS + step, blocks, stride=PADDED_ROWS), :] = jnp.where(
            last, zero, north_ref[span, :]
        )
    for block in range(blocks):
        rows_ref[block * PADDED_ROWS + 8 : block * PADDED_ROWS + 16, :] = tracer_ref[
            block * ROWS : (block + 1) * ROWS, :
        ]
    row = lax.broadcasted_iota(jnp.int32, (ROWS, LANES), 0)
    for level in range(levels):
        north_face = courant_ref[half + level * ROWS : half + (level + 1) * ROWS, :]
        below = jnp.where(first, 0.0, south_ref[3 * blocks + level : 3 * blocks + level + 1, :])
        south_face = jnp.where(row == 0, below, pltpu.roll(north_face, 1, 0))
        north_face = jnp.where(jnp.logical_and(last, row == ROWS - 1), 0.0, north_face)
        taps = divergence_weights(north_face, south_face)
        for offset in range(7):
            weight_ref[level, offset] = 1.0 - taps[3] if offset == 3 else -taps[offset]

    ratio = None
    response = []
    for level in range(levels):
        pivot = jnp.ones((ROWS, LANES), jnp.float32)
        if level > 0:
            pivot = pivot + mixing_ref[level - 1]
        if level < levels - 1:
            pivot = pivot + mixing_ref[level]
        if level > 0:
            pivot = pivot - mixing_ref[level - 1] * ratio
        inverse = 1.0 / pivot
        carried = inverse
        if level > 0:
            carried = mixing_ref[level - 1] * inverse
            response.append(carried * response[-1])
        else:
            response.append(inverse)
        pivot_ref[level, 0] = inverse
        pivot_ref[level, 1] = carried
        if level < levels - 1:
            ratio = mixing_ref[level] * inverse
            pivot_ref[level, 2] = ratio
    for level in range(levels - 1, -1, -1):
        if level < levels - 1:
            response[level] = response[level] + pivot_ref[level, 2] * response[level + 1]
        response_ref[level] = response[level]

    together = 4

    def member_step(index, carry):
        swept = [None] * together
        stored = [[None] * levels for _ in range(together)]
        for level in range(levels):
            for step in range(together):
                block = (index * together + step) * levels + level
                base = pl.multiple_of(block * PADDED_ROWS, PADDED_ROWS)
                total = -lon_ref[pl.ds(pl.multiple_of(block * ROWS, ROWS), ROWS), :]
                for offset in range(7):
                    total = (
                        total
                        + weight_ref[level, offset] * rows_ref[pl.ds(base + 5 + offset, ROWS), :]
                    )
                total = total * pivot_ref[level, 0]
                if level > 0:
                    total = total + pivot_ref[level, 1] * swept[step]
                swept[step] = total
                stored[step][level] = total
        for level in range(levels - 1, -1, -1):
            for step in range(together):
                if level < levels - 1:
                    swept[step] = stored[step][level] + pivot_ref[level, 2] * swept[step]
                out_ref[index * together + step, level] = swept[step]
        return carry

    lax.fori_loop(0, members // together, member_step, 0)


def advect_and_mix(lat_place, tracer_rows, courant_rows, mixing, south, north, west, east):
    levels, rows, lanes = mixing.shape[0] + 1, mixing.shape[1], mixing.shape[2]
    blocks = tracer_rows.shape[0] // rows
    members = blocks // levels
    squares = tracer_rows.shape[0] // lanes
    vmem = pl.BlockSpec(memory_space=pltpu.VMEM)
    return pl.pallas_call(
        advect_kernel,
        out_shape=(
            jax.ShapeDtypeStruct((members, levels, rows, lanes), jnp.float32),
            jax.ShapeDtypeStruct((levels, rows, lanes), jnp.float32),
        ),
        in_specs=[pl.BlockSpec(memory_space=pltpu.SMEM)] + [vmem] * 7,
        out_specs=(vmem, vmem),
        scratch_shapes=[
            pltpu.VMEM((squares * TURNED_ROWS, LANES), jnp.float32),
            pltpu.VMEM((squares * LANES, LANES), jnp.float32),
            pltpu.VMEM((LANES + 8, LANES), jnp.float32),
            pltpu.VMEM((squares * LANES, LANES), jnp.float32),
            pltpu.VMEM(((blocks + 1) * PADDED_ROWS, LANES), jnp.float32),
            pltpu.VMEM((levels, 7, ROWS, LANES), jnp.float32),
            pltpu.VMEM((levels, 3, ROWS, LANES), jnp.float32),
        ],
        compiler_params=pltpu.CompilerParams(vmem_limit_bytes=VMEM_BYTES),
        cost_estimate=pl.CostEstimate(flops=12000000, bytes_accessed=ADVECT_BYTES, transcendentals=0),
        name="advect_and_mix",
    )(lat_place, tracer_rows, courant_rows, mixing, south, north, west, east)


def arrhenius(energy, leaf_temp):
    return jnp.exp(energy * (leaf_temp - 25.0) / (298.15 * GAS_CONSTANT * (leaf_temp + 273.15)))


CHUNK = 4


def flux_kernel(
    received_ref, cell_ref, params_ref, bottom_ref, partial_ref, response_ref,
    out_ref, surface_ref,
    column_ref, left_ref, right_ref, result_ref, copy_sems,
):
    members = params_ref.shape[1]
    types = params_ref.shape[2]
    sources, places = cell_ref.shape
    groups = sources // 2
    levels = response_ref.shape[0]
    quarters = ROWS // 2
    one, zero = jnp.bfloat16(1.0), jnp.bfloat16(0.0)

    carbox = 30.0 + 70.0 * params_ref[0]
    tables = jnp.concatenate(
        [carbox, (1.4 + 0.8 * params_ref[1]) * carbox, (0.005 + 0.025 * params_ref[2]) * carbox],
        axis=0,
    )
    table_parts = jnp.concatenate(bf16_parts(tables, 2), axis=1)
    bottom = jnp.concatenate(
        [
            jnp.concatenate(
                [bottom_ref[:, 0, 2 * quarter, :], bottom_ref[:, 0, 2 * quarter + 1, :]], axis=1
            )
            for quarter in range(quarters)
        ],
        axis=0,
    )
    bottom_parts = jnp.concatenate(bf16_parts(bottom, 2), axis=0)

    half = lax.broadcasted_iota(jnp.int32, (groups, LANES), 1) < places

    def pair(values):
        low, high = values[0:groups], values[groups : 2 * groups]
        return (
            jnp.where(half, low, pltpu.roll(high, places, 1)),
            jnp.where(half, pltpu.roll(low, places, 1), high),
        )

    light, leaf_temp = pair(received_ref[:, 0, 0:LANES])
    water, flux_scale = pair(received_ref[:, 0, LANES : 2 * LANES])
    plant, _ = pair(received_ref[:, 0, 2 * LANES : 3 * LANES])
    leaf_temp = 35.0 * leaf_temp
    absorbed = 0.425 * (2000.0 * light)
    michaelis_carbon = 404.9 * arrhenius(79430.0, leaf_temp)
    michaelis_oxygen = 278.4 * arrhenius(36380.0, leaf_temp)
    compensation = 42.75 * arrhenius(37830.0, leaf_temp)
    column_ref[0] = absorbed
    column_ref[1] = arrhenius(65330.0, leaf_temp) * (0.2 + 0.8 * water)
    column_ref[2] = arrhenius(43540.0, leaf_temp)
    column_ref[3] = michaelis_carbon * (1.0 + 210.0 / michaelis_oxygen)
    column_ref[4] = compensation
    column_ref[5] = flux_scale
    column_ref[6] = 2.8 * absorbed
    column_ref[7] = (1.4 * 8.0) * compensation
    column_ref[8] = plant
    cells = jnp.concatenate(
        [cell_ref[pl.ds(tile, sources // 4, stride=4), :] for tile in range(4)], axis=0
    )
    cells = jnp.concatenate([cells[0:groups], cells[groups : 2 * groups]], axis=1)
    column_ref[9] = jnp.right_shift(cells, 8).astype(jnp.float32)
    column_ref[10] = jnp.bitwise_and(cells, 255).astype(jnp.float32)

    def ids(count, mask):
        return (
            jnp.bitwise_and(lax.broadcasted_iota(jnp.int32, (count, LANES), 0), mask)
            .astype(jnp.float32)
            .astype(jnp.bfloat16)
        )

    cell_ids = ids(256, 255)
    type_ids = ids(2 * types, types - 1)

    for chunk in range(groups // CHUNK):
        rows = range(chunk * CHUNK, (chunk + 1) * CHUNK)
        span = slice(chunk * CHUNK * LANES, (chunk + 1) * CHUNK * LANES)

        def spread(quantity, count=members):
            return jnp.concatenate(
                [
                    jnp.broadcast_to(column_ref[quantity, row : row + 1, :], (count, LANES))
                    for row in rows
                ],
                axis=1,
            )

        def onehot(row_ids, quantity):
            return jnp.concatenate(
                [
                    jnp.where(
                        row_ids == column_ref[quantity, row : row + 1, :].astype(jnp.bfloat16),
                        one,
                        zero,
                    )
                    for row in rows
                ],
                axis=1,
            )

        cell_onehot = onehot(cell_ids, 10)
        right_ref[:, span] = cell_onehot
        near = jnp.dot(bottom_parts, cell_onehot, preferred_element_type=jnp.float32)
        near = near[0 : quarters * members] + near[quarters * members : 2 * quarters * members]
        quarter_index = spread(9)
        picked = near[0:members]
        for quarter in range(1, quarters):
            picked = jnp.where(
                quarter_index == quarter, near[quarter * members : (quarter + 1) * members], picked
            )
        params = jnp.dot(
            table_parts, onehot(type_ids, 8), preferred_element_type=jnp.float32
        )
        carbon_leaf = 280.0 + 70.0 * picked
        warm = spread(1)
        carboxylation = params[0:members] * warm
        transport_max = params[members : 2 * members] * spread(2)
        respiration = params[2 * members : 3 * members] * warm
        total_rate = spread(0) + transport_max
        square = total_rate * total_rate - spread(6) * transport_max
        electron_rate = total_rate - square * lax.rsqrt(square)
        excess = carbon_leaf - spread(4)
        rubisco_base = carbon_leaf + spread(3)
        light_base = (1.4 * 4.0) * carbon_leaf + spread(7)
        shared = excess / (rubisco_base * light_base)
        rubisco_rate = carboxylation * light_base * shared
        light_rate = electron_rate * rubisco_base * shared
        flux = spread(5) * (jnp.minimum(rubisco_rate, light_rate) - respiration)
        high, low = bf16_parts(flux, 2)
        quarter_index = quarter_index.astype(jnp.bfloat16)
        for quarter in range(quarters):
            here = quarter_index == jnp.bfloat16(quarter)
            start = quarter * 2 * members
            left_ref[start : start + members, span] = jnp.where(here, high, zero)
            left_ref[start + members : start + 2 * members, span] = jnp.where(here, low, zero)

    summed = nt_dot(left_ref[...], right_ref[...])
    for quarter in range(quarters):
        start = quarter * 2 * members
        total = summed[start : start + members] + summed[start + members : start + 2 * members]
        surface_ref[:, 2 * quarter, :] = total[:, 0:LANES]
        surface_ref[:, 2 * quarter + 1, :] = total[:, LANES : 2 * LANES]

    copies = []
    quarter = members // 4
    for part in range(4):

        def member_step(member, carry):
            surface = surface_ref[member]
            for level in range(levels):
                result_ref[member, level] = (
                    partial_ref[member, level] + response_ref[level] * surface
                )
            return carry

        lax.fori_loop(part * quarter, (part + 1) * quarter, member_step, 0, unroll=4)
        span = pl.ds(part * quarter, quarter)
        copy = pltpu.make_async_copy(result_ref.at[span], out_ref.at[span], copy_sems.at[part])
        copy.start()
        copies.append(copy)
    for copy in copies:
        copy.wait()


def fluxes(received, recv_cell, land_params, tracer, partial, response):
    members, levels, rows, lanes = tracer.shape
    tiles = received.shape[0]
    place_count = recv_cell.shape[0] * recv_cell.shape[1]

    def whole(array):
        return pl.BlockSpec(array.shape, lambda step: (0,) * array.ndim)

    return pl.pallas_call(
        flux_kernel,
        out_shape=(
            jax.ShapeDtypeStruct(tracer.shape, jnp.float32),
            jax.ShapeDtypeStruct((members, rows, lanes), jnp.float32),
        ),
        in_specs=[
            whole(received),
            whole(recv_cell),
            whole(land_params),
            pl.BlockSpec((members, 1, rows, lanes), lambda step: (0, 0, 0, 0)),
            whole(partial),
            whole(response),
        ],
        out_specs=(
            pl.BlockSpec(memory_space=pltpu.HBM),
            pl.BlockSpec((members, rows, lanes), lambda step: (0, 0, 0)),
        ),
        grid=(1,),
        scratch_shapes=[
            pltpu.VMEM((11, tiles // 2, LANES), jnp.float32),
            pltpu.VMEM((ROWS * members, place_count), jnp.bfloat16),
            pltpu.VMEM((256, place_count), jnp.bfloat16),
            pltpu.VMEM(tracer.shape, jnp.float32),
            pltpu.SemaphoreType.DMA((4,)),
        ],
        compiler_params=pltpu.CompilerParams(vmem_limit_bytes=VMEM_BYTES),
        cost_estimate=pl.CostEstimate(flops=600000000, bytes_accessed=3000000, transcendentals=400000),
        name="fluxes",
    )(received, recv_cell, land_params, tracer, partial, response)


def per_device(tracer, courant, mixing, forcing, plant_type, land_params, send_slot, recv_cell):
    members, levels, row_count, column_count = tracer.shape
    lon_count, lat_count = lax.axis_size("lon"), lax.axis_size("lat")
    tracer_rows = tracer.reshape(members * levels * row_count, column_count)
    courant_rows = courant.reshape(2 * levels * row_count, column_count)
    outgoing, low, high, westward, eastward = pack(
        tracer_rows, courant_rows, forcing, plant_type, send_slot, lon_count * lat_count
    )
    north = lax.ppermute(low, "lat", [((i + 1) % lat_count, i) for i in range(lat_count)])
    south = lax.ppermute(high, "lat", [(i, (i + 1) % lat_count) for i in range(lat_count)])
    west = lax.ppermute(eastward, "lon", [(i, (i + 1) % lon_count) for i in range(lon_count)])
    east = lax.ppermute(westward, "lon", [((i + 1) % lon_count, i) for i in range(lon_count)])
    received = lax.all_to_all(outgoing, ("lat", "lon"), split_axis=0, concat_axis=0, tiled=True)
    lat_place = jnp.stack([lax.axis_index("lat"), jnp.int32(lat_count)]).astype(jnp.int32)
    partial, response = advect_and_mix(
        lat_place, tracer_rows, courant_rows, mixing, south, north, west, east
    )
    return fluxes(received, recv_cell, land_params, tracer, partial, response)


def solution(mesh):
    in_specs = (
        P("mem", None, "lat", "lon"),
        P(None, None, "lat", "lon"),
        P(None, "lat", "lon"),
        P(None, ("lon", "lat")),
        P(("lon", "lat")),
        P(None, "mem", None),
        P(("lon", "lat")),
        P(("lon", "lat"), None),
    )
    out_specs = (P("mem", None, "lat", "lon"), P("mem", "lat", "lon"))
    return jax.shard_map(
        per_device, mesh=mesh, in_specs=in_specs, out_specs=out_specs, check_vma=False
    )
```

```python
import functools

import jax
import jax.numpy as jnp
from jax import lax
from jax.experimental import pallas as pl
from jax.experimental.pallas import tpu as pltpu
from jax.sharding import PartitionSpec as P

FLUX_SCALE = 0.02
GAS_CONSTANT = 8.314
LANES = 128
ROWS = 8
VMEM_BYTES = 40 * 2**20
PARTS = 2


def nt_dot(left, right):
    return lax.dot_general(
        left, right, (((1,), (1,)), ((), ())), preferred_element_type=jnp.float32
    )


def bf16_parts(values, count):
    parts = []
    rest = values
    for _ in range(count):
        part = rest.astype(jnp.bfloat16)
        rest = rest - part.astype(jnp.float32)
        parts.append(part)
    return parts


def pack_kernel(
    tracer_hbm, courant_hbm, forcing_hbm, type_hbm, slot_hbm,
    payload_ref, low_ref, high_ref, westward_ref, eastward_ref,
    cells_ref, faces_ref, forcing_ref, type_ref, slot_ref, copy_sems,
):
    moves = (
        (slot_hbm, slot_ref),
        (forcing_hbm, forcing_ref),
        (type_hbm, type_ref),
        (tracer_hbm, cells_ref),
        (courant_hbm, faces_ref),
    )
    copies = [
        pltpu.make_async_copy(source, target, copy_sems.at[place])
        for place, (source, target) in enumerate(moves)
    ]
    for copy in copies:
        copy.start()
    for copy in copies[0:3]:
        copy.wait()

    columns = slot_ref.shape[1]
    slot = slot_ref[...]
    lon_tile = jnp.right_shift(slot, 8).astype(jnp.float32).astype(jnp.bfloat16)
    place = jnp.bitwise_and(slot, 255).astype(jnp.float32).astype(jnp.bfloat16)
    one, zero = jnp.bfloat16(1.0), jnp.bfloat16(0.0)

    def ids(count):
        return (
            lax.broadcasted_iota(jnp.int32, (count, columns), 0)
            .astype(jnp.float32)
            .astype(jnp.bfloat16)
        )

    tile_mask = ids(16) == lon_tile
    place_onehot = jnp.where(ids(256) == place, one, zero)
    leaf_area = 0.5 + 5.5 * forcing_ref[3:4, :]
    area_share = 0.05 + 0.55 * forcing_ref[4:5, :]
    canopy_scale = (1.0 - jnp.exp(-0.5 * leaf_area)) / 0.5
    values = [
        (forcing_ref[0:1, :], PARTS),
        (forcing_ref[1:2, :], PARTS),
        (forcing_ref[2:3, :], PARTS),
        (-FLUX_SCALE * area_share * canopy_scale, PARTS),
        (type_ref[...].astype(jnp.float32), 1),
    ]
    rows = []
    for value, count in values:
        for part in bf16_parts(value, count):
            rows.append(jnp.where(tile_mask, jnp.broadcast_to(part, (16, columns)), zero))
    moved = nt_dot(jnp.concatenate(rows, axis=0), place_onehot)
    placed = []
    start = 0
    for value, count in values:
        total = moved[start : start + 16]
        for step in range(1, count):
            total = total + moved[start + 16 * step : start + 16 * (step + 1)]
        placed.append(total)
        start += 16 * count
    low_half = lax.broadcasted_iota(jnp.int32, (16, LANES), 1) < 64
    for tile in range(4):
        span = slice((tile // 2) * LANES, (tile // 2 + 1) * LANES)
        for pair in range(3):
            left = placed[2 * pair][:, span]
            right = placed[min(2 * pair + 1, 4)][:, span]
            if tile % 2 == 0:
                joined = jnp.where(low_half, left, pltpu.roll(right, 64, 1))
            else:
                joined = jnp.where(low_half, pltpu.roll(left, 64, 1), right)
            payload_ref[tile * 16 : (tile + 1) * 16, 0, pair * LANES : (pair + 1) * LANES] = joined

    for copy in copies[3:5]:
        copy.wait()
    blocks = cells_ref.shape[0] // ROWS
    levels = faces_ref.shape[0] // (2 * ROWS)
    for step in range(3):
        low_ref[step * blocks : (step + 1) * blocks, :] = cells_ref[
            pl.ds(step, blocks, stride=ROWS), :
        ]
        high_ref[step * blocks : (step + 1) * blocks, :] = cells_ref[
            pl.ds(ROWS - 3 + step, blocks, stride=ROWS), :
        ]
    high_ref[3 * blocks : 3 * blocks + levels, :] = faces_ref[
        pl.ds(levels * ROWS + ROWS - 1, levels, stride=ROWS), :
    ]
    squares = cells_ref.shape[0] // LANES
    for square in range(squares):
        turned = cells_ref[square * LANES : (square + 1) * LANES, :].T
        westward_ref[3 * square : 3 * square + 3, :] = turned[0:3]
        eastward_ref[3 * square : 3 * square + 3, :] = turned[LANES - 3 : LANES]
    turned = faces_ref[...].T
    westward_ref[3 * squares : 3 * squares + ROWS, :] = turned[LANES - ROWS : LANES]
    eastward_ref[3 * squares : 3 * squares + ROWS, :] = turned[LANES - ROWS : LANES]


def pack(tracer_rows, courant_rows, forcing, plant_type, send_slot, tiles):
    columns = send_slot.shape[0]
    blocks = tracer_rows.shape[0] // ROWS
    levels = courant_rows.shape[0] // (2 * ROWS)
    side_rows = 3 * (tracer_rows.shape[0] // LANES) + ROWS
    vmem = pl.BlockSpec(memory_space=pltpu.VMEM)
    hbm = pl.BlockSpec(memory_space=pltpu.HBM)
    return pl.pallas_call(
        pack_kernel,
        out_shape=(
            jax.ShapeDtypeStruct((tiles, 1, 3 * LANES), jnp.float32),
            jax.ShapeDtypeStruct((3 * blocks, LANES), jnp.float32),
            jax.ShapeDtypeStruct((3 * blocks + levels, LANES), jnp.float32),
            jax.ShapeDtypeStruct((side_rows, LANES), jnp.float32),
            jax.ShapeDtypeStruct((side_rows, LANES), jnp.float32),
        ),
        in_specs=[hbm] * 5,
        out_specs=(vmem,) * 5,
        scratch_shapes=[
            pltpu.VMEM(tracer_rows.shape, jnp.float32),
            pltpu.VMEM(courant_rows.shape, jnp.float32),
            pltpu.VMEM(forcing.shape, jnp.float32),
            pltpu.VMEM((1, columns), jnp.int32),
            pltpu.VMEM((1, columns), jnp.int32),
            pltpu.SemaphoreType.DMA((5,)),
        ],
        compiler_params=pltpu.CompilerParams(vmem_limit_bytes=VMEM_BYTES),
        cost_estimate=pl.CostEstimate(
            flops=300000000, bytes_accessed=2500000, transcendentals=columns
        ),
        name="pack",
    )(*(
        pltpu.with_memory_space_constraint(array, pltpu.HBM)
        for array in (
            tracer_rows, courant_rows, forcing,
            plant_type.reshape(1, columns), send_slot.reshape(1, columns),
        )
    ))


def face_weights(face_courant):
    half = 0.5 * face_courant
    upwind = face_courant > 0
    shrink_left = 1.0 - 2.0 / 3.0 * face_courant
    shrink_right = 1.0 + 2.0 / 3.0 * face_courant
    curve = half * jnp.where(upwind, shrink_left, shrink_right)
    middle = face_courant * jnp.where(upwind, 1.0 - half - 3.0 * curve, 1.0 + half + 3.0 * curve)
    left_edge = face_courant * jnp.where(upwind, half - 3.0 * curve, 0.0)
    right_edge = face_courant * jnp.where(upwind, 0.0, 3.0 * curve - half)
    left_cell = face_courant * jnp.where(upwind, 6.0 * curve, 0.0)
    right_cell = face_courant * jnp.where(upwind, 0.0, -6.0 * curve)
    near, far = 7.0 / 12.0, 1.0 / 12.0
    return [
        -far * left_edge,
        near * left_edge - far * middle,
        near * (middle + left_edge) - far * right_edge + left_cell,
        near * (middle + right_edge) - far * left_edge + right_cell,
        near * right_edge - far * middle,
        -far * right_edge,
    ]


def divergence_weights(face_after, face_before):
    after = face_weights(face_after)
    before = face_weights(face_before)
    taps = []
    for offset in range(7):
        if offset == 0:
            taps.append(-before[0])
        elif offset == 6:
            taps.append(after[5])
        else:
            taps.append(after[offset - 1] - before[offset])
    return taps


TURNED_ROWS = LANES + 16
PADDED_ROWS = 2 * ROWS


def lat_kernel(
    lat_ref, tracer_ref, courant_ref, mixing_ref, south_ref, north_ref,
    sum_ref, response_ref, pivot_ref,
    rows_ref, weight_ref,
):
    levels = mixing_ref.shape[0] + 1
    blocks = tracer_ref.shape[0] // ROWS
    members = blocks // levels
    half = levels * ROWS
    first = lat_ref[0] == 0
    last = lat_ref[0] == lat_ref[1] - 1

    zero = jnp.zeros((blocks, LANES), jnp.float32)
    for step in range(3):
        span = slice(step * blocks, (step + 1) * blocks)
        rows_ref[pl.ds(5 + step, blocks, stride=PADDED_ROWS), :] = jnp.where(
            first, zero, south_ref[span, :]
        )
        rows_ref[pl.ds(PADDED_ROWS + step, blocks, stride=PADDED_ROWS), :] = jnp.where(
            last, zero, north_ref[span, :]
        )
    for block in range(blocks):
        rows_ref[block * PADDED_ROWS + 8 : block * PADDED_ROWS + 16, :] = tracer_ref[
            block * ROWS : (block + 1) * ROWS, :
        ]
    row = lax.broadcasted_iota(jnp.int32, (ROWS, LANES), 0)
    for level in range(levels):
        north_face = courant_ref[half + level * ROWS : half + (level + 1) * ROWS, :]
        below = jnp.where(first, 0.0, south_ref[3 * blocks + level : 3 * blocks + level + 1, :])
        south_face = jnp.where(row == 0, below, pltpu.roll(north_face, 1, 0))
        north_face = jnp.where(jnp.logical_and(last, row == ROWS - 1), 0.0, north_face)
        taps = divergence_weights(north_face, south_face)
        for offset in range(7):
            weight_ref[level, offset] = 1.0 - taps[3] if offset == 3 else -taps[offset]

    ratio = None
    response = []
    for level in range(levels):
        pivot = jnp.ones((ROWS, LANES), jnp.float32)
        if level > 0:
            pivot = pivot + mixing_ref[level - 1]
        if level < levels - 1:
            pivot = pivot + mixing_ref[level]
        if level > 0:
            pivot = pivot - mixing_ref[level - 1] * ratio
        inverse = 1.0 / pivot
        carried = inverse
        if level > 0:
            carried = mixing_ref[level - 1] * inverse
            response.append(carried * response[-1])
        else:
            response.append(inverse)
        pivot_ref[level, 0] = inverse
        pivot_ref[level, 1] = carried
        if level < levels - 1:
            ratio = mixing_ref[level] * inverse
            pivot_ref[level, 2] = ratio
    for level in range(levels - 1, -1, -1):
        if level < levels - 1:
            response[level] = response[level] + pivot_ref[level, 2] * response[level + 1]
        response_ref[level] = response[level]

    together = 4

    def member_step(index, carry):
        for level in range(levels):
            taps = [weight_ref[level, offset] for offset in range(7)]
            for step in range(together):
                block = (index * together + step) * levels + level
                base = pl.multiple_of(block * PADDED_ROWS, PADDED_ROWS) + 5
                total = taps[0] * rows_ref[pl.ds(base, ROWS), :]
                for offset in range(1, 7):
                    total = total + taps[offset] * rows_ref[pl.ds(base + offset, ROWS), :]
                sum_ref[pl.ds(pl.multiple_of(block * ROWS, ROWS), ROWS), :] = total
        return carry

    lax.fori_loop(0, members // together, member_step, 0)


def lon_kernel(
    tracer_ref, courant_ref, west_ref, east_ref, sum_ref, pivot_ref,
    out_ref,
    turned_ref, turned_sum_ref, turned_courant_ref, lon_ref,
):
    members, levels = out_ref.shape[0], out_ref.shape[1]
    squares = tracer_ref.shape[0] // LANES

    for square in range(squares):
        base = square * TURNED_ROWS
        turned_ref[base + 5 : base + 8, :] = west_ref[3 * square : 3 * square + 3, :]
        turned_ref[base + 8 + LANES : base + 11 + LANES, :] = east_ref[
            3 * square : 3 * square + 3, :
        ]
        turned_ref[base + 8 : base + 8 + LANES, :] = tracer_ref[
            square * LANES : (square + 1) * LANES, :
        ].T
    half = levels * ROWS
    turned_faces = courant_ref[...].T
    low_half = lax.broadcasted_iota(jnp.int32, (LANES, LANES), 1) < half
    turned_faces = jnp.where(low_half, turned_faces, pltpu.roll(turned_faces, half, 1))
    turned_courant_ref[8 : 8 + LANES, :] = turned_faces
    side_face = west_ref[3 * squares : 3 * squares + ROWS, :]
    side_face = jnp.where(low_half[0:ROWS], side_face, pltpu.roll(side_face, half, 1))
    turned_courant_ref[0:8, :] = side_face

    def lon_step(tile, carry):
        start = pl.multiple_of(tile * ROWS, ROWS)
        taps = divergence_weights(
            turned_courant_ref[pl.ds(start + 8, ROWS), :],
            turned_courant_ref[pl.ds(start + 7, ROWS), :],
        )
        for square in range(squares):
            base = square * TURNED_ROWS + start + 5
            total = taps[0] * turned_ref[pl.ds(base, ROWS), :]
            for offset in range(1, 7):
                total = total + taps[offset] * turned_ref[pl.ds(base + offset, ROWS), :]
            turned_sum_ref[pl.ds(square * LANES + start, ROWS), :] = total
        return carry

    lax.fori_loop(0, LANES // ROWS, lon_step, 0)
    for square in range(squares):
        span = slice(square * LANES, (square + 1) * LANES)
        lon_ref[span, :] = turned_sum_ref[span, :].T

    together = 4

    def member_step(index, carry):
        swept = [None] * together
        stored = [[None] * levels for _ in range(together)]
        for level in range(levels):
            inverse = pivot_ref[level, 0]
            carried = pivot_ref[level, 1]
            for step in range(together):
                block = (index * together + step) * levels + level
                span = pl.ds(pl.multiple_of(block * ROWS, ROWS), ROWS)
                total = (sum_ref[span, :] - lon_ref[span, :]) * inverse
                if level > 0:
                    total = total + carried * swept[step]
                swept[step] = total
                stored[step][level] = total
        for level in range(levels - 1, -1, -1):
            ratio = pivot_ref[level, 2] if level < levels - 1 else None
            for step in range(together):
                if level < levels - 1:
                    swept[step] = stored[step][level] + ratio * swept[step]
                out_ref[index * together + step, level] = swept[step]
        return carry

    lax.fori_loop(0, members // together, member_step, 0)


def advect_and_mix(lat_place, tracer_rows, courant_rows, mixing, south, north, west, east):
    levels, rows, lanes = mixing.shape[0] + 1, mixing.shape[1], mixing.shape[2]
    blocks = tracer_rows.shape[0] // rows
    members = blocks // levels
    squares = tracer_rows.shape[0] // lanes
    vmem = pl.BlockSpec(memory_space=pltpu.VMEM)
    params = pltpu.CompilerParams(vmem_limit_bytes=VMEM_BYTES)
    cost = pl.CostEstimate(flops=6000000, bytes_accessed=4000000, transcendentals=0)
    lat_sum, response, pivots = pl.pallas_call(
        lat_kernel,
        out_shape=(
            jax.ShapeDtypeStruct(tracer_rows.shape, jnp.float32),
            jax.ShapeDtypeStruct((levels, rows, lanes), jnp.float32),
            jax.ShapeDtypeStruct((levels, 3, rows, lanes), jnp.float32),
        ),
        in_specs=[pl.BlockSpec(memory_space=pltpu.SMEM)] + [vmem] * 5,
        out_specs=(vmem,) * 3,
        scratch_shapes=[
            pltpu.VMEM(((blocks + 1) * PADDED_ROWS, LANES), jnp.float32),
            pltpu.VMEM((levels, 7, ROWS, LANES), jnp.float32),
        ],
        compiler_params=params,
        cost_estimate=cost,
        name="advect_lat",
    )(lat_place, tracer_rows, courant_rows, mixing, south, north)
    partial = pl.pallas_call(
        lon_kernel,
        out_shape=jax.ShapeDtypeStruct((members, levels, rows, lanes), jnp.float32),
        in_specs=[vmem] * 6,
        out_specs=vmem,
        scratch_shapes=[
            pltpu.VMEM((squares * TURNED_ROWS, LANES), jnp.float32),
            pltpu.VMEM((squares * LANES, LANES), jnp.float32),
            pltpu.VMEM((LANES + 8, LANES), jnp.float32),
            pltpu.VMEM((squares * LANES, LANES), jnp.float32),
        ],
        compiler_params=params,
        cost_estimate=cost,
        name="advect_lon_and_mix",
    )(tracer_rows, courant_rows, west, east, lat_sum, pivots)
    return partial, response


def arrhenius(energy, leaf_temp):
    return jnp.exp(energy * (leaf_temp - 25.0) / (298.15 * GAS_CONSTANT * (leaf_temp + 273.15)))


CHUNK = 4


def flux_kernel(
    received_ref, cell_ref, params_ref, bottom_ref, partial_ref, response_ref,
    out_ref, surface_ref,
    column_ref, left_ref, right_ref, result_ref, copy_sems,
):
    members = params_ref.shape[1]
    types = params_ref.shape[2]
    sources, places = cell_ref.shape
    groups = sources // 2
    levels = response_ref.shape[0]
    quarters = ROWS // 2
    one, zero = jnp.bfloat16(1.0), jnp.bfloat16(0.0)

    carbox = 30.0 + 70.0 * params_ref[0]
    tables = jnp.concatenate(
        [carbox, (1.4 + 0.8 * params_ref[1]) * carbox, (0.005 + 0.025 * params_ref[2]) * carbox],
        axis=0,
    )
    table_parts = jnp.concatenate(bf16_parts(tables, 2), axis=1)
    bottom = jnp.concatenate(
        [
            jnp.concatenate(
                [bottom_ref[:, 0, 2 * quarter, :], bottom_ref[:, 0, 2 * quarter + 1, :]], axis=1
            )
            for quarter in range(quarters)
        ],
        axis=0,
    )
    bottom_parts = jnp.concatenate(bf16_parts(bottom, 2), axis=0)

    half = lax.broadcasted_iota(jnp.int32, (groups, LANES), 1) < places

    def pair(values):
        low, high = values[0:groups], values[groups : 2 * groups]
        return (
            jnp.where(half, low, pltpu.roll(high, places, 1)),
            jnp.where(half, pltpu.roll(low, places, 1), high),
        )

    light, leaf_temp = pair(received_ref[:, 0, 0:LANES])
    water, flux_scale = pair(received_ref[:, 0, LANES : 2 * LANES])
    plant, _ = pair(received_ref[:, 0, 2 * LANES : 3 * LANES])
    leaf_temp = 35.0 * leaf_temp
    absorbed = 0.425 * (2000.0 * light)
    michaelis_carbon = 404.9 * arrhenius(79430.0, leaf_temp)
    michaelis_oxygen = 278.4 * arrhenius(36380.0, leaf_temp)
    compensation = 42.75 * arrhenius(37830.0, leaf_temp)
    column_ref[0] = absorbed
    column_ref[1] = arrhenius(65330.0, leaf_temp) * (0.2 + 0.8 * water)
    column_ref[2] = arrhenius(43540.0, leaf_temp)
    column_ref[3] = michaelis_carbon * (1.0 + 210.0 / michaelis_oxygen)
    column_ref[4] = compensation
    column_ref[5] = flux_scale
    column_ref[6] = 2.8 * absorbed
    column_ref[7] = (1.4 * 8.0) * compensation
    column_ref[8] = plant
    cells = jnp.concatenate(
        [cell_ref[pl.ds(tile, sources // 4, stride=4), :] for tile in range(4)], axis=0
    )
    cells = jnp.concatenate([cells[0:groups], cells[groups : 2 * groups]], axis=1)
    column_ref[9] = jnp.right_shift(cells, 8).astype(jnp.float32)
    column_ref[10] = jnp.bitwise_and(cells, 255).astype(jnp.float32)

    def ids(count, mask):
        return (
            jnp.bitwise_and(lax.broadcasted_iota(jnp.int32, (count, LANES), 0), mask)
            .astype(jnp.float32)
            .astype(jnp.bfloat16)
        )

    cell_ids = ids(256, 255)
    type_ids = ids(2 * types, types - 1)

    for chunk in range(groups // CHUNK):
        rows = range(chunk * CHUNK, (chunk + 1) * CHUNK)
        span = slice(chunk * CHUNK * LANES, (chunk + 1) * CHUNK * LANES)

        def spread(quantity, count=members):
            return jnp.concatenate(
                [
                    jnp.broadcast_to(column_ref[quantity, row : row + 1, :], (count, LANES))
                    for row in rows
                ],
                axis=1,
            )

        def onehot(row_ids, quantity):
            return jnp.concatenate(
                [
                    jnp.where(
                        row_ids == column_ref[quantity, row : row + 1, :].astype(jnp.bfloat16),
                        one,
                        zero,
                    )
                    for row in rows
                ],
                axis=1,
            )

        cell_onehot = onehot(cell_ids, 10)
        right_ref[:, span] = cell_onehot
        near = jnp.dot(bottom_parts, cell_onehot, preferred_element_type=jnp.float32)
        near = near[0 : quarters * members] + near[quarters * members : 2 * quarters * members]
        quarter_index = spread(9)
        picked = near[0:members]
        for quarter in range(1, quarters):
            picked = jnp.where(
                quarter_index == quarter, near[quarter * members : (quarter + 1) * members], picked
            )
        params = jnp.dot(
            table_parts, onehot(type_ids, 8), preferred_element_type=jnp.float32
        )
        carbon_leaf = 280.0 + 70.0 * picked
        warm = spread(1)
        carboxylation = params[0:members] * warm
        transport_max = params[members : 2 * members] * spread(2)
        respiration = params[2 * members : 3 * members] * warm
        total_rate = spread(0) + transport_max
        square = total_rate * total_rate - spread(6) * transport_max
        electron_rate = total_rate - square * lax.rsqrt(square)
        excess = carbon_leaf - spread(4)
        rubisco_base = carbon_leaf + spread(3)
        light_base = (1.4 * 4.0) * carbon_leaf + spread(7)
        shared = excess / (rubisco_base * light_base)
        rubisco_rate = carboxylation * light_base * shared
        light_rate = electron_rate * rubisco_base * shared
        flux = spread(5) * (jnp.minimum(rubisco_rate, light_rate) - respiration)
        high, low = bf16_parts(flux, 2)
        quarter_index = quarter_index.astype(jnp.bfloat16)
        for quarter in range(quarters):
            here = quarter_index == jnp.bfloat16(quarter)
            start = quarter * 2 * members
            left_ref[start : start + members, span] = jnp.where(here, high, zero)
            left_ref[start + members : start + 2 * members, span] = jnp.where(here, low, zero)

    summed = nt_dot(left_ref[...], right_ref[...])
    for quarter in range(quarters):
        start = quarter * 2 * members
        total = summed[start : start + members] + summed[start + members : start + 2 * members]
        surface_ref[:, 2 * quarter, :] = total[:, 0:LANES]
        surface_ref[:, 2 * quarter + 1, :] = total[:, LANES : 2 * LANES]

    copies = []
    quarter = members // 4
    for part in range(4):

        def member_step(member, carry):
            surface = surface_ref[member]
            for level in range(levels):
                result_ref[member, level] = (
                    partial_ref[member, level] + response_ref[level] * surface
                )
            return carry

        lax.fori_loop(part * quarter, (part + 1) * quarter, member_step, 0, unroll=4)
        span = pl.ds(part * quarter, quarter)
        copy = pltpu.make_async_copy(result_ref.at[span], out_ref.at[span], copy_sems.at[part])
        copy.start()
        copies.append(copy)
    for copy in copies:
        copy.wait()


def fluxes(received, recv_cell, land_params, tracer, partial, response):
    members, levels, rows, lanes = tracer.shape
    tiles = received.shape[0]
    place_count = recv_cell.shape[0] * recv_cell.shape[1]

    def whole(array):
        return pl.BlockSpec(array.shape, lambda step: (0,) * array.ndim)

    return pl.pallas_call(
        flux_kernel,
        out_shape=(
            jax.ShapeDtypeStruct(tracer.shape, jnp.float32),
            jax.ShapeDtypeStruct((members, rows, lanes), jnp.float32),
        ),
        in_specs=[
            whole(received),
            whole(recv_cell),
            whole(land_params),
            pl.BlockSpec((members, 1, rows, lanes), lambda step: (0, 0, 0, 0)),
            whole(partial),
            whole(response),
        ],
        out_specs=(
            pl.BlockSpec(memory_space=pltpu.HBM),
            pl.BlockSpec((members, rows, lanes), lambda step: (0, 0, 0)),
        ),
        grid=(1,),
        scratch_shapes=[
            pltpu.VMEM((11, tiles // 2, LANES), jnp.float32),
            pltpu.VMEM((ROWS * members, place_count), jnp.bfloat16),
            pltpu.VMEM((256, place_count), jnp.bfloat16),
            pltpu.VMEM(tracer.shape, jnp.float32),
            pltpu.SemaphoreType.DMA((4,)),
        ],
        compiler_params=pltpu.CompilerParams(vmem_limit_bytes=VMEM_BYTES),
        cost_estimate=pl.CostEstimate(flops=600000000, bytes_accessed=3000000, transcendentals=400000),
        name="fluxes",
    )(received, recv_cell, land_params, tracer, partial, response)


def per_device(tracer, courant, mixing, forcing, plant_type, land_params, send_slot, recv_cell):
    members, levels, row_count, column_count = tracer.shape
    lon_count, lat_count = lax.axis_size("lon"), lax.axis_size("lat")
    tracer_rows = tracer.reshape(members * levels * row_count, column_count)
    courant_rows = courant.reshape(2 * levels * row_count, column_count)
    outgoing, low, high, westward, eastward = pack(
        tracer_rows, courant_rows, forcing, plant_type, send_slot, lon_count * lat_count
    )
    north = lax.ppermute(low, "lat", [((i + 1) % lat_count, i) for i in range(lat_count)])
    south = lax.ppermute(high, "lat", [(i, (i + 1) % lat_count) for i in range(lat_count)])
    west = lax.ppermute(eastward, "lon", [(i, (i + 1) % lon_count) for i in range(lon_count)])
    east = lax.ppermute(westward, "lon", [((i + 1) % lon_count, i) for i in range(lon_count)])
    received = lax.all_to_all(outgoing, ("lat", "lon"), split_axis=0, concat_axis=0, tiled=True)
    lat_place = jnp.stack([lax.axis_index("lat"), jnp.int32(lat_count)]).astype(jnp.int32)
    partial, response = advect_and_mix(
        lat_place, tracer_rows, courant_rows, mixing, south, north, west, east
    )
    return fluxes(received, recv_cell, land_params, tracer, partial, response)


def solution(mesh):
    in_specs = (
        P("mem", None, "lat", "lon"),
        P(None, None, "lat", "lon"),
        P(None, "lat", "lon"),
        P(None, ("lon", "lat")),
        P(("lon", "lat")),
        P(None, "mem", None),
        P(("lon", "lat")),
        P(("lon", "lat"), None),
    )
    out_specs = (P("mem", None, "lat", "lon"), P("mem", "lat", "lon"))
    return jax.shard_map(
        per_device, mesh=mesh, in_specs=in_specs, out_specs=out_specs, check_vma=False
    )
```

```python
import functools

import jax
import jax.numpy as jnp
from jax import lax
from jax.experimental import pallas as pl
from jax.experimental.pallas import tpu as pltpu
from jax.sharding import PartitionSpec as P

FLUX_SCALE = 0.02
GAS_CONSTANT = 8.314
LANES = 128
ROWS = 8
VMEM_BYTES = 40 * 2**20
PARTS = 2
OUT_COPIES = 4


def nt_dot(left, right):
    return lax.dot_general(
        left, right, (((1,), (1,)), ((), ())), preferred_element_type=jnp.float32
    )


def bf16_parts(values, count):
    parts = []
    rest = values
    for _ in range(count):
        part = rest.astype(jnp.bfloat16)
        rest = rest - part.astype(jnp.float32)
        parts.append(part)
    return parts


def pack_kernel(
    tracer_hbm, courant_hbm, forcing_hbm, type_hbm, slot_hbm,
    payload_ref, low_ref, high_ref, westward_ref, eastward_ref,
    cells_ref, faces_ref, forcing_ref, type_ref, slot_ref, copy_sems,
):
    moves = (
        (slot_hbm, slot_ref),
        (forcing_hbm, forcing_ref),
        (type_hbm, type_ref),
        (tracer_hbm, cells_ref),
        (courant_hbm, faces_ref),
    )
    copies = [
        pltpu.make_async_copy(source, target, copy_sems.at[place])
        for place, (source, target) in enumerate(moves)
    ]
    for copy in copies:
        copy.start()
    for copy in copies[0:3]:
        copy.wait()

    columns = slot_ref.shape[1]
    slot = slot_ref[...]
    lon_tile = jnp.right_shift(slot, 8).astype(jnp.float32).astype(jnp.bfloat16)
    place = jnp.bitwise_and(slot, 255).astype(jnp.float32).astype(jnp.bfloat16)
    one, zero = jnp.bfloat16(1.0), jnp.bfloat16(0.0)

    def ids(count):
        return (
            lax.broadcasted_iota(jnp.int32, (count, columns), 0)
            .astype(jnp.float32)
            .astype(jnp.bfloat16)
        )

    tile_mask = ids(16) == lon_tile
    place_onehot = jnp.where(ids(256) == place, one, zero)
    leaf_area = 0.5 + 5.5 * forcing_ref[3:4, :]
    area_share = 0.05 + 0.55 * forcing_ref[4:5, :]
    canopy_scale = (1.0 - jnp.exp(-0.5 * leaf_area)) / 0.5
    values = [
        (forcing_ref[0:1, :], PARTS),
        (forcing_ref[1:2, :], PARTS),
        (forcing_ref[2:3, :], PARTS),
        (-FLUX_SCALE * area_share * canopy_scale, PARTS),
        (type_ref[...].astype(jnp.float32), 1),
    ]
    rows = []
    for value, count in values:
        for part in bf16_parts(value, count):
            rows.append(jnp.where(tile_mask, jnp.broadcast_to(part, (16, columns)), zero))
    moved = nt_dot(jnp.concatenate(rows, axis=0), place_onehot)
    placed = []
    start = 0
    for value, count in values:
        total = moved[start : start + 16]
        for step in range(1, count):
            total = total + moved[start + 16 * step : start + 16 * (step + 1)]
        placed.append(total)
        start += 16 * count
    low_half = lax.broadcasted_iota(jnp.int32, (16, LANES), 1) < 64
    for tile in range(4):
        span = slice((tile // 2) * LANES, (tile // 2 + 1) * LANES)
        for pair in range(3):
            left = placed[2 * pair][:, span]
            right = placed[min(2 * pair + 1, 4)][:, span]
            if tile % 2 == 0:
                joined = jnp.where(low_half, left, pltpu.roll(right, 64, 1))
            else:
                joined = jnp.where(low_half, pltpu.roll(left, 64, 1), right)
            payload_ref[tile * 16 : (tile + 1) * 16, 0, pair * LANES : (pair + 1) * LANES] = joined

    for copy in copies[3:5]:
        copy.wait()
    blocks = cells_ref.shape[0] // ROWS
    levels = faces_ref.shape[0] // (2 * ROWS)
    for step in range(3):
        low_ref[step * blocks : (step + 1) * blocks, :] = cells_ref[
            pl.ds(step, blocks, stride=ROWS), :
        ]
        high_ref[step * blocks : (step + 1) * blocks, :] = cells_ref[
            pl.ds(ROWS - 3 + step, blocks, stride=ROWS), :
        ]
    high_ref[3 * blocks : 3 * blocks + levels, :] = faces_ref[
        pl.ds(levels * ROWS + ROWS - 1, levels, stride=ROWS), :
    ]
    squares = cells_ref.shape[0] // LANES
    for square in range(squares):
        turned = cells_ref[square * LANES : (square + 1) * LANES, :].T
        westward_ref[3 * square : 3 * square + 3, :] = turned[0:3]
        eastward_ref[3 * square : 3 * square + 3, :] = turned[LANES - 3 : LANES]
    turned = faces_ref[...].T
    westward_ref[3 * squares : 3 * squares + ROWS, :] = turned[LANES - ROWS : LANES]
    eastward_ref[3 * squares : 3 * squares + ROWS, :] = turned[LANES - ROWS : LANES]


def pack(tracer_rows, courant_rows, forcing, plant_type, send_slot, tiles):
    columns = send_slot.shape[0]
    blocks = tracer_rows.shape[0] // ROWS
    levels = courant_rows.shape[0] // (2 * ROWS)
    side_rows = 3 * (tracer_rows.shape[0] // LANES) + ROWS
    vmem = pl.BlockSpec(memory_space=pltpu.VMEM)
    hbm = pl.BlockSpec(memory_space=pltpu.HBM)
    return pl.pallas_call(
        pack_kernel,
        out_shape=(
            jax.ShapeDtypeStruct((tiles, 1, 3 * LANES), jnp.float32),
            jax.ShapeDtypeStruct((3 * blocks, LANES), jnp.float32),
            jax.ShapeDtypeStruct((3 * blocks + levels, LANES), jnp.float32),
            jax.ShapeDtypeStruct((side_rows, LANES), jnp.float32),
            jax.ShapeDtypeStruct((side_rows, LANES), jnp.float32),
        ),
        in_specs=[hbm] * 5,
        out_specs=(vmem,) * 5,
        scratch_shapes=[
            pltpu.VMEM(tracer_rows.shape, jnp.float32),
            pltpu.VMEM(courant_rows.shape, jnp.float32),
            pltpu.VMEM(forcing.shape, jnp.float32),
            pltpu.VMEM((1, columns), jnp.int32),
            pltpu.VMEM((1, columns), jnp.int32),
            pltpu.SemaphoreType.DMA((5,)),
        ],
        compiler_params=pltpu.CompilerParams(vmem_limit_bytes=VMEM_BYTES),
        cost_estimate=pl.CostEstimate(
            flops=300000000, bytes_accessed=2500000, transcendentals=columns
        ),
        name="pack",
    )(*(
        pltpu.with_memory_space_constraint(array, pltpu.HBM)
        for array in (
            tracer_rows, courant_rows, forcing,
            plant_type.reshape(1, columns), send_slot.reshape(1, columns),
        )
    ))


def face_weights(face_courant):
    half = 0.5 * face_courant
    upwind = face_courant > 0
    shrink_left = 1.0 - 2.0 / 3.0 * face_courant
    shrink_right = 1.0 + 2.0 / 3.0 * face_courant
    curve = half * jnp.where(upwind, shrink_left, shrink_right)
    middle = face_courant * jnp.where(upwind, 1.0 - half - 3.0 * curve, 1.0 + half + 3.0 * curve)
    left_edge = face_courant * jnp.where(upwind, half - 3.0 * curve, 0.0)
    right_edge = face_courant * jnp.where(upwind, 0.0, 3.0 * curve - half)
    left_cell = face_courant * jnp.where(upwind, 6.0 * curve, 0.0)
    right_cell = face_courant * jnp.where(upwind, 0.0, -6.0 * curve)
    near, far = 7.0 / 12.0, 1.0 / 12.0
    return [
        -far * left_edge,
        near * left_edge - far * middle,
        near * (middle + left_edge) - far * right_edge + left_cell,
        near * (middle + right_edge) - far * left_edge + right_cell,
        near * right_edge - far * middle,
        -far * right_edge,
    ]


def divergence_weights(face_after, face_before):
    after = face_weights(face_after)
    before = face_weights(face_before)
    taps = []
    for offset in range(7):
        if offset == 0:
            taps.append(-before[0])
        elif offset == 6:
            taps.append(after[5])
        else:
            taps.append(after[offset - 1] - before[offset])
    return taps


CHUNK = 4
TURNED_ROWS = LANES + 16
PADDED_ROWS = 2 * ROWS


def lat_kernel(
    lat_ref, tracer_ref, courant_ref, mixing_ref, south_ref, north_ref,
    sum_ref, response_ref, pivot_ref,
    rows_ref, weight_ref,
):
    levels = mixing_ref.shape[0] + 1
    blocks = tracer_ref.shape[0] // ROWS
    members = blocks // levels
    half = levels * ROWS
    first = lat_ref[0] == 0
    last = lat_ref[0] == lat_ref[1] - 1

    zero = jnp.zeros((blocks, LANES), jnp.float32)
    for step in range(3):
        span = slice(step * blocks, (step + 1) * blocks)
        rows_ref[pl.ds(5 + step, blocks, stride=PADDED_ROWS), :] = jnp.where(
            first, zero, south_ref[span, :]
        )
        rows_ref[pl.ds(PADDED_ROWS + step, blocks, stride=PADDED_ROWS), :] = jnp.where(
            last, zero, north_ref[span, :]
        )
    for block in range(blocks):
        rows_ref[block * PADDED_ROWS + 8 : block * PADDED_ROWS + 16, :] = tracer_ref[
            block * ROWS : (block + 1) * ROWS, :
        ]
    row = lax.broadcasted_iota(jnp.int32, (ROWS, LANES), 0)
    for level in range(levels):
        north_face = courant_ref[half + level * ROWS : half + (level + 1) * ROWS, :]
        below = jnp.where(first, 0.0, south_ref[3 * blocks + level : 3 * blocks + level + 1, :])
        south_face = jnp.where(row == 0, below, pltpu.roll(north_face, 1, 0))
        north_face = jnp.where(jnp.logical_and(last, row == ROWS - 1), 0.0, north_face)
        taps = divergence_weights(north_face, south_face)
        for offset in range(7):
            weight_ref[level, offset] = 1.0 - taps[3] if offset == 3 else -taps[offset]

    ratio = None
    response = []
    for level in range(levels):
        pivot = jnp.ones((ROWS, LANES), jnp.float32)
        if level > 0:
            pivot = pivot + mixing_ref[level - 1]
        if level < levels - 1:
            pivot = pivot + mixing_ref[level]
        if level > 0:
            pivot = pivot - mixing_ref[level - 1] * ratio
        inverse = 1.0 / pivot
        carried = inverse
        if level > 0:
            carried = mixing_ref[level - 1] * inverse
            response.append(carried * response[-1])
        else:
            response.append(inverse)
        pivot_ref[level, 0] = inverse
        pivot_ref[level, 1] = carried
        if level < levels - 1:
            ratio = mixing_ref[level] * inverse
            pivot_ref[level, 2] = ratio
    for level in range(levels - 1, -1, -1):
        if level < levels - 1:
            response[level] = response[level] + pivot_ref[level, 2] * response[level + 1]
        response_ref[level] = response[level]

    together = 4

    def member_step(index, carry):
        for level in range(levels):
            taps = [weight_ref[level, offset] for offset in range(7)]
            for step in range(together):
                block = (index * together + step) * levels + level
                base = pl.multiple_of(block * PADDED_ROWS, PADDED_ROWS) + 5
                total = taps[0] * rows_ref[pl.ds(base, ROWS), :]
                for offset in range(1, 7):
                    total = total + taps[offset] * rows_ref[pl.ds(base + offset, ROWS), :]
                sum_ref[pl.ds(pl.multiple_of(block * ROWS, ROWS), ROWS), :] = total
        return carry

    lax.fori_loop(0, members // together, member_step, 0)


def lon_kernel(
    tracer_ref, courant_ref, west_ref, east_ref, sum_ref, pivot_ref, cell_ref,
    out_ref, leaf_ref, place_ref,
    turned_ref, turned_sum_ref, turned_courant_ref, lon_ref,
):
    members, levels = out_ref.shape[0], out_ref.shape[1]
    squares = tracer_ref.shape[0] // LANES

    for square in range(squares):
        base = square * TURNED_ROWS
        turned_ref[base + 5 : base + 8, :] = west_ref[3 * square : 3 * square + 3, :]
        turned_ref[base + 8 + LANES : base + 11 + LANES, :] = east_ref[
            3 * square : 3 * square + 3, :
        ]
        turned_ref[base + 8 : base + 8 + LANES, :] = tracer_ref[
            square * LANES : (square + 1) * LANES, :
        ].T
    half = levels * ROWS
    turned_faces = courant_ref[...].T
    low_half = lax.broadcasted_iota(jnp.int32, (LANES, LANES), 1) < half
    turned_faces = jnp.where(low_half, turned_faces, pltpu.roll(turned_faces, half, 1))
    turned_courant_ref[8 : 8 + LANES, :] = turned_faces
    side_face = west_ref[3 * squares : 3 * squares + ROWS, :]
    side_face = jnp.where(low_half[0:ROWS], side_face, pltpu.roll(side_face, half, 1))
    turned_courant_ref[0:8, :] = side_face

    def lon_step(tile, carry):
        start = pl.multiple_of(tile * ROWS, ROWS)
        taps = divergence_weights(
            turned_courant_ref[pl.ds(start + 8, ROWS), :],
            turned_courant_ref[pl.ds(start + 7, ROWS), :],
        )
        for square in range(squares):
            base = square * TURNED_ROWS + start + 5
            total = taps[0] * turned_ref[pl.ds(base, ROWS), :]
            for offset in range(1, 7):
                total = total + taps[offset] * turned_ref[pl.ds(base + offset, ROWS), :]
            turned_sum_ref[pl.ds(square * LANES + start, ROWS), :] = total
        return carry

    lax.fori_loop(0, LANES // ROWS, lon_step, 0)
    for square in range(squares):
        span = slice(square * LANES, (square + 1) * LANES)
        lon_ref[span, :] = turned_sum_ref[span, :].T

    together = 4

    def member_step(index, carry):
        swept = [None] * together
        stored = [[None] * levels for _ in range(together)]
        for level in range(levels):
            inverse = pivot_ref[level, 0]
            carried = pivot_ref[level, 1]
            for step in range(together):
                block = (index * together + step) * levels + level
                span = pl.ds(pl.multiple_of(block * ROWS, ROWS), ROWS)
                total = (sum_ref[span, :] - lon_ref[span, :]) * inverse
                if level > 0:
                    total = total + carried * swept[step]
                swept[step] = total
                stored[step][level] = total
        for level in range(levels - 1, -1, -1):
            ratio = pivot_ref[level, 2] if level < levels - 1 else None
            for step in range(together):
                if level < levels - 1:
                    swept[step] = stored[step][level] + ratio * swept[step]
                out_ref[index * together + step, level] = swept[step]
        return carry

    lax.fori_loop(0, members // together, member_step, 0)
    near_cells(tracer_ref, cell_ref, leaf_ref, place_ref, members, levels)


def near_cells(tracer_ref, cell_ref, leaf_ref, place_ref, members, levels):
    sources = cell_ref.shape[0]
    groups = sources // 2
    quarters = ROWS // 2
    stride = levels * ROWS
    bottom = jnp.concatenate(
        [
            jnp.concatenate(
                [
                    tracer_ref[pl.ds(2 * quarter + side, members, stride=stride), :]
                    for side in range(2)
                ],
                axis=1,
            )
            for quarter in range(quarters)
        ],
        axis=0,
    )
    bottom_parts = jnp.concatenate(bf16_parts(bottom, 2), axis=0)
    cells = jnp.concatenate(
        [cell_ref[pl.ds(tile, sources // 4, stride=4), :] for tile in range(4)], axis=0
    )
    cells = jnp.concatenate([cells[0:groups], cells[groups : 2 * groups]], axis=1)
    place_ref[0] = jnp.right_shift(cells, 8).astype(jnp.float32)
    lane = jnp.bitwise_and(cells, 255).astype(jnp.float32)
    place_ref[1] = lane
    cell_ids = (
        lax.broadcasted_iota(jnp.int32, (256, LANES), 0).astype(jnp.float32).astype(jnp.bfloat16)
    )
    one, zero = jnp.bfloat16(1.0), jnp.bfloat16(0.0)
    for chunk in range(groups // CHUNK):
        rows = range(chunk * CHUNK, (chunk + 1) * CHUNK)
        span = slice(chunk * CHUNK * LANES, (chunk + 1) * CHUNK * LANES)
        cell_onehot = jnp.concatenate(
            [
                jnp.where(cell_ids == lane[row : row + 1, :].astype(jnp.bfloat16), one, zero)
                for row in rows
            ],
            axis=1,
        )
        near = jnp.dot(bottom_parts, cell_onehot, preferred_element_type=jnp.float32)
        near = near[0 : quarters * members] + near[quarters * members : 2 * quarters * members]
        quarter_index = jnp.concatenate(
            [
                jnp.broadcast_to(place_ref[0, row : row + 1, :], (members, LANES))
                for row in rows
            ],
            axis=1,
        )
        picked = near[0:members]
        for quarter in range(1, quarters):
            picked = jnp.where(
                quarter_index == quarter, near[quarter * members : (quarter + 1) * members], picked
            )
        leaf_ref[:, span] = 280.0 + 70.0 * picked


def advect_and_mix(
    lat_place, tracer_rows, courant_rows, mixing, south, north, west, east, recv_cell
):
    levels, rows, lanes = mixing.shape[0] + 1, mixing.shape[1], mixing.shape[2]
    blocks = tracer_rows.shape[0] // rows
    members = blocks // levels
    squares = tracer_rows.shape[0] // lanes
    vmem = pl.BlockSpec(memory_space=pltpu.VMEM)
    params = pltpu.CompilerParams(vmem_limit_bytes=VMEM_BYTES)
    cost = pl.CostEstimate(flops=6000000, bytes_accessed=4000000, transcendentals=0)
    lat_sum, response, pivots = pl.pallas_call(
        lat_kernel,
        out_shape=(
            jax.ShapeDtypeStruct(tracer_rows.shape, jnp.float32),
            jax.ShapeDtypeStruct((levels, rows, lanes), jnp.float32),
            jax.ShapeDtypeStruct((levels, 3, rows, lanes), jnp.float32),
        ),
        in_specs=[pl.BlockSpec(memory_space=pltpu.SMEM)] + [vmem] * 5,
        out_specs=(vmem,) * 3,
        scratch_shapes=[
            pltpu.VMEM(((blocks + 1) * PADDED_ROWS, LANES), jnp.float32),
            pltpu.VMEM((levels, 7, ROWS, LANES), jnp.float32),
        ],
        compiler_params=params,
        cost_estimate=cost,
        name="advect_lat",
    )(lat_place, tracer_rows, courant_rows, mixing, south, north)
    sources, places = recv_cell.shape
    place_count = sources * places
    partial, leaf, place = pl.pallas_call(
        lon_kernel,
        out_shape=(
            jax.ShapeDtypeStruct((members, levels, rows, lanes), jnp.float32),
            jax.ShapeDtypeStruct((members, place_count), jnp.float32),
            jax.ShapeDtypeStruct((2, place_count // LANES, LANES), jnp.float32),
        ),
        in_specs=[vmem] * 7,
        out_specs=(vmem,) * 3,
        scratch_shapes=[
            pltpu.VMEM((squares * TURNED_ROWS, LANES), jnp.float32),
            pltpu.VMEM((squares * LANES, LANES), jnp.float32),
            pltpu.VMEM((LANES + 8, LANES), jnp.float32),
            pltpu.VMEM((squares * LANES, LANES), jnp.float32),
        ],
        compiler_params=params,
        cost_estimate=cost,
        name="advect_lon_and_mix",
    )(tracer_rows, courant_rows, west, east, lat_sum, pivots, recv_cell)
    return partial, response, leaf, place


def arrhenius(energy, leaf_temp):
    return jnp.exp(energy * (leaf_temp - 25.0) / (298.15 * GAS_CONSTANT * (leaf_temp + 273.15)))


def flux_kernel(
    received_ref, params_ref, leaf_ref, place_ref, partial_ref, response_ref,
    out_ref, surface_ref,
    column_ref, result_ref, copy_sems,
):
    members = params_ref.shape[1]
    types = params_ref.shape[2]
    sources = received_ref.shape[0]
    groups = sources // 2
    places = LANES // 2
    levels = response_ref.shape[0]
    quarters = ROWS // 2
    one, zero = jnp.bfloat16(1.0), jnp.bfloat16(0.0)

    carbox = 30.0 + 70.0 * params_ref[0]
    tables = jnp.concatenate(
        [carbox, (1.4 + 0.8 * params_ref[1]) * carbox, (0.005 + 0.025 * params_ref[2]) * carbox],
        axis=0,
    )
    table_parts = jnp.concatenate(bf16_parts(tables, 2), axis=1)

    half = lax.broadcasted_iota(jnp.int32, (groups, LANES), 1) < places

    def pair(values):
        low, high = values[0:groups], values[groups : 2 * groups]
        return (
            jnp.where(half, low, pltpu.roll(high, places, 1)),
            jnp.where(half, pltpu.roll(low, places, 1), high),
        )

    light, leaf_temp = pair(received_ref[:, 0, 0:LANES])
    water, flux_scale = pair(received_ref[:, 0, LANES : 2 * LANES])
    plant, _ = pair(received_ref[:, 0, 2 * LANES : 3 * LANES])
    leaf_temp = 35.0 * leaf_temp
    absorbed = 0.425 * (2000.0 * light)
    michaelis_carbon = 404.9 * arrhenius(79430.0, leaf_temp)
    michaelis_oxygen = 278.4 * arrhenius(36380.0, leaf_temp)
    compensation = 42.75 * arrhenius(37830.0, leaf_temp)
    column_ref[0] = absorbed
    column_ref[1] = arrhenius(65330.0, leaf_temp) * (0.2 + 0.8 * water)
    column_ref[2] = arrhenius(43540.0, leaf_temp)
    column_ref[3] = michaelis_carbon * (1.0 + 210.0 / michaelis_oxygen)
    column_ref[4] = compensation
    column_ref[5] = flux_scale
    column_ref[6] = 2.8 * absorbed
    column_ref[7] = (1.4 * 8.0) * compensation
    column_ref[8] = plant

    type_ids = (
        jnp.bitwise_and(lax.broadcasted_iota(jnp.int32, (2 * types, LANES), 0), types - 1)
        .astype(jnp.float32)
        .astype(jnp.bfloat16)
    )

    cell_ids = (
        lax.broadcasted_iota(jnp.int32, (256, LANES), 0).astype(jnp.float32).astype(jnp.bfloat16)
    )
    lefts, onehots = [], []
    for chunk in range(groups // CHUNK):
        rows = range(chunk * CHUNK, (chunk + 1) * CHUNK)
        span = slice(chunk * CHUNK * LANES, (chunk + 1) * CHUNK * LANES)

        def spread(ref):
            return jnp.concatenate(
                [jnp.broadcast_to(ref[row : row + 1, :], (members, LANES)) for row in rows],
                axis=1,
            )

        type_onehot = jnp.concatenate(
            [
                jnp.where(
                    type_ids == column_ref[8, row : row + 1, :].astype(jnp.bfloat16), one, zero
                )
                for row in rows
            ],
            axis=1,
        )
        params = jnp.dot(table_parts, type_onehot, preferred_element_type=jnp.float32)
        carbon_leaf = leaf_ref[:, span]
        warm = spread(column_ref.at[1])
        carboxylation = params[0:members] * warm
        transport_max = params[members : 2 * members] * spread(column_ref.at[2])
        respiration = params[2 * members : 3 * members] * warm
        total_rate = spread(column_ref.at[0]) + transport_max
        square = total_rate * total_rate - spread(column_ref.at[6]) * transport_max
        electron_rate = total_rate - square * lax.rsqrt(square)
        excess = carbon_leaf - spread(column_ref.at[4])
        rubisco_base = carbon_leaf + spread(column_ref.at[3])
        light_base = (1.4 * 4.0) * carbon_leaf + spread(column_ref.at[7])
        shared = excess / (rubisco_base * light_base)
        rubisco_rate = carboxylation * light_base * shared
        light_rate = electron_rate * rubisco_base * shared
        flux = spread(column_ref.at[5]) * (jnp.minimum(rubisco_rate, light_rate) - respiration)
        high, low = bf16_parts(flux, 2)
        quarter_index = spread(place_ref.at[0]).astype(jnp.bfloat16)
        left = []
        for quarter in range(quarters):
            here = quarter_index == jnp.bfloat16(quarter)
            left.append(jnp.where(here, high, zero))
            left.append(jnp.where(here, low, zero))
        cell_onehot = jnp.concatenate(
            [
                jnp.where(
                    cell_ids == place_ref[1, row : row + 1, :].astype(jnp.bfloat16), one, zero
                )
                for row in rows
            ],
            axis=1,
        )
        lefts.append(jnp.concatenate(left, axis=0))
        onehots.append(cell_onehot)

    summed = nt_dot(jnp.concatenate(lefts, axis=1), jnp.concatenate(onehots, axis=1))
    for quarter in range(quarters):
        start = quarter * 2 * members
        total = summed[start : start + members] + summed[start + members : start + 2 * members]
        surface_ref[:, 2 * quarter, :] = total[:, 0:LANES]
        surface_ref[:, 2 * quarter + 1, :] = total[:, LANES : 2 * LANES]

    copies = []
    share = members // OUT_COPIES
    for part in range(OUT_COPIES):
        responses = [response_ref[level] for level in range(levels)]
        for member in range(part * share, (part + 1) * share):
            surface = surface_ref[member]
            for level in range(levels):
                result_ref[member, level] = partial_ref[member, level] + responses[level] * surface
        span = pl.ds(part * share, share)
        copy = pltpu.make_async_copy(result_ref.at[span], out_ref.at[span], copy_sems.at[part])
        copy.start()
        copies.append(copy)
    for copy in copies:
        copy.wait()


def fluxes(received, land_params, leaf, place, partial, response):
    members, levels, rows, lanes = partial.shape
    vmem = pl.BlockSpec(memory_space=pltpu.VMEM)
    return pl.pallas_call(
        flux_kernel,
        out_shape=(
            jax.ShapeDtypeStruct(partial.shape, jnp.float32),
            jax.ShapeDtypeStruct((members, rows, lanes), jnp.float32),
        ),
        in_specs=[vmem] * 6,
        out_specs=(pl.BlockSpec(memory_space=pltpu.HBM), vmem),
        scratch_shapes=[
            pltpu.VMEM((9, received.shape[0] // 2, LANES), jnp.float32),
            pltpu.VMEM(partial.shape, jnp.float32),
            pltpu.SemaphoreType.DMA((OUT_COPIES,)),
        ],
        compiler_params=pltpu.CompilerParams(vmem_limit_bytes=VMEM_BYTES),
        cost_estimate=pl.CostEstimate(flops=600000000, bytes_accessed=3000000, transcendentals=400000),
        name="fluxes",
    )(received, land_params, leaf, place, partial, response)


def per_device(tracer, courant, mixing, forcing, plant_type, land_params, send_slot, recv_cell):
    members, levels, row_count, column_count = tracer.shape
    lon_count, lat_count = lax.axis_size("lon"), lax.axis_size("lat")
    tracer_rows = tracer.reshape(members * levels * row_count, column_count)
    courant_rows = courant.reshape(2 * levels * row_count, column_count)
    outgoing, low, high, westward, eastward = pack(
        tracer_rows, courant_rows, forcing, plant_type, send_slot, lon_count * lat_count
    )
    north = lax.ppermute(low, "lat", [((i + 1) % lat_count, i) for i in range(lat_count)])
    south = lax.ppermute(high, "lat", [(i, (i + 1) % lat_count) for i in range(lat_count)])
    west = lax.ppermute(eastward, "lon", [(i, (i + 1) % lon_count) for i in range(lon_count)])
    east = lax.ppermute(westward, "lon", [((i + 1) % lon_count, i) for i in range(lon_count)])
    received = lax.all_to_all(outgoing, ("lat", "lon"), split_axis=0, concat_axis=0, tiled=True)
    lat_place = jnp.stack([lax.axis_index("lat"), jnp.int32(lat_count)]).astype(jnp.int32)
    partial, response, leaf, place = advect_and_mix(
        lat_place, tracer_rows, courant_rows, mixing, south, north, west, east, recv_cell
    )
    return fluxes(received, land_params, leaf, place, partial, response)


def solution(mesh):
    in_specs = (
        P("mem", None, "lat", "lon"),
        P(None, None, "lat", "lon"),
        P(None, "lat", "lon"),
        P(None, ("lon", "lat")),
        P(("lon", "lat")),
        P(None, "mem", None),
        P(("lon", "lat")),
        P(("lon", "lat"), None),
    )
    out_specs = (P("mem", None, "lat", "lon"), P("mem", "lat", "lon"))
    return jax.shard_map(
        per_device, mesh=mesh, in_specs=in_specs, out_specs=out_specs, check_vma=False
    )
```

```python
import functools

import jax
import jax.numpy as jnp
from jax import lax
from jax.experimental import pallas as pl
from jax.experimental.pallas import tpu as pltpu
from jax.sharding import PartitionSpec as P

FLUX_SCALE = 0.02
GAS_CONSTANT = 8.314
LANES = 128
ROWS = 8
VMEM_BYTES = 40 * 2**20
PARTS = 2
OUT_COPIES = 4


def nt_dot(left, right):
    return lax.dot_general(
        left, right, (((1,), (1,)), ((), ())), preferred_element_type=jnp.float32
    )


def bf16_parts(values, count):
    parts = []
    rest = values
    for _ in range(count):
        part = rest.astype(jnp.bfloat16)
        rest = rest - part.astype(jnp.float32)
        parts.append(part)
    return parts


def pack_kernel(
    tracer_hbm, courant_hbm, forcing_hbm, type_hbm, slot_hbm,
    payload_ref, first_ref, second_ref, westward_ref, eastward_ref,
    cells_ref, faces_ref, forcing_ref, type_ref, slot_ref, copy_sems,
):
    moves = (
        (slot_hbm, slot_ref),
        (forcing_hbm, forcing_ref),
        (type_hbm, type_ref),
        (tracer_hbm, cells_ref),
        (courant_hbm, faces_ref),
    )
    copies = [
        pltpu.make_async_copy(source, target, copy_sems.at[place])
        for place, (source, target) in enumerate(moves)
    ]
    for copy in copies:
        copy.start()
    for copy in copies[0:3]:
        copy.wait()

    columns = slot_ref.shape[1]
    slot = slot_ref[...]
    lon_tile = jnp.right_shift(slot, 8).astype(jnp.float32).astype(jnp.bfloat16)
    place = jnp.bitwise_and(slot, 255).astype(jnp.float32).astype(jnp.bfloat16)
    one, zero = jnp.bfloat16(1.0), jnp.bfloat16(0.0)

    def ids(count):
        return (
            lax.broadcasted_iota(jnp.int32, (count, columns), 0)
            .astype(jnp.float32)
            .astype(jnp.bfloat16)
        )

    tile_mask = ids(16) == lon_tile
    place_onehot = jnp.where(ids(256) == place, one, zero)
    leaf_area = 0.5 + 5.5 * forcing_ref[3:4, :]
    area_share = 0.05 + 0.55 * forcing_ref[4:5, :]
    canopy_scale = (1.0 - jnp.exp(-0.5 * leaf_area)) / 0.5
    values = [
        (forcing_ref[0:1, :], PARTS),
        (forcing_ref[1:2, :], PARTS),
        (forcing_ref[2:3, :], PARTS),
        (-FLUX_SCALE * area_share * canopy_scale, PARTS),
        (type_ref[...].astype(jnp.float32), 1),
    ]
    rows = []
    for value, count in values:
        for part in bf16_parts(value, count):
            rows.append(jnp.where(tile_mask, jnp.broadcast_to(part, (16, columns)), zero))
    moved = nt_dot(jnp.concatenate(rows, axis=0), place_onehot)
    placed = []
    start = 0
    for value, count in values:
        total = moved[start : start + 16]
        for step in range(1, count):
            total = total + moved[start + 16 * step : start + 16 * (step + 1)]
        placed.append(total)
        start += 16 * count
    low_half = lax.broadcasted_iota(jnp.int32, (16, LANES), 1) < 64
    for tile in range(4):
        span = slice((tile // 2) * LANES, (tile // 2 + 1) * LANES)
        for pair in range(3):
            left = placed[2 * pair][:, span]
            right = placed[min(2 * pair + 1, 4)][:, span]
            if tile % 2 == 0:
                joined = jnp.where(low_half, left, pltpu.roll(right, 64, 1))
            else:
                joined = jnp.where(low_half, pltpu.roll(left, 64, 1), right)
            payload_ref[tile * 16 : (tile + 1) * 16, 0, pair * LANES : (pair + 1) * LANES] = joined

    for copy in copies[3:5]:
        copy.wait()
    blocks = cells_ref.shape[0] // ROWS
    levels = faces_ref.shape[0] // (2 * ROWS)
    even = lax.rem(lax.axis_index("lat"), 2) == 0
    for step in range(3):
        low = cells_ref[pl.ds(step, blocks, stride=ROWS), :]
        high = cells_ref[pl.ds(ROWS - 3 + step, blocks, stride=ROWS), :]
        span = slice(step * blocks, (step + 1) * blocks)
        first_ref[span, :] = jnp.where(even, high, low)
        second_ref[span, :] = jnp.where(even, low, high)
    last_faces = faces_ref[pl.ds(levels * ROWS + ROWS - 1, levels, stride=ROWS), :]
    first_ref[3 * blocks : 3 * blocks + levels, :] = last_faces
    second_ref[3 * blocks : 3 * blocks + levels, :] = last_faces
    squares = cells_ref.shape[0] // LANES
    for square in range(squares):
        turned = cells_ref[square * LANES : (square + 1) * LANES, :].T
        westward_ref[3 * square : 3 * square + 3, :] = turned[0:3]
        eastward_ref[3 * square : 3 * square + 3, :] = turned[LANES - 3 : LANES]
    turned = faces_ref[...].T
    westward_ref[3 * squares : 3 * squares + ROWS, :] = turned[LANES - ROWS : LANES]
    eastward_ref[3 * squares : 3 * squares + ROWS, :] = turned[LANES - ROWS : LANES]


def pack(tracer_rows, courant_rows, forcing, plant_type, send_slot, tiles):
    columns = send_slot.shape[0]
    blocks = tracer_rows.shape[0] // ROWS
    levels = courant_rows.shape[0] // (2 * ROWS)
    side_rows = 3 * (tracer_rows.shape[0] // LANES) + ROWS
    vmem = pl.BlockSpec(memory_space=pltpu.VMEM)
    hbm = pl.BlockSpec(memory_space=pltpu.HBM)
    return pl.pallas_call(
        pack_kernel,
        out_shape=(
            jax.ShapeDtypeStruct((tiles, 1, 3 * LANES), jnp.float32),
            jax.ShapeDtypeStruct((3 * blocks + levels, LANES), jnp.float32),
            jax.ShapeDtypeStruct((3 * blocks + levels, LANES), jnp.float32),
            jax.ShapeDtypeStruct((side_rows, LANES), jnp.float32),
            jax.ShapeDtypeStruct((side_rows, LANES), jnp.float32),
        ),
        in_specs=[hbm] * 5,
        out_specs=(vmem,) * 5,
        scratch_shapes=[
            pltpu.VMEM(tracer_rows.shape, jnp.float32),
            pltpu.VMEM(courant_rows.shape, jnp.float32),
            pltpu.VMEM(forcing.shape, jnp.float32),
            pltpu.VMEM((1, columns), jnp.int32),
            pltpu.VMEM((1, columns), jnp.int32),
            pltpu.SemaphoreType.DMA((5,)),
        ],
        compiler_params=pltpu.CompilerParams(vmem_limit_bytes=VMEM_BYTES),
        cost_estimate=pl.CostEstimate(
            flops=300000000, bytes_accessed=2500000, transcendentals=columns
        ),
        name="pack",
    )(*(
        pltpu.with_memory_space_constraint(array, pltpu.HBM)
        for array in (
            tracer_rows, courant_rows, forcing,
            plant_type.reshape(1, columns), send_slot.reshape(1, columns),
        )
    ))


def face_weights(face_courant):
    half = 0.5 * face_courant
    upwind = face_courant > 0
    shrink_left = 1.0 - 2.0 / 3.0 * face_courant
    shrink_right = 1.0 + 2.0 / 3.0 * face_courant
    curve = half * jnp.where(upwind, shrink_left, shrink_right)
    middle = face_courant * jnp.where(upwind, 1.0 - half - 3.0 * curve, 1.0 + half + 3.0 * curve)
    left_edge = face_courant * jnp.where(upwind, half - 3.0 * curve, 0.0)
    right_edge = face_courant * jnp.where(upwind, 0.0, 3.0 * curve - half)
    left_cell = face_courant * jnp.where(upwind, 6.0 * curve, 0.0)
    right_cell = face_courant * jnp.where(upwind, 0.0, -6.0 * curve)
    near, far = 7.0 / 12.0, 1.0 / 12.0
    return [
        -far * left_edge,
        near * left_edge - far * middle,
        near * (middle + left_edge) - far * right_edge + left_cell,
        near * (middle + right_edge) - far * left_edge + right_cell,
        near * right_edge - far * middle,
        -far * right_edge,
    ]


def divergence_weights(face_after, face_before):
    after = face_weights(face_after)
    before = face_weights(face_before)
    taps = []
    for offset in range(7):
        if offset == 0:
            taps.append(-before[0])
        elif offset == 6:
            taps.append(after[5])
        else:
            taps.append(after[offset - 1] - before[offset])
    return taps


CHUNK = 4
TURNED_ROWS = LANES + 16
PADDED_ROWS = 2 * ROWS


def lat_kernel(
    lat_ref, tracer_ref, courant_ref, mixing_ref, swap_ref, next_swap_ref,
    sum_ref, response_ref, pivot_ref,
    rows_ref, weight_ref,
):
    levels = mixing_ref.shape[0] + 1
    blocks = tracer_ref.shape[0] // ROWS
    members = blocks // levels
    half = levels * ROWS
    first = lat_ref[0] == 0
    even = lax.rem(lat_ref[0], 2) == 0
    last = lat_ref[0] == lat_ref[1] - 1

    zero = jnp.zeros((blocks, LANES), jnp.float32)
    for step in range(3):
        span = slice(step * blocks, (step + 1) * blocks)
        rows_ref[pl.ds(5 + step, blocks, stride=PADDED_ROWS), :] = jnp.where(
            first, zero, jnp.where(even, next_swap_ref[span, :], swap_ref[span, :])
        )
        rows_ref[pl.ds(PADDED_ROWS + step, blocks, stride=PADDED_ROWS), :] = jnp.where(
            last, zero, jnp.where(even, swap_ref[span, :], next_swap_ref[span, :])
        )
    for block in range(blocks):
        rows_ref[block * PADDED_ROWS + 8 : block * PADDED_ROWS + 16, :] = tracer_ref[
            block * ROWS : (block + 1) * ROWS, :
        ]
    row = lax.broadcasted_iota(jnp.int32, (ROWS, LANES), 0)
    for level in range(levels):
        north_face = courant_ref[half + level * ROWS : half + (level + 1) * ROWS, :]
        place = slice(3 * blocks + level, 3 * blocks + level + 1)
        below = jnp.where(even, next_swap_ref[place, :], swap_ref[place, :])
        below = jnp.where(first, 0.0, below)
        south_face = jnp.where(row == 0, below, pltpu.roll(north_face, 1, 0))
        north_face = jnp.where(jnp.logical_and(last, row == ROWS - 1), 0.0, north_face)
        taps = divergence_weights(north_face, south_face)
        for offset in range(7):
            weight_ref[level, offset] = 1.0 - taps[3] if offset == 3 else -taps[offset]

    ratio = None
    response = []
    for level in range(levels):
        pivot = jnp.ones((ROWS, LANES), jnp.float32)
        if level > 0:
            pivot = pivot + mixing_ref[level - 1]
        if level < levels - 1:
            pivot = pivot + mixing_ref[level]
        if level > 0:
            pivot = pivot - mixing_ref[level - 1] * ratio
        inverse = 1.0 / pivot
        carried = inverse
        if level > 0:
            carried = mixing_ref[level - 1] * inverse
            response.append(carried * response[-1])
        else:
            response.append(inverse)
        pivot_ref[level, 0] = inverse
        pivot_ref[level, 1] = carried
        if level < levels - 1:
            ratio = mixing_ref[level] * inverse
            pivot_ref[level, 2] = ratio
    for level in range(levels - 1, -1, -1):
        if level < levels - 1:
            response[level] = response[level] + pivot_ref[level, 2] * response[level + 1]
        response_ref[level] = response[level]

    together = 4

    def member_step(index, carry):
        for level in range(levels):
            taps = [weight_ref[level, offset] for offset in range(7)]
            for step in range(together):
                block = (index * together + step) * levels + level
                base = pl.multiple_of(block * PADDED_ROWS, PADDED_ROWS) + 5
                total = taps[0] * rows_ref[pl.ds(base, ROWS), :]
                for offset in range(1, 7):
                    total = total + taps[offset] * rows_ref[pl.ds(base + offset, ROWS), :]
                sum_ref[pl.ds(pl.multiple_of(block * ROWS, ROWS), ROWS), :] = total
        return carry

    lax.fori_loop(0, members // together, member_step, 0)


def lon_kernel(
    tracer_ref, courant_ref, west_ref, east_ref, sum_ref, pivot_ref, cell_ref,
    out_ref, leaf_ref, place_ref,
    turned_ref, turned_sum_ref, turned_courant_ref, lon_ref,
):
    members, levels = out_ref.shape[0], out_ref.shape[1]
    squares = tracer_ref.shape[0] // LANES

    for square in range(squares):
        base = square * TURNED_ROWS
        turned_ref[base + 5 : base + 8, :] = west_ref[3 * square : 3 * square + 3, :]
        turned_ref[base + 8 + LANES : base + 11 + LANES, :] = east_ref[
            3 * square : 3 * square + 3, :
        ]
        turned_ref[base + 8 : base + 8 + LANES, :] = tracer_ref[
            square * LANES : (square + 1) * LANES, :
        ].T
    half = levels * ROWS
    turned_faces = courant_ref[...].T
    low_half = lax.broadcasted_iota(jnp.int32, (LANES, LANES), 1) < half
    turned_faces = jnp.where(low_half, turned_faces, pltpu.roll(turned_faces, half, 1))
    turned_courant_ref[8 : 8 + LANES, :] = turned_faces
    side_face = west_ref[3 * squares : 3 * squares + ROWS, :]
    side_face = jnp.where(low_half[0:ROWS], side_face, pltpu.roll(side_face, half, 1))
    turned_courant_ref[0:8, :] = side_face

    def lon_step(tile, carry):
        start = pl.multiple_of(tile * ROWS, ROWS)
        taps = divergence_weights(
            turned_courant_ref[pl.ds(start + 8, ROWS), :],
            turned_courant_ref[pl.ds(start + 7, ROWS), :],
        )
        for square in range(squares):
            base = square * TURNED_ROWS + start + 5
            total = taps[0] * turned_ref[pl.ds(base, ROWS), :]
            for offset in range(1, 7):
                total = total + taps[offset] * turned_ref[pl.ds(base + offset, ROWS), :]
            turned_sum_ref[pl.ds(square * LANES + start, ROWS), :] = total
        return carry

    lax.fori_loop(0, LANES // ROWS, lon_step, 0)
    for square in range(squares):
        span = slice(square * LANES, (square + 1) * LANES)
        lon_ref[span, :] = turned_sum_ref[span, :].T

    together = 4

    def member_step(index, carry):
        swept = [None] * together
        stored = [[None] * levels for _ in range(together)]
        for level in range(levels):
            inverse = pivot_ref[level, 0]
            carried = pivot_ref[level, 1]
            for step in range(together):
                block = (index * together + step) * levels + level
                span = pl.ds(pl.multiple_of(block * ROWS, ROWS), ROWS)
                total = (sum_ref[span, :] - lon_ref[span, :]) * inverse
                if level > 0:
                    total = total + carried * swept[step]
                swept[step] = total
                stored[step][level] = total
        for level in range(levels - 1, -1, -1):
            ratio = pivot_ref[level, 2] if level < levels - 1 else None
            for step in range(together):
                if level < levels - 1:
                    swept[step] = stored[step][level] + ratio * swept[step]
                out_ref[index * together + step, level] = swept[step]
        return carry

    lax.fori_loop(0, members // together, member_step, 0)
    near_cells(tracer_ref, cell_ref, leaf_ref, place_ref, members, levels)


def near_cells(tracer_ref, cell_ref, leaf_ref, place_ref, members, levels):
    sources = cell_ref.shape[0]
    groups = sources // 2
    quarters = ROWS // 2
    stride = levels * ROWS
    bottom = jnp.concatenate(
        [
            jnp.concatenate(
                [
                    tracer_ref[pl.ds(2 * quarter + side, members, stride=stride), :]
                    for side in range(2)
                ],
                axis=1,
            )
            for quarter in range(quarters)
        ],
        axis=0,
    )
    bottom_parts = jnp.concatenate(bf16_parts(bottom, 2), axis=0)
    cells = jnp.concatenate(
        [cell_ref[pl.ds(tile, sources // 4, stride=4), :] for tile in range(4)], axis=0
    )
    cells = jnp.concatenate([cells[0:groups], cells[groups : 2 * groups]], axis=1)
    place_ref[0] = jnp.right_shift(cells, 8).astype(jnp.float32)
    lane = jnp.bitwise_and(cells, 255).astype(jnp.float32)
    place_ref[1] = lane
    cell_ids = (
        lax.broadcasted_iota(jnp.int32, (256, LANES), 0).astype(jnp.float32).astype(jnp.bfloat16)
    )
    one, zero = jnp.bfloat16(1.0), jnp.bfloat16(0.0)
    for chunk in range(groups // CHUNK):
        rows = range(chunk * CHUNK, (chunk + 1) * CHUNK)
        span = slice(chunk * CHUNK * LANES, (chunk + 1) * CHUNK * LANES)
        cell_onehot = jnp.concatenate(
            [
                jnp.where(cell_ids == lane[row : row + 1, :].astype(jnp.bfloat16), one, zero)
                for row in rows
            ],
            axis=1,
        )
        near = jnp.dot(bottom_parts, cell_onehot, preferred_element_type=jnp.float32)
        near = near[0 : quarters * members] + near[quarters * members : 2 * quarters * members]
        quarter_index = jnp.concatenate(
            [
                jnp.broadcast_to(place_ref[0, row : row + 1, :], (members, LANES))
                for row in rows
            ],
            axis=1,
        )
        picked = near[0:members]
        for quarter in range(1, quarters):
            picked = jnp.where(
                quarter_index == quarter, near[quarter * members : (quarter + 1) * members], picked
            )
        leaf_ref[:, span] = 280.0 + 70.0 * picked


def advect_and_mix(
    lat_place, tracer_rows, courant_rows, mixing, swap, next_swap, west, east, recv_cell
):
    levels, rows, lanes = mixing.shape[0] + 1, mixing.shape[1], mixing.shape[2]
    blocks = tracer_rows.shape[0] // rows
    members = blocks // levels
    squares = tracer_rows.shape[0] // lanes
    vmem = pl.BlockSpec(memory_space=pltpu.VMEM)
    params = pltpu.CompilerParams(vmem_limit_bytes=VMEM_BYTES)
    cost = pl.CostEstimate(flops=6000000, bytes_accessed=4000000, transcendentals=0)
    lat_sum, response, pivots = pl.pallas_call(
        lat_kernel,
        out_shape=(
            jax.ShapeDtypeStruct(tracer_rows.shape, jnp.float32),
            jax.ShapeDtypeStruct((levels, rows, lanes), jnp.float32),
            jax.ShapeDtypeStruct((levels, 3, rows, lanes), jnp.float32),
        ),
        in_specs=[pl.BlockSpec(memory_space=pltpu.SMEM)] + [vmem] * 5,
        out_specs=(vmem,) * 3,
        scratch_shapes=[
            pltpu.VMEM(((blocks + 1) * PADDED_ROWS, LANES), jnp.float32),
            pltpu.VMEM((levels, 7, ROWS, LANES), jnp.float32),
        ],
        compiler_params=params,
        cost_estimate=cost,
        name="advect_lat",
    )(lat_place, tracer_rows, courant_rows, mixing, swap, next_swap)
    sources, places = recv_cell.shape
    place_count = sources * places
    partial, leaf, place = pl.pallas_call(
        lon_kernel,
        out_shape=(
            jax.ShapeDtypeStruct((members, levels, rows, lanes), jnp.float32),
            jax.ShapeDtypeStruct((members, place_count), jnp.float32),
            jax.ShapeDtypeStruct((2, place_count // LANES, LANES), jnp.float32),
        ),
        in_specs=[vmem] * 7,
        out_specs=(vmem,) * 3,
        scratch_shapes=[
            pltpu.VMEM((squares * TURNED_ROWS, LANES), jnp.float32),
            pltpu.VMEM((squares * LANES, LANES), jnp.float32),
            pltpu.VMEM((LANES + 8, LANES), jnp.float32),
            pltpu.VMEM((squares * LANES, LANES), jnp.float32),
        ],
        compiler_params=params,
        cost_estimate=cost,
        name="advect_lon_and_mix",
    )(tracer_rows, courant_rows, west, east, lat_sum, pivots, recv_cell)
    return partial, response, leaf, place


def arrhenius(energy, leaf_temp):
    return jnp.exp(energy * (leaf_temp - 25.0) / (298.15 * GAS_CONSTANT * (leaf_temp + 273.15)))


def flux_kernel(
    received_ref, params_ref, leaf_ref, place_ref, partial_ref, response_ref,
    out_ref, surface_ref,
    column_ref, result_ref, copy_sems,
):
    members = params_ref.shape[1]
    types = params_ref.shape[2]
    sources = received_ref.shape[0]
    groups = sources // 2
    places = LANES // 2
    levels = response_ref.shape[0]
    quarters = ROWS // 2
    one, zero = jnp.bfloat16(1.0), jnp.bfloat16(0.0)

    carbox = 30.0 + 70.0 * params_ref[0]
    tables = jnp.concatenate(
        [carbox, (1.4 + 0.8 * params_ref[1]) * carbox, (0.005 + 0.025 * params_ref[2]) * carbox],
        axis=0,
    )
    table_parts = jnp.concatenate(bf16_parts(tables, 2), axis=1)

    half = lax.broadcasted_iota(jnp.int32, (groups, LANES), 1) < places

    def pair(values):
        low, high = values[0:groups], values[groups : 2 * groups]
        return (
            jnp.where(half, low, pltpu.roll(high, places, 1)),
            jnp.where(half, pltpu.roll(low, places, 1), high),
        )

    light, leaf_temp = pair(received_ref[:, 0, 0:LANES])
    water, flux_scale = pair(received_ref[:, 0, LANES : 2 * LANES])
    plant, _ = pair(received_ref[:, 0, 2 * LANES : 3 * LANES])
    leaf_temp = 35.0 * leaf_temp
    absorbed = 0.425 * (2000.0 * light)
    michaelis_carbon = 404.9 * arrhenius(79430.0, leaf_temp)
    michaelis_oxygen = 278.4 * arrhenius(36380.0, leaf_temp)
    compensation = 42.75 * arrhenius(37830.0, leaf_temp)
    column_ref[0] = absorbed
    column_ref[1] = arrhenius(65330.0, leaf_temp) * (0.2 + 0.8 * water)
    column_ref[2] = arrhenius(43540.0, leaf_temp)
    column_ref[3] = michaelis_carbon * (1.0 + 210.0 / michaelis_oxygen)
    column_ref[4] = compensation
    column_ref[5] = flux_scale
    column_ref[6] = 2.8 * absorbed
    column_ref[7] = (1.4 * 8.0) * compensation
    column_ref[8] = plant

    type_ids = (
        jnp.bitwise_and(lax.broadcasted_iota(jnp.int32, (2 * types, LANES), 0), types - 1)
        .astype(jnp.float32)
        .astype(jnp.bfloat16)
    )

    cell_ids = (
        lax.broadcasted_iota(jnp.int32, (256, LANES), 0).astype(jnp.float32).astype(jnp.bfloat16)
    )
    lefts, onehots = [], []
    for chunk in range(groups // CHUNK):
        rows = range(chunk * CHUNK, (chunk + 1) * CHUNK)
        span = slice(chunk * CHUNK * LANES, (chunk + 1) * CHUNK * LANES)

        def spread(ref):
            return jnp.concatenate(
                [jnp.broadcast_to(ref[row : row + 1, :], (members, LANES)) for row in rows],
                axis=1,
            )

        type_onehot = jnp.concatenate(
            [
                jnp.where(
                    type_ids == column_ref[8, row : row + 1, :].astype(jnp.bfloat16), one, zero
                )
                for row in rows
            ],
            axis=1,
        )
        params = jnp.dot(table_parts, type_onehot, preferred_element_type=jnp.float32)
        carbon_leaf = leaf_ref[:, span]
        warm = spread(column_ref.at[1])
        carboxylation = params[0:members] * warm
        transport_max = params[members : 2 * members] * spread(column_ref.at[2])
        respiration = params[2 * members : 3 * members] * warm
        total_rate = spread(column_ref.at[0]) + transport_max
        square = total_rate * total_rate - spread(column_ref.at[6]) * transport_max
        electron_rate = total_rate - square * lax.rsqrt(square)
        excess = carbon_leaf - spread(column_ref.at[4])
        rubisco_base = carbon_leaf + spread(column_ref.at[3])
        light_base = (1.4 * 4.0) * carbon_leaf + spread(column_ref.at[7])
        shared = excess / (rubisco_base * light_base)
        rubisco_rate = carboxylation * light_base * shared
        light_rate = electron_rate * rubisco_base * shared
        flux = spread(column_ref.at[5]) * (jnp.minimum(rubisco_rate, light_rate) - respiration)
        high, low = bf16_parts(flux, 2)
        quarter_index = spread(place_ref.at[0]).astype(jnp.bfloat16)
        left = []
        for quarter in range(quarters):
            here = quarter_index == jnp.bfloat16(quarter)
            left.append(jnp.where(here, high, zero))
            left.append(jnp.where(here, low, zero))
        cell_onehot = jnp.concatenate(
            [
                jnp.where(
                    cell_ids == place_ref[1, row : row + 1, :].astype(jnp.bfloat16), one, zero
                )
                for row in rows
            ],
            axis=1,
        )
        lefts.append(jnp.concatenate(left, axis=0))
        onehots.append(cell_onehot)

    summed = nt_dot(jnp.concatenate(lefts, axis=1), jnp.concatenate(onehots, axis=1))
    for quarter in range(quarters):
        start = quarter * 2 * members
        total = summed[start : start + members] + summed[start + members : start + 2 * members]
        surface_ref[:, 2 * quarter, :] = total[:, 0:LANES]
        surface_ref[:, 2 * quarter + 1, :] = total[:, LANES : 2 * LANES]

    copies = []
    share = members // OUT_COPIES
    for part in range(OUT_COPIES):
        responses = [response_ref[level] for level in range(levels)]
        for member in range(part * share, (part + 1) * share):
            surface = surface_ref[member]
            for level in range(levels):
                result_ref[member, level] = partial_ref[member, level] + responses[level] * surface
        span = pl.ds(part * share, share)
        copy = pltpu.make_async_copy(result_ref.at[span], out_ref.at[span], copy_sems.at[part])
        copy.start()
        copies.append(copy)
    for copy in copies:
        copy.wait()


def fluxes(received, land_params, leaf, place, partial, response):
    members, levels, rows, lanes = partial.shape
    vmem = pl.BlockSpec(memory_space=pltpu.VMEM)
    return pl.pallas_call(
        flux_kernel,
        out_shape=(
            jax.ShapeDtypeStruct(partial.shape, jnp.float32),
            jax.ShapeDtypeStruct((members, rows, lanes), jnp.float32),
        ),
        in_specs=[vmem] * 6,
        out_specs=(pl.BlockSpec(memory_space=pltpu.HBM), vmem),
        scratch_shapes=[
            pltpu.VMEM((9, received.shape[0] // 2, LANES), jnp.float32),
            pltpu.VMEM(partial.shape, jnp.float32),
            pltpu.SemaphoreType.DMA((OUT_COPIES,)),
        ],
        compiler_params=pltpu.CompilerParams(vmem_limit_bytes=VMEM_BYTES),
        cost_estimate=pl.CostEstimate(flops=600000000, bytes_accessed=3000000, transcendentals=400000),
        name="fluxes",
    )(received, land_params, leaf, place, partial, response)


def per_device(tracer, courant, mixing, forcing, plant_type, land_params, send_slot, recv_cell):
    members, levels, row_count, column_count = tracer.shape
    lon_count, lat_count = lax.axis_size("lon"), lax.axis_size("lat")
    tracer_rows = tracer.reshape(members * levels * row_count, column_count)
    courant_rows = courant.reshape(2 * levels * row_count, column_count)
    outgoing, first, second, westward, eastward = pack(
        tracer_rows, courant_rows, forcing, plant_type, send_slot, lon_count * lat_count
    )
    pairs = [(i, i + 1) for i in range(0, lat_count, 2)]
    next_pairs = [(i + 1, (i + 2) % lat_count) for i in range(0, lat_count, 2)]
    swap = lax.ppermute(first, "lat", pairs + [(b, a) for a, b in pairs])
    next_swap = lax.ppermute(second, "lat", next_pairs + [(b, a) for a, b in next_pairs])
    west = lax.ppermute(eastward, "lon", [(i, (i + 1) % lon_count) for i in range(lon_count)])
    east = lax.ppermute(westward, "lon", [((i + 1) % lon_count, i) for i in range(lon_count)])
    received = lax.all_to_all(outgoing, ("lat", "lon"), split_axis=0, concat_axis=0, tiled=True)
    lat_place = jnp.stack([lax.axis_index("lat"), jnp.int32(lat_count)]).astype(jnp.int32)
    partial, response, leaf, place = advect_and_mix(
        lat_place, tracer_rows, courant_rows, mixing, swap, next_swap, west, east, recv_cell
    )
    return fluxes(received, land_params, leaf, place, partial, response)


def solution(mesh):
    in_specs = (
        P("mem", None, "lat", "lon"),
        P(None, None, "lat", "lon"),
        P(None, "lat", "lon"),
        P(None, ("lon", "lat")),
        P(("lon", "lat")),
        P(None, "mem", None),
        P(("lon", "lat")),
        P(("lon", "lat"), None),
    )
    out_specs = (P("mem", None, "lat", "lon"), P("mem", "lat", "lon"))
    return jax.shard_map(
        per_device, mesh=mesh, in_specs=in_specs, out_specs=out_specs, check_vma=False
    )
```

```python
import functools

import jax
import jax.numpy as jnp
from jax import lax
from jax.experimental import pallas as pl
from jax.experimental.pallas import tpu as pltpu
from jax.sharding import PartitionSpec as P

FLUX_SCALE = 0.02
GAS_CONSTANT = 8.314
LANES = 128
ROWS = 8
VMEM_BYTES = 40 * 2**20
PARTS = 2
OUT_COPIES = 4


def nt_dot(left, right):
    return lax.dot_general(
        left, right, (((1,), (1,)), ((), ())), preferred_element_type=jnp.float32
    )


def bf16_parts(values, count):
    parts = []
    rest = values
    for _ in range(count):
        part = rest.astype(jnp.bfloat16)
        rest = rest - part.astype(jnp.float32)
        parts.append(part)
    return parts


def pack_kernel(
    tracer_hbm, courant_hbm, forcing_hbm, type_hbm, slot_hbm,
    payload_hbm, first_ref, second_ref, westward_ref, eastward_ref,
    payload_ref, cells_ref, faces_ref, forcing_ref, type_ref, slot_ref, copy_sems,
):
    moves = (
        (slot_hbm, slot_ref),
        (forcing_hbm, forcing_ref),
        (type_hbm, type_ref),
        (tracer_hbm, cells_ref),
        (courant_hbm, faces_ref),
    )
    copies = [
        pltpu.make_async_copy(source, target, copy_sems.at[place])
        for place, (source, target) in enumerate(moves)
    ]
    for copy in copies:
        copy.start()
    for copy in copies[0:3]:
        copy.wait()

    columns = slot_ref.shape[1]
    slot = slot_ref[...]
    lon_tile = jnp.right_shift(slot, 8).astype(jnp.float32).astype(jnp.bfloat16)
    place = jnp.bitwise_and(slot, 255).astype(jnp.float32).astype(jnp.bfloat16)
    one, zero = jnp.bfloat16(1.0), jnp.bfloat16(0.0)

    def ids(count):
        return (
            lax.broadcasted_iota(jnp.int32, (count, columns), 0)
            .astype(jnp.float32)
            .astype(jnp.bfloat16)
        )

    tile_mask = ids(16) == lon_tile
    place_onehot = jnp.where(ids(256) == place, one, zero)
    leaf_area = 0.5 + 5.5 * forcing_ref[3:4, :]
    area_share = 0.05 + 0.55 * forcing_ref[4:5, :]
    canopy_scale = (1.0 - jnp.exp(-0.5 * leaf_area)) / 0.5
    values = [
        (forcing_ref[0:1, :], PARTS),
        (forcing_ref[1:2, :], PARTS),
        (forcing_ref[2:3, :], PARTS),
        (-FLUX_SCALE * area_share * canopy_scale, PARTS),
        (type_ref[...].astype(jnp.float32), 1),
    ]
    rows = []
    for value, count in values:
        for part in bf16_parts(value, count):
            rows.append(jnp.where(tile_mask, jnp.broadcast_to(part, (16, columns)), zero))
    moved = nt_dot(jnp.concatenate(rows, axis=0), place_onehot)
    placed = []
    start = 0
    for value, count in values:
        total = moved[start : start + 16]
        for step in range(1, count):
            total = total + moved[start + 16 * step : start + 16 * (step + 1)]
        placed.append(total)
        start += 16 * count
    low_half = lax.broadcasted_iota(jnp.int32, (16, LANES), 1) < 64
    for tile in range(4):
        span = slice((tile // 2) * LANES, (tile // 2 + 1) * LANES)
        for pair in range(3):
            left = placed[2 * pair][:, span]
            right = placed[min(2 * pair + 1, 4)][:, span]
            if tile % 2 == 0:
                joined = jnp.where(low_half, left, pltpu.roll(right, 64, 1))
            else:
                joined = jnp.where(low_half, pltpu.roll(left, 64, 1), right)
            payload_ref[tile * 16 : (tile + 1) * 16, 0, pair * LANES : (pair + 1) * LANES] = joined

    send = pltpu.make_async_copy(payload_ref, payload_hbm, copy_sems.at[5])
    send.start()
    for copy in copies[3:5]:
        copy.wait()
    blocks = cells_ref.shape[0] // ROWS
    levels = faces_ref.shape[0] // (2 * ROWS)
    even = lax.rem(lax.axis_index("lat"), 2) == 0
    for step in range(3):
        low = cells_ref[pl.ds(step, blocks, stride=ROWS), :]
        high = cells_ref[pl.ds(ROWS - 3 + step, blocks, stride=ROWS), :]
        span = slice(step * blocks, (step + 1) * blocks)
        first_ref[span, :] = jnp.where(even, high, low)
        second_ref[span, :] = jnp.where(even, low, high)
    last_faces = faces_ref[pl.ds(levels * ROWS + ROWS - 1, levels, stride=ROWS), :]
    first_ref[3 * blocks : 3 * blocks + levels, :] = last_faces
    second_ref[3 * blocks : 3 * blocks + levels, :] = last_faces
    squares = cells_ref.shape[0] // LANES
    for square in range(squares):
        turned = cells_ref[square * LANES : (square + 1) * LANES, :].T
        westward_ref[3 * square : 3 * square + 3, :] = turned[0:3]
        eastward_ref[3 * square : 3 * square + 3, :] = turned[LANES - 3 : LANES]
    turned = faces_ref[...].T
    westward_ref[3 * squares : 3 * squares + ROWS, :] = turned[LANES - ROWS : LANES]
    eastward_ref[3 * squares : 3 * squares + ROWS, :] = turned[LANES - ROWS : LANES]
    send.wait()


def pack(tracer_rows, courant_rows, forcing, plant_type, send_slot, tiles):
    columns = send_slot.shape[0]
    blocks = tracer_rows.shape[0] // ROWS
    levels = courant_rows.shape[0] // (2 * ROWS)
    side_rows = 3 * (tracer_rows.shape[0] // LANES) + ROWS
    vmem = pl.BlockSpec(memory_space=pltpu.VMEM)
    hbm = pl.BlockSpec(memory_space=pltpu.HBM)
    return pl.pallas_call(
        pack_kernel,
        out_shape=(
            jax.ShapeDtypeStruct((tiles, 1, 3 * LANES), jnp.float32),
            jax.ShapeDtypeStruct((3 * blocks + levels, LANES), jnp.float32),
            jax.ShapeDtypeStruct((3 * blocks + levels, LANES), jnp.float32),
            jax.ShapeDtypeStruct((side_rows, LANES), jnp.float32),
            jax.ShapeDtypeStruct((side_rows, LANES), jnp.float32),
        ),
        in_specs=[hbm] * 5,
        out_specs=(hbm,) + (vmem,) * 4,
        scratch_shapes=[
            pltpu.VMEM((tiles, 1, 3 * LANES), jnp.float32),
            pltpu.VMEM(tracer_rows.shape, jnp.float32),
            pltpu.VMEM(courant_rows.shape, jnp.float32),
            pltpu.VMEM(forcing.shape, jnp.float32),
            pltpu.VMEM((1, columns), jnp.int32),
            pltpu.VMEM((1, columns), jnp.int32),
            pltpu.SemaphoreType.DMA((6,)),
        ],
        compiler_params=pltpu.CompilerParams(vmem_limit_bytes=VMEM_BYTES),
        cost_estimate=pl.CostEstimate(
            flops=300000000, bytes_accessed=2500000, transcendentals=columns
        ),
        name="pack",
    )(*(
        pltpu.with_memory_space_constraint(array, pltpu.HBM)
        for array in (
            tracer_rows, courant_rows, forcing,
            plant_type.reshape(1, columns), send_slot.reshape(1, columns),
        )
    ))


def face_weights(face_courant):
    half = 0.5 * face_courant
    upwind = face_courant > 0
    shrink_left = 1.0 - 2.0 / 3.0 * face_courant
    shrink_right = 1.0 + 2.0 / 3.0 * face_courant
    curve = half * jnp.where(upwind, shrink_left, shrink_right)
    middle = face_courant * jnp.where(upwind, 1.0 - half - 3.0 * curve, 1.0 + half + 3.0 * curve)
    left_edge = face_courant * jnp.where(upwind, half - 3.0 * curve, 0.0)
    right_edge = face_courant * jnp.where(upwind, 0.0, 3.0 * curve - half)
    left_cell = face_courant * jnp.where(upwind, 6.0 * curve, 0.0)
    right_cell = face_courant * jnp.where(upwind, 0.0, -6.0 * curve)
    near, far = 7.0 / 12.0, 1.0 / 12.0
    return [
        -far * left_edge,
        near * left_edge - far * middle,
        near * (middle + left_edge) - far * right_edge + left_cell,
        near * (middle + right_edge) - far * left_edge + right_cell,
        near * right_edge - far * middle,
        -far * right_edge,
    ]


def divergence_weights(face_after, face_before):
    after = face_weights(face_after)
    before = face_weights(face_before)
    taps = []
    for offset in range(7):
        if offset == 0:
            taps.append(-before[0])
        elif offset == 6:
            taps.append(after[5])
        else:
            taps.append(after[offset - 1] - before[offset])
    return taps


CHUNK = 4
TURNED_ROWS = LANES + 16
PADDED_ROWS = 2 * ROWS


def lat_kernel(
    lat_ref, tracer_ref, courant_ref, mixing_ref, swap_ref, next_swap_ref,
    sum_ref, response_ref, pivot_ref,
    rows_ref, weight_ref,
):
    levels = mixing_ref.shape[0] + 1
    blocks = tracer_ref.shape[0] // ROWS
    members = blocks // levels
    half = levels * ROWS
    first = lat_ref[0] == 0
    even = lax.rem(lat_ref[0], 2) == 0
    last = lat_ref[0] == lat_ref[1] - 1

    zero = jnp.zeros((blocks, LANES), jnp.float32)
    for step in range(3):
        span = slice(step * blocks, (step + 1) * blocks)
        rows_ref[pl.ds(5 + step, blocks, stride=PADDED_ROWS), :] = jnp.where(
            first, zero, jnp.where(even, next_swap_ref[span, :], swap_ref[span, :])
        )
        rows_ref[pl.ds(PADDED_ROWS + step, blocks, stride=PADDED_ROWS), :] = jnp.where(
            last, zero, jnp.where(even, swap_ref[span, :], next_swap_ref[span, :])
        )
    for block in range(blocks):
        rows_ref[block * PADDED_ROWS + 8 : block * PADDED_ROWS + 16, :] = tracer_ref[
            block * ROWS : (block + 1) * ROWS, :
        ]
    row = lax.broadcasted_iota(jnp.int32, (ROWS, LANES), 0)
    for level in range(levels):
        north_face = courant_ref[half + level * ROWS : half + (level + 1) * ROWS, :]
        place = slice(3 * blocks + level, 3 * blocks + level + 1)
        below = jnp.where(even, next_swap_ref[place, :], swap_ref[place, :])
        below = jnp.where(first, 0.0, below)
        south_face = jnp.where(row == 0, below, pltpu.roll(north_face, 1, 0))
        north_face = jnp.where(jnp.logical_and(last, row == ROWS - 1), 0.0, north_face)
        taps = divergence_weights(north_face, south_face)
        for offset in range(7):
            weight_ref[level, offset] = 1.0 - taps[3] if offset == 3 else -taps[offset]

    ratio = None
    response = []
    for level in range(levels):
        pivot = jnp.ones((ROWS, LANES), jnp.float32)
        if level > 0:
            pivot = pivot + mixing_ref[level - 1]
        if level < levels - 1:
            pivot = pivot + mixing_ref[level]
        if level > 0:
            pivot = pivot - mixing_ref[level - 1] * ratio
        inverse = 1.0 / pivot
        carried = inverse
        if level > 0:
            carried = mixing_ref[level - 1] * inverse
            response.append(carried * response[-1])
        else:
            response.append(inverse)
        pivot_ref[level, 0] = inverse
        pivot_ref[level, 1] = carried
        if level < levels - 1:
            ratio = mixing_ref[level] * inverse
            pivot_ref[level, 2] = ratio
    for level in range(levels - 1, -1, -1):
        if level < levels - 1:
            response[level] = response[level] + pivot_ref[level, 2] * response[level + 1]
        response_ref[level] = response[level]

    together = 4

    def member_step(index, carry):
        for level in range(levels):
            taps = [weight_ref[level, offset] for offset in range(7)]
            for step in range(together):
                block = (index * together + step) * levels + level
                base = pl.multiple_of(block * PADDED_ROWS, PADDED_ROWS) + 5
                total = taps[0] * rows_ref[pl.ds(base, ROWS), :]
                for offset in range(1, 7):
                    total = total + taps[offset] * rows_ref[pl.ds(base + offset, ROWS), :]
                sum_ref[pl.ds(pl.multiple_of(block * ROWS, ROWS), ROWS), :] = total
        return carry

    lax.fori_loop(0, members // together, member_step, 0)


def lon_kernel(
    tracer_ref, courant_ref, west_ref, east_ref, sum_ref, pivot_ref, cell_ref,
    out_ref, leaf_ref, place_ref,
    turned_ref, turned_sum_ref, turned_courant_ref, lon_ref,
):
    members, levels = out_ref.shape[0], out_ref.shape[1]
    squares = tracer_ref.shape[0] // LANES

    for square in range(squares):
        base = square * TURNED_ROWS
        turned_ref[base + 5 : base + 8, :] = west_ref[3 * square : 3 * square + 3, :]
        turned_ref[base + 8 + LANES : base + 11 + LANES, :] = east_ref[
            3 * square : 3 * square + 3, :
        ]
        turned_ref[base + 8 : base + 8 + LANES, :] = tracer_ref[
            square * LANES : (square + 1) * LANES, :
        ].T
    half = levels * ROWS
    turned_faces = courant_ref[...].T
    low_half = lax.broadcasted_iota(jnp.int32, (LANES, LANES), 1) < half
    turned_faces = jnp.where(low_half, turned_faces, pltpu.roll(turned_faces, half, 1))
    turned_courant_ref[8 : 8 + LANES, :] = turned_faces
    side_face = west_ref[3 * squares : 3 * squares + ROWS, :]
    side_face = jnp.where(low_half[0:ROWS], side_face, pltpu.roll(side_face, half, 1))
    turned_courant_ref[0:8, :] = side_face

    def lon_step(tile, carry):
        start = pl.multiple_of(tile * ROWS, ROWS)
        taps = divergence_weights(
            turned_courant_ref[pl.ds(start + 8, ROWS), :],
            turned_courant_ref[pl.ds(start + 7, ROWS), :],
        )
        for square in range(squares):
            base = square * TURNED_ROWS + start + 5
            total = taps[0] * turned_ref[pl.ds(base, ROWS), :]
            for offset in range(1, 7):
                total = total + taps[offset] * turned_ref[pl.ds(base + offset, ROWS), :]
            turned_sum_ref[pl.ds(square * LANES + start, ROWS), :] = total
        return carry

    lax.fori_loop(0, LANES // ROWS, lon_step, 0)
    for square in range(squares):
        span = slice(square * LANES, (square + 1) * LANES)
        lon_ref[span, :] = turned_sum_ref[span, :].T

    together = 4

    def member_step(index, carry):
        swept = [None] * together
        stored = [[None] * levels for _ in range(together)]
        for level in range(levels):
            inverse = pivot_ref[level, 0]
            carried = pivot_ref[level, 1]
            for step in range(together):
                block = (index * together + step) * levels + level
                span = pl.ds(pl.multiple_of(block * ROWS, ROWS), ROWS)
                total = (sum_ref[span, :] - lon_ref[span, :]) * inverse
                if level > 0:
                    total = total + carried * swept[step]
                swept[step] = total
                stored[step][level] = total
        for level in range(levels - 1, -1, -1):
            ratio = pivot_ref[level, 2] if level < levels - 1 else None
            for step in range(together):
                if level < levels - 1:
                    swept[step] = stored[step][level] + ratio * swept[step]
                out_ref[index * together + step, level] = swept[step]
        return carry

    lax.fori_loop(0, members // together, member_step, 0)
    near_cells(tracer_ref, cell_ref, leaf_ref, place_ref, members, levels)


def near_cells(tracer_ref, cell_ref, leaf_ref, place_ref, members, levels):
    sources = cell_ref.shape[0]
    groups = sources // 2
    quarters = ROWS // 2
    stride = levels * ROWS
    bottom = jnp.concatenate(
        [
            jnp.concatenate(
                [
                    tracer_ref[pl.ds(2 * quarter + side, members, stride=stride), :]
                    for side in range(2)
                ],
                axis=1,
            )
            for quarter in range(quarters)
        ],
        axis=0,
    )
    bottom_parts = jnp.concatenate(bf16_parts(bottom, 2), axis=0)
    cells = jnp.concatenate(
        [cell_ref[pl.ds(tile, sources // 4, stride=4), :] for tile in range(4)], axis=0
    )
    cells = jnp.concatenate([cells[0:groups], cells[groups : 2 * groups]], axis=1)
    place_ref[0] = jnp.right_shift(cells, 8).astype(jnp.float32)
    lane = jnp.bitwise_and(cells, 255).astype(jnp.float32)
    place_ref[1] = lane
    cell_ids = (
        lax.broadcasted_iota(jnp.int32, (256, LANES), 0).astype(jnp.float32).astype(jnp.bfloat16)
    )
    one, zero = jnp.bfloat16(1.0), jnp.bfloat16(0.0)
    for chunk in range(groups // CHUNK):
        rows = range(chunk * CHUNK, (chunk + 1) * CHUNK)
        span = slice(chunk * CHUNK * LANES, (chunk + 1) * CHUNK * LANES)
        cell_onehot = jnp.concatenate(
            [
                jnp.where(cell_ids == lane[row : row + 1, :].astype(jnp.bfloat16), one, zero)
                for row in rows
            ],
            axis=1,
        )
        near = jnp.dot(bottom_parts, cell_onehot, preferred_element_type=jnp.float32)
        near = near[0 : quarters * members] + near[quarters * members : 2 * quarters * members]
        quarter_index = jnp.concatenate(
            [
                jnp.broadcast_to(place_ref[0, row : row + 1, :], (members, LANES))
                for row in rows
            ],
            axis=1,
        )
        picked = near[0:members]
        for quarter in range(1, quarters):
            picked = jnp.where(
                quarter_index == quarter, near[quarter * members : (quarter + 1) * members], picked
            )
        leaf_ref[:, span] = 280.0 + 70.0 * picked


def advect_and_mix(
    lat_place, tracer_rows, courant_rows, mixing, swap, next_swap, west, east, recv_cell
):
    levels, rows, lanes = mixing.shape[0] + 1, mixing.shape[1], mixing.shape[2]
    blocks = tracer_rows.shape[0] // rows
    members = blocks // levels
    squares = tracer_rows.shape[0] // lanes
    vmem = pl.BlockSpec(memory_space=pltpu.VMEM)
    params = pltpu.CompilerParams(vmem_limit_bytes=VMEM_BYTES)
    cost = pl.CostEstimate(flops=6000000, bytes_accessed=4000000, transcendentals=0)
    lat_sum, response, pivots = pl.pallas_call(
        lat_kernel,
        out_shape=(
            jax.ShapeDtypeStruct(tracer_rows.shape, jnp.float32),
            jax.ShapeDtypeStruct((levels, rows, lanes), jnp.float32),
            jax.ShapeDtypeStruct((levels, 3, rows, lanes), jnp.float32),
        ),
        in_specs=[pl.BlockSpec(memory_space=pltpu.SMEM)] + [vmem] * 5,
        out_specs=(vmem,) * 3,
        scratch_shapes=[
            pltpu.VMEM(((blocks + 1) * PADDED_ROWS, LANES), jnp.float32),
            pltpu.VMEM((levels, 7, ROWS, LANES), jnp.float32),
        ],
        compiler_params=params,
        cost_estimate=cost,
        name="advect_lat",
    )(lat_place, tracer_rows, courant_rows, mixing, swap, next_swap)
    sources, places = recv_cell.shape
    place_count = sources * places
    partial, leaf, place = pl.pallas_call(
        lon_kernel,
        out_shape=(
            jax.ShapeDtypeStruct((members, levels, rows, lanes), jnp.float32),
            jax.ShapeDtypeStruct((members, place_count), jnp.float32),
            jax.ShapeDtypeStruct((2, place_count // LANES, LANES), jnp.float32),
        ),
        in_specs=[vmem] * 7,
        out_specs=(vmem,) * 3,
        scratch_shapes=[
            pltpu.VMEM((squares * TURNED_ROWS, LANES), jnp.float32),
            pltpu.VMEM((squares * LANES, LANES), jnp.float32),
            pltpu.VMEM((LANES + 8, LANES), jnp.float32),
            pltpu.VMEM((squares * LANES, LANES), jnp.float32),
        ],
        compiler_params=params,
        cost_estimate=cost,
        name="advect_lon_and_mix",
    )(tracer_rows, courant_rows, west, east, lat_sum, pivots, recv_cell)
    return partial, response, leaf, place


def arrhenius(energy, leaf_temp):
    return jnp.exp(energy * (leaf_temp - 25.0) / (298.15 * GAS_CONSTANT * (leaf_temp + 273.15)))


def flux_kernel(
    received_ref, params_ref, leaf_ref, place_ref, partial_ref, response_ref,
    out_ref, surface_ref,
    column_ref, result_ref, copy_sems,
):
    members = params_ref.shape[1]
    types = params_ref.shape[2]
    sources = received_ref.shape[0]
    groups = sources // 2
    places = LANES // 2
    levels = response_ref.shape[0]
    quarters = ROWS // 2
    one, zero = jnp.bfloat16(1.0), jnp.bfloat16(0.0)

    carbox = 30.0 + 70.0 * params_ref[0]
    tables = jnp.concatenate(
        [carbox, (1.4 + 0.8 * params_ref[1]) * carbox, (0.005 + 0.025 * params_ref[2]) * carbox],
        axis=0,
    )
    table_parts = jnp.concatenate(bf16_parts(tables, 2), axis=1)

    half = lax.broadcasted_iota(jnp.int32, (groups, LANES), 1) < places

    def pair(values):
        low, high = values[0:groups], values[groups : 2 * groups]
        return (
            jnp.where(half, low, pltpu.roll(high, places, 1)),
            jnp.where(half, pltpu.roll(low, places, 1), high),
        )

    light, leaf_temp = pair(received_ref[:, 0, 0:LANES])
    water, flux_scale = pair(received_ref[:, 0, LANES : 2 * LANES])
    plant, _ = pair(received_ref[:, 0, 2 * LANES : 3 * LANES])
    leaf_temp = 35.0 * leaf_temp
    absorbed = 0.425 * (2000.0 * light)
    michaelis_carbon = 404.9 * arrhenius(79430.0, leaf_temp)
    michaelis_oxygen = 278.4 * arrhenius(36380.0, leaf_temp)
    compensation = 42.75 * arrhenius(37830.0, leaf_temp)
    column_ref[0] = absorbed
    column_ref[1] = arrhenius(65330.0, leaf_temp) * (0.2 + 0.8 * water)
    column_ref[2] = arrhenius(43540.0, leaf_temp)
    column_ref[3] = michaelis_carbon * (1.0 + 210.0 / michaelis_oxygen)
    column_ref[4] = compensation
    column_ref[5] = flux_scale
    column_ref[6] = 2.8 * absorbed
    column_ref[7] = (1.4 * 8.0) * compensation
    column_ref[8] = plant

    type_ids = (
        jnp.bitwise_and(lax.broadcasted_iota(jnp.int32, (2 * types, LANES), 0), types - 1)
        .astype(jnp.float32)
        .astype(jnp.bfloat16)
    )

    cell_ids = (
        lax.broadcasted_iota(jnp.int32, (256, LANES), 0).astype(jnp.float32).astype(jnp.bfloat16)
    )
    lefts, onehots = [], []
    for chunk in range(groups // CHUNK):
        rows = range(chunk * CHUNK, (chunk + 1) * CHUNK)
        span = slice(chunk * CHUNK * LANES, (chunk + 1) * CHUNK * LANES)

        def spread(ref):
            return jnp.concatenate(
                [jnp.broadcast_to(ref[row : row + 1, :], (members, LANES)) for row in rows],
                axis=1,
            )

        type_onehot = jnp.concatenate(
            [
                jnp.where(
                    type_ids == column_ref[8, row : row + 1, :].astype(jnp.bfloat16), one, zero
                )
                for row in rows
            ],
            axis=1,
        )
        params = jnp.dot(table_parts, type_onehot, preferred_element_type=jnp.float32)
        carbon_leaf = leaf_ref[:, span]
        warm = spread(column_ref.at[1])
        carboxylation = params[0:members] * warm
        transport_max = params[members : 2 * members] * spread(column_ref.at[2])
        respiration = params[2 * members : 3 * members] * warm
        total_rate = spread(column_ref.at[0]) + transport_max
        square = total_rate * total_rate - spread(column_ref.at[6]) * transport_max
        electron_rate = total_rate - square * lax.rsqrt(square)
        excess = carbon_leaf - spread(column_ref.at[4])
        rubisco_base = carbon_leaf + spread(column_ref.at[3])
        light_base = (1.4 * 4.0) * carbon_leaf + spread(column_ref.at[7])
        shared = excess / (rubisco_base * light_base)
        rubisco_rate = carboxylation * light_base * shared
        light_rate = electron_rate * rubisco_base * shared
        flux = spread(column_ref.at[5]) * (jnp.minimum(rubisco_rate, light_rate) - respiration)
        high, low = bf16_parts(flux, 2)
        quarter_index = spread(place_ref.at[0]).astype(jnp.bfloat16)
        left = []
        for quarter in range(quarters):
            here = quarter_index == jnp.bfloat16(quarter)
            left.append(jnp.where(here, high, zero))
            left.append(jnp.where(here, low, zero))
        cell_onehot = jnp.concatenate(
            [
                jnp.where(
                    cell_ids == place_ref[1, row : row + 1, :].astype(jnp.bfloat16), one, zero
                )
                for row in rows
            ],
            axis=1,
        )
        lefts.append(jnp.concatenate(left, axis=0))
        onehots.append(cell_onehot)

    summed = nt_dot(jnp.concatenate(lefts, axis=1), jnp.concatenate(onehots, axis=1))
    for quarter in range(quarters):
        start = quarter * 2 * members
        total = summed[start : start + members] + summed[start + members : start + 2 * members]
        surface_ref[:, 2 * quarter, :] = total[:, 0:LANES]
        surface_ref[:, 2 * quarter + 1, :] = total[:, LANES : 2 * LANES]

    copies = []
    share = members // OUT_COPIES
    for part in range(OUT_COPIES):
        responses = [response_ref[level] for level in range(levels)]
        for member in range(part * share, (part + 1) * share):
            surface = surface_ref[member]
            for level in range(levels):
                result_ref[member, level] = partial_ref[member, level] + responses[level] * surface
        span = pl.ds(part * share, share)
        copy = pltpu.make_async_copy(result_ref.at[span], out_ref.at[span], copy_sems.at[part])
        copy.start()
        copies.append(copy)
    for copy in copies:
        copy.wait()


def fluxes(received, land_params, leaf, place, partial, response):
    members, levels, rows, lanes = partial.shape
    vmem = pl.BlockSpec(memory_space=pltpu.VMEM)
    return pl.pallas_call(
        flux_kernel,
        out_shape=(
            jax.ShapeDtypeStruct(partial.shape, jnp.float32),
            jax.ShapeDtypeStruct((members, rows, lanes), jnp.float32),
        ),
        in_specs=[vmem] * 6,
        out_specs=(pl.BlockSpec(memory_space=pltpu.HBM), vmem),
        scratch_shapes=[
            pltpu.VMEM((9, received.shape[0] // 2, LANES), jnp.float32),
            pltpu.VMEM(partial.shape, jnp.float32),
            pltpu.SemaphoreType.DMA((OUT_COPIES,)),
        ],
        compiler_params=pltpu.CompilerParams(vmem_limit_bytes=VMEM_BYTES),
        cost_estimate=pl.CostEstimate(flops=600000000, bytes_accessed=3000000, transcendentals=400000),
        name="fluxes",
    )(received, land_params, leaf, place, partial, response)


def per_device(tracer, courant, mixing, forcing, plant_type, land_params, send_slot, recv_cell):
    members, levels, row_count, column_count = tracer.shape
    lon_count, lat_count = lax.axis_size("lon"), lax.axis_size("lat")
    tracer_rows = tracer.reshape(members * levels * row_count, column_count)
    courant_rows = courant.reshape(2 * levels * row_count, column_count)
    outgoing, first, second, westward, eastward = pack(
        tracer_rows, courant_rows, forcing, plant_type, send_slot, lon_count * lat_count
    )
    pairs = [(i, i + 1) for i in range(0, lat_count, 2)]
    next_pairs = [(i + 1, (i + 2) % lat_count) for i in range(0, lat_count, 2)]
    swap = lax.ppermute(first, "lat", pairs + [(b, a) for a, b in pairs])
    next_swap = lax.ppermute(second, "lat", next_pairs + [(b, a) for a, b in next_pairs])
    west = lax.ppermute(eastward, "lon", [(i, (i + 1) % lon_count) for i in range(lon_count)])
    east = lax.ppermute(westward, "lon", [((i + 1) % lon_count, i) for i in range(lon_count)])
    received = lax.all_to_all(outgoing, ("lat", "lon"), split_axis=0, concat_axis=0, tiled=True)
    lat_place = jnp.stack([lax.axis_index("lat"), jnp.int32(lat_count)]).astype(jnp.int32)
    partial, response, leaf, place = advect_and_mix(
        lat_place, tracer_rows, courant_rows, mixing, swap, next_swap, west, east, recv_cell
    )
    return fluxes(received, land_params, leaf, place, partial, response)


def solution(mesh):
    in_specs = (
        P("mem", None, "lat", "lon"),
        P(None, None, "lat", "lon"),
        P(None, "lat", "lon"),
        P(None, ("lon", "lat")),
        P(("lon", "lat")),
        P(None, "mem", None),
        P(("lon", "lat")),
        P(("lon", "lat"), None),
    )
    out_specs = (P("mem", None, "lat", "lon"), P("mem", "lat", "lon"))
    return jax.shard_map(
        per_device, mesh=mesh, in_specs=in_specs, out_specs=out_specs, check_vma=False
    )
```

```python
import functools

import jax
import jax.numpy as jnp
from jax import lax
from jax.experimental import pallas as pl
from jax.experimental.pallas import tpu as pltpu
from jax.sharding import PartitionSpec as P

FLUX_SCALE = 0.02
GAS_CONSTANT = 8.314
LANES = 128
ROWS = 8
VMEM_BYTES = 40 * 2**20
PARTS = 2
OUT_COPIES = 4


def nt_dot(left, right):
    return lax.dot_general(
        left, right, (((1,), (1,)), ((), ())), preferred_element_type=jnp.float32
    )


def bf16_parts(values, count):
    parts = []
    rest = values
    for _ in range(count):
        part = rest.astype(jnp.bfloat16)
        rest = rest - part.astype(jnp.float32)
        parts.append(part)
    return parts


def pack_kernel(
    tracer_hbm, courant_hbm, forcing_hbm, type_hbm, slot_hbm,
    payload_ref, first_ref, second_ref, side_next_ref, side_first_ref,
    cells_ref, faces_ref, forcing_ref, type_ref, slot_ref, copy_sems,
):
    moves = (
        (slot_hbm, slot_ref),
        (forcing_hbm, forcing_ref),
        (type_hbm, type_ref),
        (tracer_hbm, cells_ref),
        (courant_hbm, faces_ref),
    )
    copies = [
        pltpu.make_async_copy(source, target, copy_sems.at[place])
        for place, (source, target) in enumerate(moves)
    ]
    for copy in copies:
        copy.start()
    for copy in copies[0:3]:
        copy.wait()

    columns = slot_ref.shape[1]
    slot = slot_ref[...]
    lon_tile = jnp.right_shift(slot, 8).astype(jnp.float32).astype(jnp.bfloat16)
    place = jnp.bitwise_and(slot, 255).astype(jnp.float32).astype(jnp.bfloat16)
    one, zero = jnp.bfloat16(1.0), jnp.bfloat16(0.0)

    def ids(count):
        return (
            lax.broadcasted_iota(jnp.int32, (count, columns), 0)
            .astype(jnp.float32)
            .astype(jnp.bfloat16)
        )

    tile_mask = ids(16) == lon_tile
    place_onehot = jnp.where(ids(256) == place, one, zero)
    leaf_area = 0.5 + 5.5 * forcing_ref[3:4, :]
    area_share = 0.05 + 0.55 * forcing_ref[4:5, :]
    canopy_scale = (1.0 - jnp.exp(-0.5 * leaf_area)) / 0.5
    values = [
        (forcing_ref[0:1, :], PARTS),
        (forcing_ref[1:2, :], PARTS),
        (forcing_ref[2:3, :], PARTS),
        (-FLUX_SCALE * area_share * canopy_scale, PARTS),
        (type_ref[...].astype(jnp.float32), 1),
    ]
    rows = []
    for value, count in values:
        for part in bf16_parts(value, count):
            rows.append(jnp.where(tile_mask, jnp.broadcast_to(part, (16, columns)), zero))
    moved = nt_dot(jnp.concatenate(rows, axis=0), place_onehot)
    placed = []
    start = 0
    for value, count in values:
        total = moved[start : start + 16]
        for step in range(1, count):
            total = total + moved[start + 16 * step : start + 16 * (step + 1)]
        placed.append(total)
        start += 16 * count
    low_half = lax.broadcasted_iota(jnp.int32, (16, LANES), 1) < 64
    for tile in range(4):
        span = slice((tile // 2) * LANES, (tile // 2 + 1) * LANES)
        for pair in range(3):
            left = placed[2 * pair][:, span]
            right = placed[min(2 * pair + 1, 4)][:, span]
            if tile % 2 == 0:
                joined = jnp.where(low_half, left, pltpu.roll(right, 64, 1))
            else:
                joined = jnp.where(low_half, pltpu.roll(left, 64, 1), right)
            payload_ref[tile * 16 : (tile + 1) * 16, 0, pair * LANES : (pair + 1) * LANES] = joined

    for copy in copies[3:5]:
        copy.wait()
    blocks = cells_ref.shape[0] // ROWS
    levels = faces_ref.shape[0] // (2 * ROWS)
    even = lax.rem(lax.axis_index("lat"), 2) == 0
    even_lon = lax.rem(lax.axis_index("lon"), 2) == 0
    for step in range(3):
        low = cells_ref[pl.ds(step, blocks, stride=ROWS), :]
        high = cells_ref[pl.ds(ROWS - 3 + step, blocks, stride=ROWS), :]
        span = slice(step * blocks, (step + 1) * blocks)
        first_ref[span, :] = jnp.where(even, high, low)
        second_ref[span, :] = jnp.where(even, low, high)
    last_faces = faces_ref[pl.ds(levels * ROWS + ROWS - 1, levels, stride=ROWS), :]
    first_ref[3 * blocks : 3 * blocks + levels, :] = last_faces
    second_ref[3 * blocks : 3 * blocks + levels, :] = last_faces
    squares = cells_ref.shape[0] // LANES
    for square in range(squares):
        turned = cells_ref[square * LANES : (square + 1) * LANES, :].T
        low, high = turned[0:3], turned[LANES - 3 : LANES]
        side_next_ref[3 * square : 3 * square + 3, :] = jnp.where(even_lon, low, high)
        side_first_ref[3 * square : 3 * square + 3, :] = jnp.where(even_lon, high, low)
    turned = faces_ref[...].T
    side_next_ref[3 * squares : 3 * squares + ROWS, :] = turned[LANES - ROWS : LANES]
    side_first_ref[3 * squares : 3 * squares + ROWS, :] = turned[LANES - ROWS : LANES]


def pack(tracer_rows, courant_rows, forcing, plant_type, send_slot, tiles):
    columns = send_slot.shape[0]
    blocks = tracer_rows.shape[0] // ROWS
    levels = courant_rows.shape[0] // (2 * ROWS)
    side_rows = 3 * (tracer_rows.shape[0] // LANES) + ROWS
    vmem = pl.BlockSpec(memory_space=pltpu.VMEM)
    hbm = pl.BlockSpec(memory_space=pltpu.HBM)
    return pl.pallas_call(
        pack_kernel,
        out_shape=(
            jax.ShapeDtypeStruct((tiles, 1, 3 * LANES), jnp.float32),
            jax.ShapeDtypeStruct((3 * blocks + levels, LANES), jnp.float32),
            jax.ShapeDtypeStruct((3 * blocks + levels, LANES), jnp.float32),
            jax.ShapeDtypeStruct((side_rows, LANES), jnp.float32),
            jax.ShapeDtypeStruct((side_rows, LANES), jnp.float32),
        ),
        in_specs=[hbm] * 5,
        out_specs=(vmem,) * 5,
        scratch_shapes=[
            pltpu.VMEM(tracer_rows.shape, jnp.float32),
            pltpu.VMEM(courant_rows.shape, jnp.float32),
            pltpu.VMEM(forcing.shape, jnp.float32),
            pltpu.VMEM((1, columns), jnp.int32),
            pltpu.VMEM((1, columns), jnp.int32),
            pltpu.SemaphoreType.DMA((5,)),
        ],
        compiler_params=pltpu.CompilerParams(vmem_limit_bytes=VMEM_BYTES),
        cost_estimate=pl.CostEstimate(
            flops=300000000, bytes_accessed=2500000, transcendentals=columns
        ),
        name="pack",
    )(*(
        pltpu.with_memory_space_constraint(array, pltpu.HBM)
        for array in (
            tracer_rows, courant_rows, forcing,
            plant_type.reshape(1, columns), send_slot.reshape(1, columns),
        )
    ))


def face_weights(face_courant):
    half = 0.5 * face_courant
    upwind = face_courant > 0
    shrink_left = 1.0 - 2.0 / 3.0 * face_courant
    shrink_right = 1.0 + 2.0 / 3.0 * face_courant
    curve = half * jnp.where(upwind, shrink_left, shrink_right)
    middle = face_courant * jnp.where(upwind, 1.0 - half - 3.0 * curve, 1.0 + half + 3.0 * curve)
    left_edge = face_courant * jnp.where(upwind, half - 3.0 * curve, 0.0)
    right_edge = face_courant * jnp.where(upwind, 0.0, 3.0 * curve - half)
    left_cell = face_courant * jnp.where(upwind, 6.0 * curve, 0.0)
    right_cell = face_courant * jnp.where(upwind, 0.0, -6.0 * curve)
    near, far = 7.0 / 12.0, 1.0 / 12.0
    return [
        -far * left_edge,
        near * left_edge - far * middle,
        near * (middle + left_edge) - far * right_edge + left_cell,
        near * (middle + right_edge) - far * left_edge + right_cell,
        near * right_edge - far * middle,
        -far * right_edge,
    ]


def divergence_weights(face_after, face_before):
    after = face_weights(face_after)
    before = face_weights(face_before)
    taps = []
    for offset in range(7):
        if offset == 0:
            taps.append(-before[0])
        elif offset == 6:
            taps.append(after[5])
        else:
            taps.append(after[offset - 1] - before[offset])
    return taps


CHUNK = 4
TURNED_ROWS = LANES + 16
PADDED_ROWS = 2 * ROWS


def lat_kernel(
    lat_ref, tracer_ref, courant_ref, mixing_ref, swap_ref, next_swap_ref,
    sum_ref, response_ref, pivot_ref,
    rows_ref, weight_ref,
):
    levels = mixing_ref.shape[0] + 1
    blocks = tracer_ref.shape[0] // ROWS
    members = blocks // levels
    half = levels * ROWS
    first = lat_ref[0] == 0
    even = lax.rem(lat_ref[0], 2) == 0
    last = lat_ref[0] == lat_ref[1] - 1

    zero = jnp.zeros((blocks, LANES), jnp.float32)
    for step in range(3):
        span = slice(step * blocks, (step + 1) * blocks)
        rows_ref[pl.ds(5 + step, blocks, stride=PADDED_ROWS), :] = jnp.where(
            first, zero, jnp.where(even, next_swap_ref[span, :], swap_ref[span, :])
        )
        rows_ref[pl.ds(PADDED_ROWS + step, blocks, stride=PADDED_ROWS), :] = jnp.where(
            last, zero, jnp.where(even, swap_ref[span, :], next_swap_ref[span, :])
        )
    for block in range(blocks):
        rows_ref[block * PADDED_ROWS + 8 : block * PADDED_ROWS + 16, :] = tracer_ref[
            block * ROWS : (block + 1) * ROWS, :
        ]
    row = lax.broadcasted_iota(jnp.int32, (ROWS, LANES), 0)
    for level in range(levels):
        north_face = courant_ref[half + level * ROWS : half + (level + 1) * ROWS, :]
        place = slice(3 * blocks + level, 3 * blocks + level + 1)
        below = jnp.where(even, next_swap_ref[place, :], swap_ref[place, :])
        below = jnp.where(first, 0.0, below)
        south_face = jnp.where(row == 0, below, pltpu.roll(north_face, 1, 0))
        north_face = jnp.where(jnp.logical_and(last, row == ROWS - 1), 0.0, north_face)
        taps = divergence_weights(north_face, south_face)
        for offset in range(7):
            weight_ref[level, offset] = 1.0 - taps[3] if offset == 3 else -taps[offset]

    ratio = None
    response = []
    for level in range(levels):
        pivot = jnp.ones((ROWS, LANES), jnp.float32)
        if level > 0:
            pivot = pivot + mixing_ref[level - 1]
        if level < levels - 1:
            pivot = pivot + mixing_ref[level]
        if level > 0:
            pivot = pivot - mixing_ref[level - 1] * ratio
        inverse = 1.0 / pivot
        carried = inverse
        if level > 0:
            carried = mixing_ref[level - 1] * inverse
            response.append(carried * response[-1])
        else:
            response.append(inverse)
        pivot_ref[level, 0] = inverse
        pivot_ref[level, 1] = carried
        if level < levels - 1:
            ratio = mixing_ref[level] * inverse
            pivot_ref[level, 2] = ratio
    for level in range(levels - 1, -1, -1):
        if level < levels - 1:
            response[level] = response[level] + pivot_ref[level, 2] * response[level + 1]
        response_ref[level] = response[level]

    together = 4

    def member_step(index, carry):
        for level in range(levels):
            taps = [weight_ref[level, offset] for offset in range(7)]
            for step in range(together):
                block = (index * together + step) * levels + level
                base = pl.multiple_of(block * PADDED_ROWS, PADDED_ROWS) + 5
                total = taps[0] * rows_ref[pl.ds(base, ROWS), :]
                for offset in range(1, 7):
                    total = total + taps[offset] * rows_ref[pl.ds(base + offset, ROWS), :]
                sum_ref[pl.ds(pl.multiple_of(block * ROWS, ROWS), ROWS), :] = total
        return carry

    lax.fori_loop(0, members // together, member_step, 0)


def lon_kernel(
    tracer_ref, courant_ref, side_ref, side_next_ref, sum_ref, pivot_ref, cell_ref,
    out_ref, leaf_ref, place_ref,
    turned_ref, turned_sum_ref, turned_courant_ref, lon_ref,
):
    members, levels = out_ref.shape[0], out_ref.shape[1]
    squares = tracer_ref.shape[0] // LANES

    even = lax.rem(lax.axis_index("lon"), 2) == 0
    for square in range(squares):
        base = square * TURNED_ROWS
        span = slice(3 * square, 3 * square + 3)
        turned_ref[base + 5 : base + 8, :] = jnp.where(
            even, side_next_ref[span, :], side_ref[span, :]
        )
        turned_ref[base + 8 + LANES : base + 11 + LANES, :] = jnp.where(
            even, side_ref[span, :], side_next_ref[span, :]
        )
        turned_ref[base + 8 : base + 8 + LANES, :] = tracer_ref[
            square * LANES : (square + 1) * LANES, :
        ].T
    half = levels * ROWS
    turned_faces = courant_ref[...].T
    low_half = lax.broadcasted_iota(jnp.int32, (LANES, LANES), 1) < half
    turned_faces = jnp.where(low_half, turned_faces, pltpu.roll(turned_faces, half, 1))
    turned_courant_ref[8 : 8 + LANES, :] = turned_faces
    span = slice(3 * squares, 3 * squares + ROWS)
    side_face = jnp.where(even, side_next_ref[span, :], side_ref[span, :])
    side_face = jnp.where(low_half[0:ROWS], side_face, pltpu.roll(side_face, half, 1))
    turned_courant_ref[0:8, :] = side_face

    def lon_step(tile, carry):
        start = pl.multiple_of(tile * ROWS, ROWS)
        taps = divergence_weights(
            turned_courant_ref[pl.ds(start + 8, ROWS), :],
            turned_courant_ref[pl.ds(start + 7, ROWS), :],
        )
        for square in range(squares):
            base = square * TURNED_ROWS + start + 5
            total = taps[0] * turned_ref[pl.ds(base, ROWS), :]
            for offset in range(1, 7):
                total = total + taps[offset] * turned_ref[pl.ds(base + offset, ROWS), :]
            turned_sum_ref[pl.ds(square * LANES + start, ROWS), :] = total
        return carry

    lax.fori_loop(0, LANES // ROWS, lon_step, 0)
    for square in range(squares):
        span = slice(square * LANES, (square + 1) * LANES)
        lon_ref[span, :] = turned_sum_ref[span, :].T

    together = 4

    def member_step(index, carry):
        swept = [None] * together
        stored = [[None] * levels for _ in range(together)]
        for level in range(levels):
            inverse = pivot_ref[level, 0]
            carried = pivot_ref[level, 1]
            for step in range(together):
                block = (index * together + step) * levels + level
                span = pl.ds(pl.multiple_of(block * ROWS, ROWS), ROWS)
                total = (sum_ref[span, :] - lon_ref[span, :]) * inverse
                if level > 0:
                    total = total + carried * swept[step]
                swept[step] = total
                stored[step][level] = total
        for level in range(levels - 1, -1, -1):
            ratio = pivot_ref[level, 2] if level < levels - 1 else None
            for step in range(together):
                if level < levels - 1:
                    swept[step] = stored[step][level] + ratio * swept[step]
                out_ref[index * together + step, level] = swept[step]
        return carry

    lax.fori_loop(0, members // together, member_step, 0)
    near_cells(tracer_ref, cell_ref, leaf_ref, place_ref, members, levels)


def near_cells(tracer_ref, cell_ref, leaf_ref, place_ref, members, levels):
    sources = cell_ref.shape[0]
    groups = sources // 2
    quarters = ROWS // 2
    stride = levels * ROWS
    bottom = jnp.concatenate(
        [
            jnp.concatenate(
                [
                    tracer_ref[pl.ds(2 * quarter + side, members, stride=stride), :]
                    for side in range(2)
                ],
                axis=1,
            )
            for quarter in range(quarters)
        ],
        axis=0,
    )
    bottom_parts = jnp.concatenate(bf16_parts(bottom, 2), axis=0)
    cells = jnp.concatenate(
        [cell_ref[pl.ds(tile, sources // 4, stride=4), :] for tile in range(4)], axis=0
    )
    cells = jnp.concatenate([cells[0:groups], cells[groups : 2 * groups]], axis=1)
    place_ref[0] = jnp.right_shift(cells, 8).astype(jnp.float32)
    lane = jnp.bitwise_and(cells, 255).astype(jnp.float32)
    place_ref[1] = lane
    cell_ids = (
        lax.broadcasted_iota(jnp.int32, (256, LANES), 0).astype(jnp.float32).astype(jnp.bfloat16)
    )
    one, zero = jnp.bfloat16(1.0), jnp.bfloat16(0.0)
    for chunk in range(groups // CHUNK):
        rows = range(chunk * CHUNK, (chunk + 1) * CHUNK)
        span = slice(chunk * CHUNK * LANES, (chunk + 1) * CHUNK * LANES)
        cell_onehot = jnp.concatenate(
            [
                jnp.where(cell_ids == lane[row : row + 1, :].astype(jnp.bfloat16), one, zero)
                for row in rows
            ],
            axis=1,
        )
        near = jnp.dot(bottom_parts, cell_onehot, preferred_element_type=jnp.float32)
        near = near[0 : quarters * members] + near[quarters * members : 2 * quarters * members]
        quarter_index = jnp.concatenate(
            [
                jnp.broadcast_to(place_ref[0, row : row + 1, :], (members, LANES))
                for row in rows
            ],
            axis=1,
        )
        picked = near[0:members]
        for quarter in range(1, quarters):
            picked = jnp.where(
                quarter_index == quarter, near[quarter * members : (quarter + 1) * members], picked
            )
        leaf_ref[:, span] = 280.0 + 70.0 * picked


def advect_and_mix(
    lat_place, tracer_rows, courant_rows, mixing, swap, next_swap, side_swap, side_swap_next, recv_cell
):
    levels, rows, lanes = mixing.shape[0] + 1, mixing.shape[1], mixing.shape[2]
    blocks = tracer_rows.shape[0] // rows
    members = blocks // levels
    squares = tracer_rows.shape[0] // lanes
    vmem = pl.BlockSpec(memory_space=pltpu.VMEM)
    params = pltpu.CompilerParams(vmem_limit_bytes=VMEM_BYTES)
    cost = pl.CostEstimate(flops=6000000, bytes_accessed=4000000, transcendentals=0)
    lat_sum, response, pivots = pl.pallas_call(
        lat_kernel,
        out_shape=(
            jax.ShapeDtypeStruct(tracer_rows.shape, jnp.float32),
            jax.ShapeDtypeStruct((levels, rows, lanes), jnp.float32),
            jax.ShapeDtypeStruct((levels, 3, rows, lanes), jnp.float32),
        ),
        in_specs=[pl.BlockSpec(memory_space=pltpu.SMEM)] + [vmem] * 5,
        out_specs=(vmem,) * 3,
        scratch_shapes=[
            pltpu.VMEM(((blocks + 1) * PADDED_ROWS, LANES), jnp.float32),
            pltpu.VMEM((levels, 7, ROWS, LANES), jnp.float32),
        ],
        compiler_params=params,
        cost_estimate=cost,
        name="advect_lat",
    )(lat_place, tracer_rows, courant_rows, mixing, swap, next_swap)
    sources, places = recv_cell.shape
    place_count = sources * places
    partial, leaf, place = pl.pallas_call(
        lon_kernel,
        out_shape=(
            jax.ShapeDtypeStruct((members, levels, rows, lanes), jnp.float32),
            jax.ShapeDtypeStruct((members, place_count), jnp.float32),
            jax.ShapeDtypeStruct((2, place_count // LANES, LANES), jnp.float32),
        ),
        in_specs=[vmem] * 7,
        out_specs=(vmem,) * 3,
        scratch_shapes=[
            pltpu.VMEM((squares * TURNED_ROWS, LANES), jnp.float32),
            pltpu.VMEM((squares * LANES, LANES), jnp.float32),
            pltpu.VMEM((LANES + 8, LANES), jnp.float32),
            pltpu.VMEM((squares * LANES, LANES), jnp.float32),
        ],
        compiler_params=params,
        cost_estimate=cost,
        name="advect_lon_and_mix",
    )(tracer_rows, courant_rows, side_swap, side_swap_next, lat_sum, pivots, recv_cell)
    return partial, response, leaf, place


def arrhenius(energy, leaf_temp):
    return jnp.exp(energy * (leaf_temp - 25.0) / (298.15 * GAS_CONSTANT * (leaf_temp + 273.15)))


def flux_kernel(
    received_ref, params_ref, leaf_ref, place_ref, partial_ref, response_ref,
    out_ref, surface_ref,
    column_ref, result_ref, copy_sems,
):
    members = params_ref.shape[1]
    types = params_ref.shape[2]
    sources = received_ref.shape[0]
    groups = sources // 2
    places = LANES // 2
    levels = response_ref.shape[0]
    quarters = ROWS // 2
    one, zero = jnp.bfloat16(1.0), jnp.bfloat16(0.0)

    carbox = 30.0 + 70.0 * params_ref[0]
    tables = jnp.concatenate(
        [carbox, (1.4 + 0.8 * params_ref[1]) * carbox, (0.005 + 0.025 * params_ref[2]) * carbox],
        axis=0,
    )
    table_parts = jnp.concatenate(bf16_parts(tables, 2), axis=1)

    half = lax.broadcasted_iota(jnp.int32, (groups, LANES), 1) < places

    def pair(values):
        low, high = values[0:groups], values[groups : 2 * groups]
        return (
            jnp.where(half, low, pltpu.roll(high, places, 1)),
            jnp.where(half, pltpu.roll(low, places, 1), high),
        )

    light, leaf_temp = pair(received_ref[:, 0, 0:LANES])
    water, flux_scale = pair(received_ref[:, 0, LANES : 2 * LANES])
    plant, _ = pair(received_ref[:, 0, 2 * LANES : 3 * LANES])
    leaf_temp = 35.0 * leaf_temp
    absorbed = 0.425 * (2000.0 * light)
    michaelis_carbon = 404.9 * arrhenius(79430.0, leaf_temp)
    michaelis_oxygen = 278.4 * arrhenius(36380.0, leaf_temp)
    compensation = 42.75 * arrhenius(37830.0, leaf_temp)
    column_ref[0] = absorbed
    column_ref[1] = arrhenius(65330.0, leaf_temp) * (0.2 + 0.8 * water)
    column_ref[2] = arrhenius(43540.0, leaf_temp)
    column_ref[3] = michaelis_carbon * (1.0 + 210.0 / michaelis_oxygen)
    column_ref[4] = compensation
    column_ref[5] = flux_scale
    column_ref[6] = 2.8 * absorbed
    column_ref[7] = (1.4 * 8.0) * compensation
    column_ref[8] = plant

    type_ids = (
        jnp.bitwise_and(lax.broadcasted_iota(jnp.int32, (2 * types, LANES), 0), types - 1)
        .astype(jnp.float32)
        .astype(jnp.bfloat16)
    )

    cell_ids = (
        lax.broadcasted_iota(jnp.int32, (256, LANES), 0).astype(jnp.float32).astype(jnp.bfloat16)
    )
    lefts, onehots = [], []
    for chunk in range(groups // CHUNK):
        rows = range(chunk * CHUNK, (chunk + 1) * CHUNK)
        span = slice(chunk * CHUNK * LANES, (chunk + 1) * CHUNK * LANES)

        def spread(ref):
            return jnp.concatenate(
                [jnp.broadcast_to(ref[row : row + 1, :], (members, LANES)) for row in rows],
                axis=1,
            )

        type_onehot = jnp.concatenate(
            [
                jnp.where(
                    type_ids == column_ref[8, row : row + 1, :].astype(jnp.bfloat16), one, zero
                )
                for row in rows
            ],
            axis=1,
        )
        params = jnp.dot(table_parts, type_onehot, preferred_element_type=jnp.float32)
        carbon_leaf = leaf_ref[:, span]
        warm = spread(column_ref.at[1])
        carboxylation = params[0:members] * warm
        transport_max = params[members : 2 * members] * spread(column_ref.at[2])
        respiration = params[2 * members : 3 * members] * warm
        total_rate = spread(column_ref.at[0]) + transport_max
        square = total_rate * total_rate - spread(column_ref.at[6]) * transport_max
        electron_rate = total_rate - square * lax.rsqrt(square)
        excess = carbon_leaf - spread(column_ref.at[4])
        rubisco_base = carbon_leaf + spread(column_ref.at[3])
        light_base = (1.4 * 4.0) * carbon_leaf + spread(column_ref.at[7])
        shared = excess / (rubisco_base * light_base)
        rubisco_rate = carboxylation * light_base * shared
        light_rate = electron_rate * rubisco_base * shared
        flux = spread(column_ref.at[5]) * (jnp.minimum(rubisco_rate, light_rate) - respiration)
        high, low = bf16_parts(flux, 2)
        quarter_index = spread(place_ref.at[0]).astype(jnp.bfloat16)
        left = []
        for quarter in range(quarters):
            here = quarter_index == jnp.bfloat16(quarter)
            left.append(jnp.where(here, high, zero))
            left.append(jnp.where(here, low, zero))
        cell_onehot = jnp.concatenate(
            [
                jnp.where(
                    cell_ids == place_ref[1, row : row + 1, :].astype(jnp.bfloat16), one, zero
                )
                for row in rows
            ],
            axis=1,
        )
        lefts.append(jnp.concatenate(left, axis=0))
        onehots.append(cell_onehot)

    summed = nt_dot(jnp.concatenate(lefts, axis=1), jnp.concatenate(onehots, axis=1))
    for quarter in range(quarters):
        start = quarter * 2 * members
        total = summed[start : start + members] + summed[start + members : start + 2 * members]
        surface_ref[:, 2 * quarter, :] = total[:, 0:LANES]
        surface_ref[:, 2 * quarter + 1, :] = total[:, LANES : 2 * LANES]

    copies = []
    share = members // OUT_COPIES
    for part in range(OUT_COPIES):
        responses = [response_ref[level] for level in range(levels)]
        for member in range(part * share, (part + 1) * share):
            surface = surface_ref[member]
            for level in range(levels):
                result_ref[member, level] = partial_ref[member, level] + responses[level] * surface
        span = pl.ds(part * share, share)
        copy = pltpu.make_async_copy(result_ref.at[span], out_ref.at[span], copy_sems.at[part])
        copy.start()
        copies.append(copy)
    for copy in copies:
        copy.wait()


def fluxes(received, land_params, leaf, place, partial, response):
    members, levels, rows, lanes = partial.shape
    vmem = pl.BlockSpec(memory_space=pltpu.VMEM)
    return pl.pallas_call(
        flux_kernel,
        out_shape=(
            jax.ShapeDtypeStruct(partial.shape, jnp.float32),
            jax.ShapeDtypeStruct((members, rows, lanes), jnp.float32),
        ),
        in_specs=[vmem] * 6,
        out_specs=(pl.BlockSpec(memory_space=pltpu.HBM), vmem),
        scratch_shapes=[
            pltpu.VMEM((9, received.shape[0] // 2, LANES), jnp.float32),
            pltpu.VMEM(partial.shape, jnp.float32),
            pltpu.SemaphoreType.DMA((OUT_COPIES,)),
        ],
        compiler_params=pltpu.CompilerParams(vmem_limit_bytes=VMEM_BYTES),
        cost_estimate=pl.CostEstimate(flops=600000000, bytes_accessed=3000000, transcendentals=400000),
        name="fluxes",
    )(received, land_params, leaf, place, partial, response)


def per_device(tracer, courant, mixing, forcing, plant_type, land_params, send_slot, recv_cell):
    members, levels, row_count, column_count = tracer.shape
    lon_count, lat_count = lax.axis_size("lon"), lax.axis_size("lat")
    tracer_rows = tracer.reshape(members * levels * row_count, column_count)
    courant_rows = courant.reshape(2 * levels * row_count, column_count)
    outgoing, first, second, side_next, side_first = pack(
        tracer_rows, courant_rows, forcing, plant_type, send_slot, lon_count * lat_count
    )
    pairs = [(i, i + 1) for i in range(0, lat_count, 2)]
    next_pairs = [(i + 1, (i + 2) % lat_count) for i in range(0, lat_count, 2)]
    swap = lax.ppermute(first, "lat", pairs + [(b, a) for a, b in pairs])
    next_swap = lax.ppermute(second, "lat", next_pairs + [(b, a) for a, b in next_pairs])
    pairs = [(i, i + 1) for i in range(0, lon_count, 2)]
    next_pairs = [(i + 1, (i + 2) % lon_count) for i in range(0, lon_count, 2)]
    side_swap = lax.ppermute(side_first, "lon", pairs + [(b, a) for a, b in pairs])
    side_swap_next = lax.ppermute(side_next, "lon", next_pairs + [(b, a) for a, b in next_pairs])
    received = lax.all_to_all(outgoing, ("lat", "lon"), split_axis=0, concat_axis=0, tiled=True)
    lat_place = jnp.stack([lax.axis_index("lat"), jnp.int32(lat_count)]).astype(jnp.int32)
    partial, response, leaf, place = advect_and_mix(
        lat_place, tracer_rows, courant_rows, mixing, swap, next_swap, side_swap, side_swap_next, recv_cell
    )
    return fluxes(received, land_params, leaf, place, partial, response)


def solution(mesh):
    in_specs = (
        P("mem", None, "lat", "lon"),
        P(None, None, "lat", "lon"),
        P(None, "lat", "lon"),
        P(None, ("lon", "lat")),
        P(("lon", "lat")),
        P(None, "mem", None),
        P(("lon", "lat")),
        P(("lon", "lat"), None),
    )
    out_specs = (P("mem", None, "lat", "lon"), P("mem", "lat", "lon"))
    return jax.shard_map(
        per_device, mesh=mesh, in_specs=in_specs, out_specs=out_specs, check_vma=False
    )
```
